32 devices in a mesh: batch: 16 (over z, y, core), seq: 2 (over x).
Axes of the slice: x: 2, y: 2, z: 4, core: 2. Of those that a mesh axis runs over, the one named last changes fastest.
Arguments:
- tables_in: bfloat16 [64, 512, 768], P('batch', 'seq'), may hold values from -6 to 6
- out_cot: bfloat16 [64, 512, 768], P('batch', 'seq'), may hold values from -6 to 6
- segment_ids: int32 [64, 512], P('batch'), may hold values from 0 to 1, as said below
- row_ids: int32 [64, 512], P('batch'), may hold values from 0 to 15
- col_ids: int32 [64, 512], P('batch'), may hold values from 0 to 11
- qkv_weight: bfloat16 [3, 768, 768], replicated, may hold values from -0.21875 to 0.21875
- out_weight: bfloat16 [768, 768], replicated, may hold values from -2.5 to 2.5
- ffn_in_weight: bfloat16 [768, 3072], replicated, may hold values from -0.21875 to 0.21875
- ffn_out_weight: bfloat16 [3072, 768], replicated, may hold values from -0.109375 to 0.109375
- small_params: float32 [9216], replicated
- qkv_master: float32 [3, 768, 768], P(None, ('batch', 'seq')), may hold values from -0.21875 to 0.21875
- qkv_first: float32 [3, 768, 768], P(None, ('batch', 'seq')), may hold values from -0.66 to 0.66
- qkv_second: float32 [3, 768, 768], P(None, ('batch', 'seq')), may hold values from 0.001 to 0.004
- qkv_ema: float32 [3, 768, 768], P(None, ('batch', 'seq')), may hold values from -0.21875 to 0.21875
- out_master: float32 [768, 768], P(('batch', 'seq')), may hold values from -2.5 to 2.5
- out_first: float32 [768, 768], P(('batch', 'seq')), may hold values from -0.66 to 0.66
- out_second: float32 [768, 768], P(('batch', 'seq')), may hold values from 0.00025 to 0.001
- out_ema: float32 [768, 768], P(('batch', 'seq')), may hold values from -2.5 to 2.5
- ffn_in_master: float32 [768, 3072], P(('batch', 'seq')), may hold values from -0.21875 to 0.21875
- ffn_in_first: float32 [768, 3072], P(('batch', 'seq')), may hold values from -0.66 to 0.66
- ffn_in_second: float32 [768, 3072], P(('batch', 'seq')), may hold values from 0.001 to 0.004
- ffn_in_ema: float32 [768, 3072], P(('batch', 'seq')), may hold values from -0.21875 to 0.21875
- ffn_out_master: float32 [3072, 768], P(('batch', 'seq')), may hold values from -0.109375 to 0.109375
- ffn_out_first: float32 [3072, 768], P(('batch', 'seq')), may hold values from -0.66 to 0.66
- ffn_out_second: float32 [3072, 768], P(('batch', 'seq')), may hold values from 0.001 to 0.004
- ffn_out_ema: float32 [3072, 768], P(('batch', 'seq')), may hold values from -0.109375 to 0.109375
- small_first: float32 [9216], replicated, may hold values from -1.2 to 1.2
- small_second: float32 [9216], replicated, may hold values from 0.002 to 0.03
- small_ema: float32 [9216], replicated
Outputs:
- layer_out: bfloat16 [64, 512, 768], P('batch', 'seq')
- input_grad: bfloat16 [64, 512, 768], P('batch', 'seq')
- qkv_grad: float32 [3, 768, 768], P(None, ('batch', 'seq'))
- out_grad: float32 [768, 768], P(('batch', 'seq'))
- ffn_in_grad: float32 [768, 3072], P(('batch', 'seq'))
- ffn_out_grad: float32 [3072, 768], P(('batch', 'seq'))
- small_grad: float32 [9216], replicated
- grad_norm: float32 [], replicated
- qkv_first_new: float32 [3, 768, 768], P(None, ('batch', 'seq'))
- qkv_second_new: float32 [3, 768, 768], P(None, ('batch', 'seq'))
- qkv_master_new: float32 [3, 768, 768], P(None, ('batch', 'seq'))
- qkv_copy_new: bfloat16 [3, 768, 768], P(None, ('batch', 'seq'))
- qkv_ema_new: float32 [3, 768, 768], P(None, ('batch', 'seq'))
- out_first_new: float32 [768, 768], P(('batch', 'seq'))
- out_second_new: float32 [768, 768], P(('batch', 'seq'))
- out_master_new: float32 [768, 768], P(('batch', 'seq'))
- out_copy_new: bfloat16 [768, 768], P(('batch', 'seq'))
- out_ema_new: float32 [768, 768], P(('batch', 'seq'))
- ffn_in_first_new: float32 [768, 3072], P(('batch', 'seq'))
- ffn_in_second_new: float32 [768, 3072], P(('batch', 'seq'))
- ffn_in_master_new: float32 [768, 3072], P(('batch', 'seq'))
- ffn_in_copy_new: bfloat16 [768, 3072], P(('batch', 'seq'))
- ffn_in_ema_new: float32 [768, 3072], P(('batch', 'seq'))
- ffn_out_first_new: float32 [3072, 768], P(('batch', 'seq'))
- ffn_out_second_new: float32 [3072, 768], P(('batch', 'seq'))
- ffn_out_master_new: float32 [3072, 768], P(('batch', 'seq'))
- ffn_out_copy_new: bfloat16 [3072, 768], P(('batch', 'seq'))
- ffn_out_ema_new: float32 [3072, 768], P(('batch', 'seq'))
- small_first_new: float32 [9216], replicated
- small_second_new: float32 [9216], replicated
- small_new: float32 [9216], replicated
- small_ema_new: float32 [9216], replicated
The draws below stay inside these ranges and needn't reach their ends.
Inputs may be any that keep to these rules, and one draw needn't show every extreme that they name: In each table, segment_ids are 0 on the first n tokens and 1 on the rest, with 32 <= n <= 128.
All inputs are finite; a program needn't handle non-finite values.
Results may differ from the reference program's by a relative error of at most 0.015.
Values may be sent and summed in bfloat16 or wider, within the bound.
A program may use at most 192 MiB of HBM per device.

```python
import math
import jax
import jax.numpy as jnp
from jax import lax

D = 768
HD = 64
FF = 3072
LEN = 512
STEP = 10
TABLES = 64


def draw_segment_ids(key, part):
    lengths = jax.random.randint(key, (TABLES, 1), LEN // 16, LEN // 4 + 1)
    position = jnp.arange(LEN, dtype=jnp.int32)[None, :]
    return (position >= lengths).astype(jnp.int32)


def small_values(key, salt):
    key = jax.random.fold_in(key, salt)
    key_gain, key_rest = jax.random.split(key)
    gains = 1.0 + 0.1 * jax.random.normal(key_gain, (2 * D,), jnp.float32)
    others = 0.2 * jax.random.normal(key_rest, (6 * D + FF,), jnp.float32)
    return jnp.concatenate([gains, others])


def draw_small_params(key, part):
    return small_values(key, 11)


def draw_small_ema(key, part):
    return small_values(key, 23)


def plant(drawn, own_key, least, top_value):
    spot = [jax.random.randint(jax.random.fold_in(own_key, axis), (), 0, length) for axis, length in enumerate(drawn.shape)]
    longest = drawn.shape.index(max(drawn.shape))
    beside = spot[:longest] + [(spot[longest] + 1) % drawn.shape[longest]] + spot[longest + 1:]
    return drawn.at[tuple(spot)].set(least).at[tuple(beside)].set(top_value)


def block_scale(stream_key, extent, shards, smallest, largest):
    factor_of, own = 1.0, jax.random.fold_in(stream_key, 6)
    for dim, blocks in shards:
        heights = jnp.exp(jax.random.uniform(jax.random.fold_in(own, dim), (blocks,), jnp.float32, smallest / len(shards), largest / len(shards)))
        factor_of = factor_of * jnp.repeat(heights, extent[dim] // blocks).reshape([-1 if axis == dim else 1 for axis in range(len(extent))])
    return factor_of


def bell_draw(stream_key, shape, scale, limit, cuts=(), kind=jnp.bfloat16):
    level = block_scale(stream_key, shape, cuts, -0.22, 0.18) if cuts else 1.0
    values = jax.random.normal(stream_key, shape, jnp.float32) * scale * level
    return jnp.minimum(jnp.maximum(values, -limit), limit).astype(kind)


def setup_inputs(seed: int = 0) -> dict:
    splits = jax.random.split(jax.random.key(seed), 30)
    tables_in = bell_draw(splits[0], (TABLES, LEN, D), 1.0, 6.0, ((0, 16), (1, 2)))
    out_cot = bell_draw(splits[1], (TABLES, LEN, D), 1.0, 6.0, ((0, 16), (1, 2)))
    segment_ids = draw_segment_ids(jax.random.fold_in(splits[29], 71), 0)
    row_ids = plant(jax.random.randint(splits[3], (TABLES, LEN), 0, 16), jax.random.fold_in(splits[3], 1), 0, 15).astype(jnp.int32)
    col_ids = plant(jax.random.randint(splits[4], (TABLES, LEN), 0, 12), jax.random.fold_in(splits[4], 1), 0, 11).astype(jnp.int32)
    qkv_weight = bell_draw(splits[5], (3, D, D), D ** -0.5, 0.21875)
    out_weight = bell_draw(splits[6], (D, D), (max(D // 128, 1)) ** -0.5, 2.5)
    ffn_in_weight = bell_draw(splits[7], (D, FF), D ** -0.5, 0.21875)
    ffn_out_weight = bell_draw(splits[8], (FF, D), FF ** -0.5, 0.109375)
    small_params = draw_small_params(jax.random.fold_in(splits[29], 71), 0)
    qkv_master = bell_draw(splits[10], (3, D, D), D ** -0.5, 0.21875, ((1, 32),), jnp.float32)
    qkv_first = bell_draw(splits[11], (3, D, D), 0.11, 0.66, ((1, 32),), jnp.float32)
    qkv_second = jnp.clip(jnp.exp(math.log(0.004) - 1.3862944 * jax.random.uniform(splits[12], (3, D, D), jnp.float32) ** block_scale(splits[12], (3, D, D), ((1, 32),), -0.2, 0.2)), 0.001, 0.004)
    qkv_ema = bell_draw(splits[13], (3, D, D), D ** -0.5, 0.21875, ((1, 32),), jnp.float32)
    out_master = bell_draw(splits[14], (D, D), (max(D // 128, 1)) ** -0.5, 2.5, ((0, 32),), jnp.float32)
    out_first = bell_draw(splits[15], (D, D), 0.11, 0.66, ((0, 32),), jnp.float32)
    out_second = jnp.clip(jnp.exp(math.log(0.001) - 1.3862944 * jax.random.uniform(splits[16], (D, D), jnp.float32) ** block_scale(splits[16], (D, D), ((0, 32),), -0.2, 0.2)), 0.00025, 0.001)
    out_ema = bell_draw(splits[17], (D, D), (max(D // 128, 1)) ** -0.5, 2.5, ((0, 32),), jnp.float32)
    ffn_in_master = bell_draw(splits[18], (D, FF), D ** -0.5, 0.21875, ((0, 32),), jnp.float32)
    ffn_in_first = bell_draw(splits[19], (D, FF), 0.11, 0.66, ((0, 32),), jnp.float32)
    ffn_in_second = jnp.clip(jnp.exp(math.log(0.004) - 1.3862944 * jax.random.uniform(splits[20], (D, FF), jnp.float32) ** block_scale(splits[20], (D, FF), ((0, 32),), -0.2, 0.2)), 0.001, 0.004)
    ffn_in_ema = bell_draw(splits[21], (D, FF), D ** -0.5, 0.21875, ((0, 32),), jnp.float32)
    ffn_out_master = bell_draw(splits[22], (FF, D), FF ** -0.5, 0.109375, ((0, 32),), jnp.float32)
    ffn_out_first = bell_draw(splits[23], (FF, D), 0.11, 0.66, ((0, 32),), jnp.float32)
    ffn_out_second = jnp.clip(jnp.exp(math.log(0.004) - 1.3862944 * jax.random.uniform(splits[24], (FF, D), jnp.float32) ** block_scale(splits[24], (FF, D), ((0, 32),), -0.2, 0.2)), 0.001, 0.004)
    ffn_out_ema = bell_draw(splits[25], (FF, D), FF ** -0.5, 0.109375, ((0, 32),), jnp.float32)
    small_first = bell_draw(splits[26], (8 * D + FF,), 0.2, 1.2, (), jnp.float32)
    small_second = jnp.clip(jnp.exp(jax.random.uniform(splits[27], (8 * D + FF,), jnp.float32, math.log(0.002), math.log(0.03))), 0.002, 0.03)
    small_ema = draw_small_ema(jax.random.fold_in(splits[29], 71), 0)
    return {"tables_in": tables_in, "out_cot": out_cot, "segment_ids": segment_ids, "row_ids": row_ids, "col_ids": col_ids, "qkv_weight": qkv_weight, "out_weight": out_weight, "ffn_in_weight": ffn_in_weight, "ffn_out_weight": ffn_out_weight, "small_params": small_params, "qkv_master": qkv_master, "qkv_first": qkv_first, "qkv_second": qkv_second, "qkv_ema": qkv_ema, "out_master": out_master, "out_first": out_first, "out_second": out_second, "out_ema": out_ema, "ffn_in_master": ffn_in_master, "ffn_in_first": ffn_in_first, "ffn_in_second": ffn_in_second, "ffn_in_ema": ffn_in_ema, "ffn_out_master": ffn_out_master, "ffn_out_first": ffn_out_first, "ffn_out_second": ffn_out_second, "ffn_out_ema": ffn_out_ema, "small_first": small_first, "small_second": small_second, "small_ema": small_ema}


@jax.custom_vjp
def low(v):
    return lax.optimization_barrier(v.astype(jnp.bfloat16)).astype(jnp.float32)

@jax.custom_vjp
def low_back(v):
    return v

def low_keep(v):
    return (low(v), None)

def low_pass(kept, grad):
    return (grad,)

def back_keep(v):
    return (v, None)

def back_low(kept, grad):
    return (low(grad),)
low.defvjp(low_keep, low_pass)
low_back.defvjp(back_keep, back_low)
EPS_NORM = 1e-06
NEG_BIG = -1e+30
HIGH = lax.Precision.HIGHEST
BETA_ONE = 0.9
BETA_TWO = 0.999
ADAM_EPS = 1e-08
DECAY = 0.01
EMA_KEEP = 0.8
SMALL_RATE = 0.1

def norm_rows(rows, gain, shift):
    centre = rows - lax.optimization_barrier(jnp.mean(rows, axis=-1, keepdims=True))
    spread = lax.optimization_barrier(jnp.mean(centre * centre, axis=-1, keepdims=True))
    return centre * lax.rsqrt(spread + EPS_NORM) * gain + shift

def split_small(small_terms, model_width, hidden_units):
    pieces = [small_terms[offset * model_width:(offset + 1) * model_width] for offset in range(8)]
    return pieces + [small_terms[8 * model_width:8 * model_width + hidden_units]]

def visible_pair(seg_query, row_query, col_query, seg_key, row_key, col_key):
    return (seg_query[..., :, None] == 0) | (seg_key[..., None, :] == 0) | (row_query[..., :, None] == row_key[..., None, :]) | (col_query[..., :, None] == col_key[..., None, :])

def block_layer(weights, x_rows, seg_ids, row_pos, col_pos):
    w_qkv, w_attn, w_inner, w_outer, small_terms = weights
    group, length, model_width = x_rows.shape
    heads = model_width // HD
    gain_one, gain_two, shift_one, shift_two, bias_query, bias_value, bias_attn, bias_ffn, bias_inner = split_small(small_terms, model_width, w_inner.shape[1])

    def project(left, right):
        return jnp.einsum('gld,de->gle', left, right, precision=HIGH)
    query = low(low_back(project(x_rows, w_qkv[0]) + bias_query)).reshape(group, length, heads, HD)
    keys = low(low_back(project(x_rows, w_qkv[1]))).reshape(group, length, heads, HD)
    values = low(low_back(project(x_rows, w_qkv[2]) + bias_value)).reshape(group, length, heads, HD)
    raw = jnp.einsum('gqhe,gkhe->ghqk', query, keys, precision=HIGH) * HD ** (-0.5)
    allowed = visible_pair(seg_ids, row_pos, col_pos, seg_ids, row_pos, col_pos)[:, None]
    scores = jnp.where(allowed, low_back(raw), NEG_BIG)
    top_score = lax.optimization_barrier(jnp.max(scores, axis=-1, keepdims=True))
    exp_scores = jnp.exp(scores - top_score)
    prob_low = low(exp_scores / lax.optimization_barrier(jnp.sum(exp_scores, axis=-1, keepdims=True)))
    context = jnp.einsum('ghqk,gkhe->gqhe', prob_low, values, precision=HIGH)
    context = low(low_back(context)).reshape(group, length, model_width)
    attn = low_back(project(context, w_attn) + bias_attn)
    normed = norm_rows(x_rows + attn, gain_one, shift_one)
    inner = low_back(project(low(normed), w_inner) + bias_inner)
    active = low(jax.nn.gelu(inner, approximate=False))
    branch = low_back(project(active, w_outer) + bias_ffn)
    return norm_rows(normed + branch, gain_two, shift_two)

def adam_update(grad_new, first, second, master, ema_old, rate):
    first_new = BETA_ONE * first + (1.0 - BETA_ONE) * grad_new
    second_new = BETA_TWO * second + (1.0 - BETA_TWO) * grad_new * grad_new
    fix_one = 1.0 - BETA_ONE ** STEP
    fix_two = 1.0 - BETA_TWO ** STEP
    master_new = master - rate * (first_new / fix_one / (jnp.sqrt(second_new / fix_two) + ADAM_EPS) + DECAY * master)
    ema_new = EMA_KEEP * ema_old + (1.0 - EMA_KEEP) * master_new
    return (first_new, second_new, master_new, ema_new)

def reference(tables_in, out_cot, segment_ids, row_ids, col_ids, qkv_weight, out_weight, ffn_in_weight, ffn_out_weight, small_params, qkv_master, qkv_first, qkv_second, qkv_ema, out_master, out_first, out_second, out_ema, ffn_in_master, ffn_in_first, ffn_in_second, ffn_in_ema, ffn_out_master, ffn_out_first, ffn_out_second, ffn_out_ema, small_first, small_second, small_ema):
    weights = (qkv_weight.astype(jnp.float32), out_weight.astype(jnp.float32), ffn_in_weight.astype(jnp.float32), ffn_out_weight.astype(jnp.float32), small_params.astype(jnp.float32))
    group = math.gcd(TABLES, max(1, 4096 // LEN))
    blocks = TABLES // group
    seg_blocks = segment_ids.reshape(blocks, group, LEN)
    row_blocks = row_ids.reshape(blocks, group, LEN)
    col_blocks = col_ids.reshape(blocks, group, LEN)

    def whole(weight_set, x_all):

        def step(carry, item):
            x_block, seg_block, row_block, col_block = item
            return (carry, jax.checkpoint(block_layer)(weight_set, x_block, seg_block, row_block, col_block))
        _, outputs = lax.scan(step, jnp.zeros((), jnp.float32), (x_all.reshape(blocks, group, LEN, D), seg_blocks, row_blocks, col_blocks))
        return outputs.reshape(TABLES, LEN, D)
    outputs, pullback = jax.vjp(whole, weights, tables_in.astype(jnp.float32))
    grads, grad_input = pullback(out_cot.astype(jnp.float32))
    layer_out = outputs.astype(jnp.bfloat16)
    input_grad = grad_input.astype(jnp.bfloat16)
    g_qkv, g_out, g_in, g_outer, g_small = grads
    total_sq = jnp.sum(g_qkv * g_qkv) + jnp.sum(g_out * g_out) + jnp.sum(g_in * g_in) + jnp.sum(g_outer * g_outer) + jnp.sum(g_small * g_small)
    grad_norm = jnp.sqrt(total_sq)
    clip_limit = math.sqrt(float(4 * D * D + 2 * D * FF + 8 * D + FF))
    clip_scale = jnp.minimum(1.0, clip_limit / grad_norm)
    qkv_grad = g_qkv * clip_scale
    out_grad = g_out * clip_scale
    ffn_in_grad = g_in * clip_scale
    ffn_out_grad = g_outer * clip_scale
    small_grad = g_small * clip_scale
    qf, qs, qm, qe = adam_update(qkv_grad, qkv_first, qkv_second, qkv_master, qkv_ema, D ** (-0.5))
    of, osec, om, oe = adam_update(out_grad, out_first, out_second, out_master, out_ema, max(D // 128, 1) ** (-0.5))
    inf, ins, inm, ine = adam_update(ffn_in_grad, ffn_in_first, ffn_in_second, ffn_in_master, ffn_in_ema, D ** (-0.5))
    uf, us, um, ue = adam_update(ffn_out_grad, ffn_out_first, ffn_out_second, ffn_out_master, ffn_out_ema, FF ** (-0.5))
    sf, ss, sm, se = adam_update(small_grad, small_first, small_second, small_params, small_ema, SMALL_RATE)
    return (layer_out, input_grad, qkv_grad, out_grad, ffn_in_grad, ffn_out_grad, small_grad, grad_norm, qf, qs, qm, qm.astype(jnp.bfloat16), qe, of, osec, om, om.astype(jnp.bfloat16), oe, inf, ins, inm, inm.astype(jnp.bfloat16), ine, uf, us, um, um.astype(jnp.bfloat16), ue, sf, ss, sm, se)
```

```python
import math

import jax
import jax.numpy as jnp
from jax import lax
from jax.sharding import PartitionSpec as P

HD = 64
STEP = 10


EPS_NORM = 1e-06
NEG_BIG = -1e30
BETA_ONE = 0.9
BETA_TWO = 0.999
ADAM_EPS = 1e-08
DECAY = 0.01
EMA_KEEP = 0.8
SMALL_RATE = 0.1


def norm_rows(rows, gain, shift):
    centre = rows - jnp.mean(rows, axis=-1, keepdims=True)
    spread = jnp.mean(centre * centre, axis=-1, keepdims=True)
    return centre * lax.rsqrt(spread + EPS_NORM) * gain + shift


def gelu_exact(values):
    return jax.nn.gelu(values, approximate=False)


def split_small(small_terms, model_width, hidden_units):
    pieces = [small_terms[offset * model_width : (offset + 1) * model_width] for offset in range(8)]
    return pieces + [small_terms[8 * model_width : 8 * model_width + hidden_units]]


def visible_pair(seg_query, row_query, col_query, seg_key, row_key, col_key):
    return (
        (seg_query[..., :, None] == 0)
        | (seg_key[..., None, :] == 0)
        | (row_query[..., :, None] == row_key[..., None, :])
        | (col_query[..., :, None] == col_key[..., None, :])
    )


def product(left, right):
    return jnp.dot(left, right, preferred_element_type=jnp.float32)


def product_left_t(left, right):
    return lax.dot_general(
        left, right, (((0,), (0,)), ((), ())), preferred_element_type=jnp.float32
    )


def product_right_t(left, right):
    return lax.dot_general(
        left, right, (((1,), (1,)), ((), ())), preferred_element_type=jnp.float32
    )


def adam_update(grad_new, first, second, master, ema_old, rate):
    first_new = BETA_ONE * first + (1.0 - BETA_ONE) * grad_new
    second_new = BETA_TWO * second + (1.0 - BETA_TWO) * grad_new * grad_new
    fix_one = 1.0 - BETA_ONE**STEP
    fix_two = 1.0 - BETA_TWO**STEP
    master_new = master - rate * (
        first_new / fix_one / (jnp.sqrt(second_new / fix_two) + ADAM_EPS) + DECAY * master
    )
    ema_new = EMA_KEEP * ema_old + (1.0 - EMA_KEEP) * master_new
    return (first_new, second_new, master_new, ema_new)


AXES = ("batch", "seq")


def partner_swap(values, bit):
    count = lax.axis_size(AXES)
    return lax.ppermute(values, AXES, [(place, place ^ (1 << bit)) for place in range(count)])


def bit_order():
    bits = lax.axis_size(AXES).bit_length() - 1
    return list(range(1, bits)) + [0]


def scatter_sum(rows):
    order = bit_order()
    place = lax.axis_index(AXES)
    left = list(reversed(range(len(order))))
    held = rows.astype(jnp.bfloat16).reshape((2,) * len(order) + rows.shape[1:])
    for bit in order:
        axis = left.index(bit)
        mine = (place >> bit) & 1
        keep = lax.dynamic_index_in_dim(held, mine, axis, keepdims=False)
        send = lax.dynamic_index_in_dim(held, 1 - mine, axis, keepdims=False)
        total = keep.astype(jnp.float32) + partner_swap(send, bit).astype(jnp.float32)
        left.remove(bit)
        held = total.astype(jnp.bfloat16) if left else total
    return held


def butterfly_sum(values):
    for bit in bit_order():
        values = values + partner_swap(values, bit)
    return values


def body(
    tables_in,
    out_cot,
    segment_ids,
    row_ids,
    col_ids,
    qkv_weight,
    out_weight,
    ffn_in_weight,
    ffn_out_weight,
    small_params,
    qkv_master,
    qkv_first,
    qkv_second,
    qkv_ema,
    out_master,
    out_first,
    out_second,
    out_ema,
    ffn_in_master,
    ffn_in_first,
    ffn_in_second,
    ffn_in_ema,
    ffn_out_master,
    ffn_out_first,
    ffn_out_second,
    ffn_out_ema,
    small_first,
    small_second,
    small_ema,
):
    model_width = qkv_weight.shape[1]
    hidden_units = ffn_in_weight.shape[1]
    heads = model_width // HD
    head_scale = HD ** (-0.5)
    seq_place = lax.axis_index("seq")
    swap = lambda rows: lax.all_to_all(rows, "seq", split_axis=0, concat_axis=1, tiled=True)
    unswap = lambda rows: lax.all_to_all(rows, "seq", split_axis=1, concat_axis=0, tiled=True)
    local_x, local_cot = (swap(tables_in), swap(out_cot))
    tab_count = local_x.shape[0]
    block_rows = local_x.shape[1]
    own = lambda ids: lax.dynamic_slice_in_dim(ids, seq_place * tab_count, tab_count, 0)
    seg_keys, row_keys, col_keys = (own(segment_ids), own(row_ids), own(col_ids))
    seg_query, row_query, col_query = (seg_keys, row_keys, col_keys)
    row_count = tab_count * block_rows
    (
        gain_one,
        gain_two,
        shift_one,
        shift_two,
        bias_query,
        bias_value,
        bias_attn,
        bias_ffn,
        bias_inner,
    ) = split_small(small_params, model_width, hidden_units)
    flat_x = local_x.reshape(row_count, model_width)
    query_low = (product(flat_x, qkv_weight[0]) + bias_query).astype(jnp.bfloat16)
    key_low = (
        product(flat_x, qkv_weight[1])
        .astype(jnp.bfloat16)
        .reshape(tab_count, block_rows, model_width)
    )
    value_low = (
        (product(flat_x, qkv_weight[2]) + bias_value)
        .astype(jnp.bfloat16)
        .reshape(tab_count, block_rows, model_width)
    )
    key_all, value_all = key_low, value_low
    rows_key = key_all.shape[1]
    query_heads = query_low.reshape(tab_count, block_rows, heads, HD)
    key_heads = key_all.reshape(tab_count, rows_key, heads, HD)
    value_heads = value_all.reshape(tab_count, rows_key, heads, HD)
    allowed = visible_pair(seg_query, row_query, col_query, seg_keys, row_keys, col_keys)[:, None]

    def scores_of():
        raw = (
            jnp.einsum(
                "bqhe,bkhe->bhqk", query_heads, key_heads, preferred_element_type=jnp.float32
            )
            * head_scale
        )
        return jnp.where(allowed, raw, NEG_BIG)

    scores = scores_of()
    top_score = jnp.max(scores, axis=-1, keepdims=True)
    exp_scores = jnp.exp(scores - top_score)
    exp_total = jnp.sum(exp_scores, axis=-1, keepdims=True)
    log_total = top_score + jnp.log(exp_total)
    prob_low = (exp_scores / exp_total).astype(jnp.bfloat16)
    context = jnp.einsum(
        "bhqk,bkhe->bqhe", prob_low, value_heads, preferred_element_type=jnp.float32
    )
    context_low = context.astype(jnp.bfloat16).reshape(row_count, model_width)
    attn = product(context_low, out_weight) + bias_attn
    first_sum = flat_x.astype(jnp.float32) + attn
    normed, first_back = jax.vjp(norm_rows, first_sum, gain_one, shift_one)
    normed_low = normed.astype(jnp.bfloat16)
    ffn_inner = product(normed_low, ffn_in_weight) + bias_inner
    active, gelu_back = jax.vjp(gelu_exact, ffn_inner)
    active_low = active.astype(jnp.bfloat16)
    branch = product(active_low, ffn_out_weight) + bias_ffn
    second_sum = normed + branch
    result, second_back = jax.vjp(norm_rows, second_sum, gain_two, shift_two)
    layer_out = unswap(result.astype(jnp.bfloat16).reshape(tab_count, block_rows, model_width))
    back_rows = local_cot.reshape(row_count, model_width).astype(jnp.float32)
    d_second, d_gain_two, d_shift_two = second_back(back_rows)
    d_branch = d_second.astype(jnp.bfloat16)
    d_bias_ffn = jnp.sum(d_branch.astype(jnp.float32), axis=0)
    g_outer = product_left_t(active_low, d_branch)
    d_active = product_right_t(d_branch, ffn_out_weight)
    (d_inner,) = gelu_back(d_active)
    d_inner_low = d_inner.astype(jnp.bfloat16)
    d_bias_inner = jnp.sum(d_inner_low.astype(jnp.float32), axis=0)
    g_inner = product_left_t(normed_low, d_inner_low)
    d_normed = product_right_t(d_inner_low, ffn_in_weight) + d_second
    d_first, d_gain_one, d_shift_one = first_back(d_normed)
    d_attn = d_first.astype(jnp.bfloat16)
    d_bias_attn = jnp.sum(d_attn.astype(jnp.float32), axis=0)
    g_attn = product_left_t(context_low, d_attn)
    d_context = (
        product_right_t(d_attn, out_weight)
        .astype(jnp.bfloat16)
        .reshape(tab_count, block_rows, heads, HD)
    )
    probs_again = jnp.exp(scores_of() - log_total)
    probs_again_low = probs_again.astype(jnp.bfloat16)
    d_value = jnp.einsum(
        "bhqk,bqhe->bkhe", probs_again_low, d_context, preferred_element_type=jnp.float32
    )
    d_probs = jnp.einsum(
        "bqhe,bkhe->bhqk", d_context, value_heads, preferred_element_type=jnp.float32
    )
    d_scores = probs_again * (d_probs - jnp.sum(d_probs * probs_again, axis=-1, keepdims=True))
    d_scores_low = d_scores.astype(jnp.bfloat16)
    d_query = (
        jnp.einsum("bhqk,bkhe->bqhe", d_scores_low, key_heads, preferred_element_type=jnp.float32)
        * head_scale
    )
    d_key = (
        jnp.einsum("bhqk,bqhe->bkhe", d_scores_low, query_heads, preferred_element_type=jnp.float32)
        * head_scale
    )
    d_query_low = d_query.astype(jnp.bfloat16).reshape(row_count, model_width)
    d_key_low = d_key.astype(jnp.bfloat16).reshape(row_count, model_width)
    d_value_low = d_value.astype(jnp.bfloat16).reshape(row_count, model_width)
    d_bias_query = jnp.sum(d_query_low.astype(jnp.float32), axis=0)
    d_bias_value = jnp.sum(d_value_low.astype(jnp.float32), axis=0)
    g_qkv = jnp.stack(
        [
            product_left_t(flat_x, d_query_low),
            product_left_t(flat_x, d_key_low),
            product_left_t(flat_x, d_value_low),
        ]
    )
    d_input = (
        d_first
        + product_right_t(d_query_low, qkv_weight[0])
        + product_right_t(d_key_low, qkv_weight[1])
        + product_right_t(d_value_low, qkv_weight[2])
    )
    input_grad = unswap(d_input.astype(jnp.bfloat16).reshape(tab_count, block_rows, model_width))
    small_terms = jnp.concatenate(
        [
            d_gain_one,
            d_gain_two,
            d_shift_one,
            d_shift_two,
            d_bias_query,
            d_bias_value,
            d_bias_attn,
            d_bias_ffn,
            d_bias_inner,
        ]
    )
    shards = lax.axis_size(AXES)
    share_outer = scatter_sum(g_outer.reshape(shards, -1)).reshape(ffn_out_master.shape)
    share_inner = scatter_sum(g_inner.reshape(shards, -1)).reshape(ffn_in_master.shape)
    share_attn = scatter_sum(g_attn.reshape(shards, -1)).reshape(out_master.shape)
    share_qkv = scatter_sum(
        g_qkv.reshape(3, shards, -1).swapaxes(0, 1).reshape(shards, -1)
    ).reshape(qkv_master.shape)
    small_sum = butterfly_sum(small_terms)
    share_sq = (
        jnp.sum(share_qkv * share_qkv)
        + jnp.sum(share_attn * share_attn)
        + jnp.sum(share_inner * share_inner)
        + jnp.sum(share_outer * share_outer)
    )
    total_sq = butterfly_sum(share_sq.reshape(1))[0] + jnp.sum(small_sum * small_sum)
    grad_norm = jnp.sqrt(total_sq)
    clip_limit = math.sqrt(
        float(
            4 * model_width * model_width
            + 2 * model_width * hidden_units
            + 8 * model_width
            + hidden_units
        )
    )
    clip_scale = jnp.minimum(1.0, clip_limit / grad_norm)
    qkv_grad = share_qkv * clip_scale
    out_grad = share_attn * clip_scale
    ffn_in_grad = share_inner * clip_scale
    ffn_out_grad = share_outer * clip_scale
    small_grad = small_sum * clip_scale
    qf, qs, qm, qe = adam_update(
        qkv_grad, qkv_first, qkv_second, qkv_master, qkv_ema, model_width ** (-0.5)
    )
    of, osec, om, oe = adam_update(
        out_grad, out_first, out_second, out_master, out_ema, max(model_width // 128, 1) ** (-0.5)
    )
    inf, ins, inm, ine = adam_update(
        ffn_in_grad, ffn_in_first, ffn_in_second, ffn_in_master, ffn_in_ema, model_width ** (-0.5)
    )
    uf, us, um, ue = adam_update(
        ffn_out_grad,
        ffn_out_first,
        ffn_out_second,
        ffn_out_master,
        ffn_out_ema,
        hidden_units ** (-0.5),
    )
    sf, ss, sm, se = adam_update(
        small_grad, small_first, small_second, small_params, small_ema, SMALL_RATE
    )
    return (
        layer_out,
        input_grad,
        qkv_grad,
        out_grad,
        ffn_in_grad,
        ffn_out_grad,
        small_grad,
        grad_norm,
        qf,
        qs,
        qm,
        qm.astype(jnp.bfloat16),
        qe,
        of,
        osec,
        om,
        om.astype(jnp.bfloat16),
        oe,
        inf,
        ins,
        inm,
        inm.astype(jnp.bfloat16),
        ine,
        uf,
        us,
        um,
        um.astype(jnp.bfloat16),
        ue,
        sf,
        ss,
        sm,
        se,
    )


def solution(mesh):
    in_specs = (
        P("batch", "seq", None),
        P("batch", "seq", None),
        P("batch", None),
        P("batch", None),
        P("batch", None),
        P(),
        P(),
        P(),
        P(),
        P(),
        P(None, ("batch", "seq"), None),
        P(None, ("batch", "seq"), None),
        P(None, ("batch", "seq"), None),
        P(None, ("batch", "seq"), None),
        P(("batch", "seq"), None),
        P(("batch", "seq"), None),
        P(("batch", "seq"), None),
        P(("batch", "seq"), None),
        P(("batch", "seq"), None),
        P(("batch", "seq"), None),
        P(("batch", "seq"), None),
        P(("batch", "seq"), None),
        P(("batch", "seq"), None),
        P(("batch", "seq"), None),
        P(("batch", "seq"), None),
        P(("batch", "seq"), None),
        P(),
        P(),
        P(),
    )
    out_specs = (
        P("batch", "seq", None),
        P("batch", "seq", None),
        P(None, ("batch", "seq"), None),
        P(("batch", "seq"), None),
        P(("batch", "seq"), None),
        P(("batch", "seq"), None),
        P(),
        P(),
        P(None, ("batch", "seq"), None),
        P(None, ("batch", "seq"), None),
        P(None, ("batch", "seq"), None),
        P(None, ("batch", "seq"), None),
        P(None, ("batch", "seq"), None),
        P(("batch", "seq"), None),
        P(("batch", "seq"), None),
        P(("batch", "seq"), None),
        P(("batch", "seq"), None),
        P(("batch", "seq"), None),
        P(("batch", "seq"), None),
        P(("batch", "seq"), None),
        P(("batch", "seq"), None),
        P(("batch", "seq"), None),
        P(("batch", "seq"), None),
        P(("batch", "seq"), None),
        P(("batch", "seq"), None),
        P(("batch", "seq"), None),
        P(("batch", "seq"), None),
        P(("batch", "seq"), None),
        P(),
        P(),
        P(),
        P(),
    )
    return jax.shard_map(body, mesh=mesh, in_specs=in_specs, out_specs=out_specs, check_vma=False)
```

```python
import functools
import math

import jax
import jax.numpy as jnp
from jax import lax
from jax.experimental import pallas as pl
from jax.experimental.pallas import tpu as pltpu
from jax.sharding import PartitionSpec as P

HD = 64
STEP = 10
EPS_NORM = 1e-06
NEG_BIG = -1e30
BETA_ONE = 0.9
BETA_TWO = 0.999
ADAM_EPS = 1e-08
DECAY = 0.01
EMA_KEEP = 0.8
SMALL_RATE = 0.1
AXES = ("batch", "seq")
MESH = pl.DeviceIdType.MESH
VMEM_BYTES = 61 << 20
BF = jnp.bfloat16
F32 = jnp.float32


def nn(left, right):
    return lax.dot_general(left, right, (((1,), (0,)), ((), ())), preferred_element_type=F32)


def nt(left, right):
    return lax.dot_general(left, right, (((1,), (1,)), ((), ())), preferred_element_type=F32)


def tn(left, right):
    return lax.dot_general(left, right, (((0,), (0,)), ((), ())), preferred_element_type=F32)


def row_mean(values):
    return jnp.mean(values, axis=1, keepdims=True)


def column_sum(values):
    return jnp.sum(values, axis=0, keepdims=True)


def gelu_pair(inner):
    size = jnp.abs(inner) * 0.7071067811865476
    t = 1.0 / (1.0 + 0.3275911 * size)
    bell = jnp.exp(inner * inner * -0.5)
    series = (((1.061405429 * t - 1.453152027) * t + 1.421413741) * t - 0.284496736) * t
    half = (series + 0.254829592) * t * (0.5 * bell)
    share = jnp.where(inner > 0, 1.0 - half, half)
    return inner * share, share + inner * bell * 0.3989422804014327


def small_row(packed, index, width):
    lines = width // 128
    return jnp.concatenate([packed[index * lines + i : index * lines + i + 1, :] for i in range(lines)], axis=1)


def head_masks():
    lane = lax.broadcasted_iota(jnp.int32, (1, 2 * HD), 1)
    return (lane < HD, lane >= HD)


def forward_kernel(
    tables_h, cot_h, seg_h, row_h, col_h, wqkv_h, wo_h, w1_h, w2_h, small_h,
    x_o, q_o, k_o, v_o, e_o, rinv_o, ctx_o, h1_o, xh_o, rstd_o, a_o, g_o, dr2_o, lo_o, sg_o,
    x, cot, seg, row, col, wqkv, wo, w1, w2, small, bias, inner_bias,
    q, k, v, e, rinv, ctx, h1, xh, rstd, a, g, dr2, lo, sg, h1f,
    in_sem, out_sem, e_sem, send_sem, recv_sem,
):
    tabs, length, width = x.shape
    block = length // 2
    hidden = w1.shape[1]
    pairs = width // (2 * HD)
    batch, me = lax.axis_index("batch"), lax.axis_index("seq")
    peer = (batch, 1 - me)
    copy = pltpu.make_async_copy
    barrier = pltpu.get_barrier_semaphore()
    pl.semaphore_signal(barrier, inc=1, device_id=peer, device_id_type=MESH)
    own_rows = pl.ds(pl.multiple_of(me * block, block), block)
    peer_rows = pl.ds(pl.multiple_of((1 - me) * block, block), block)

    sources = [(small_h, small), (wqkv_h, wqkv), (seg_h, seg), (row_h, row), (col_h, col)]
    sources += [(wo_h, wo), (w1_h, w1), (w2_h, w2)]
    sources += [(tables_h.at[me * tabs + t], x.at[t, own_rows]) for t in range(tabs)]
    sources += [(cot_h.at[me * tabs + t], cot.at[t, own_rows]) for t in range(tabs)]
    loads = [copy(src, dst, in_sem.at[i]) for i, (src, dst) in enumerate(sources)]
    for i in (8, 9, 1, 0, 2, 3, 4, 5, 6, 7, 10, 11):
        loads[i].start()

    def swap(index):
        source, place = (tables_h, x) if index < tabs else (cot_h, cot)
        t = index % tabs
        return pltpu.make_async_remote_copy(
            src_ref=source.at[(1 - me) * tabs + t],
            dst_ref=place.at[t, own_rows],
            send_sem=send_sem.at[index],
            recv_sem=recv_sem.at[index],
            device_id=peer,
            device_id_type=MESH,
        )

    pl.semaphore_wait(barrier, 1)
    for index in range(2 * tabs):
        swap(index).start()

    stores = []

    def store(index, src, dst):
        stores.append(copy(src, dst, out_sem.at[index]))
        stores[-1].start()

    for i in (0, 1, 8, 9):
        loads[i].wait()
    gain1, gain2, shift1, shift2, bias_q, bias_v, bias_o, bias_f2 = (
        small_row(small, i, width) for i in range(8)
    )
    inner_bias[...] = small_row(small[8 * (width // 128) :, :], 0, hidden)
    masks = head_masks()
    zero = jnp.zeros((), BF)

    def project(t, rows):
        block_x = x[t, rows, :]
        q[t, rows, :] = ((nn(block_x, wqkv[0]) + bias_q) * (HD**-0.5)).astype(BF)
        k[t, rows, :] = nn(block_x, wqkv[1]).astype(BF)
        v[t, rows, :] = (nn(block_x, wqkv[2]) + bias_v).astype(BF)

    for t in range(tabs):
        project(t, own_rows)
    for i in (2, 3, 4):
        loads[i].wait()
    for t in range(tabs):
        keys = [ids[pl.ds(me * tabs + t, 1), :].astype(F32) for ids in (seg, row, col)]
        wide = [jnp.transpose(jnp.broadcast_to(ids, (128, length)))[:, 0:1] for ids in keys]
        seen = (wide[0] == 0.0) | (keys[0] == 0.0)
        seen = seen | (wide[1] == keys[1]) | (wide[2] == keys[2])
        bias[t] = jnp.where(seen, 0.0, NEG_BIG).astype(BF)

    for t in range(tabs):
        swap(t).wait_recv()
        project(t, peer_rows)
        store(16 * t + 14, x.at[t], x_o.at[t])

        def pair(hp, carry):
            lanes = pl.ds(pl.multiple_of(hp * 2 * HD, 2 * HD), 2 * HD)
            slot = lax.rem(hp, 2)

            @pl.when(t * pairs + hp >= 2)
            def _():
                copy(e.at[slot], e_o.at[0, 0], e_sem.at[slot]).wait()

            q2, k2, v2 = q[t, :, lanes], k[t, :, lanes], v[t, :, lanes]
            one = jnp.ones((length, 2 * HD), BF)
            off = bias[t].astype(F32)
            for h in range(2):
                scores = nt(jnp.where(masks[h], q2, zero), k2) + off
                top = jnp.max(scores, axis=1, keepdims=True)
                e[slot, :, h * length : (h + 1) * length] = jnp.exp(scores - top).astype(BF)
            right = [
                jnp.concatenate([jnp.where(m, v2, zero), jnp.where(m, one, zero)], axis=1)
                for m in masks
            ]
            both = nn(e[slot], jnp.concatenate(right, axis=0))
            inverse = 1.0 / both[:, 2 * HD :]
            rinv[t, :, lanes] = inverse.astype(BF)
            ctx[t, :, lanes] = (both[:, : 2 * HD] * inverse).astype(BF)
            copy(e.at[slot], e_o.at[t, hp], e_sem.at[slot]).start()
            return carry

        lax.fori_loop(0, pairs, pair, 0)
        for i, (src, dst) in enumerate(((q, q_o), (k, k_o), (v, v_o), (rinv, rinv_o), (ctx, ctx_o))):
            store(16 * t + i, src.at[t], dst.at[t])
        if t == 0:
            loads[5].wait()
        sum1 = x[t].astype(F32) + nn(ctx[t], wo[...]) + bias_o
        centre = sum1 - row_mean(sum1)
        scale = lax.rsqrt(row_mean(centre * centre) + EPS_NORM)
        unit = centre * scale
        xh[t] = unit.astype(BF)
        rstd[t] = jnp.broadcast_to(scale, (length, 128))
        normed = unit * gain1 + shift1
        h1f[...] = normed
        h1[t] = normed.astype(BF)
        for i, (src, dst) in enumerate(((h1, h1_o), (xh, xh_o), (rstd, rstd_o))):
            store(16 * t + 5 + i, src.at[t], dst.at[t])
        if t == 0:
            loads[6].wait()
        rows = pl.ds(t * length, length)
        step = 256

        def inner(j, carry):
            for sub in range(width // step):
                here = slice(sub * step, (sub + 1) * step)
                there = pl.ds(pl.multiple_of(j * width + sub * step, step), step)
                active, slope = gelu_pair(nn(h1[t], w1[:, there]) + inner_bias[0:1, there])
                a[j, rows, here] = active.astype(BF)
                g[j, rows, here] = slope.astype(BF)
            return carry

        lax.fori_loop(0, hidden // width, inner, 0)
        store(16 * t + 8, a.at[:, rows], a_o.at[:, rows])
        store(16 * t + 9, g.at[:, rows], g_o.at[:, rows])
        if t == 0:
            loads[7].wait()
        sum2 = h1f[...] + bias_f2
        for j in range(hidden // width):
            sum2 = sum2 + nn(a[j, rows, :], w2[j * width : (j + 1) * width, :])
        centre = sum2 - row_mean(sum2)
        scale = lax.rsqrt(row_mean(centre * centre) + EPS_NORM)
        unit = centre * scale
        lo[t] = (unit * gain2 + shift2).astype(BF)
        loads[10 + t].wait()
        swap(tabs + t).wait_recv()
        back = cot[t].astype(F32)
        d_unit = back * gain2
        d_sum2 = scale * (d_unit - row_mean(d_unit) - unit * row_mean(d_unit * unit))
        dr2[t] = d_sum2
        parts = [column_sum(back * unit), column_sum(back), column_sum(d_sum2.astype(BF).astype(F32))]
        parts = jnp.concatenate(parts + [jnp.zeros((5, width), F32)], axis=0)
        sg[...] = parts if t == 0 else sg[...] + parts
        store(16 * t + 10, dr2.at[t], dr2_o.at[t])
        store(16 * t + 11, lo.at[t], lo_o.at[t])
    store(12, sg, sg_o)
    for stored in stores:
        stored.wait()
    for slot in range(2):
        copy(e.at[slot], e_o.at[0, 0], e_sem.at[slot]).wait()
    for index in range(2 * tabs):
        swap(index).wait_send()


def anywhere(count):
    return [pl.BlockSpec(memory_space=pl.ANY)] * count


def forward(tables_in, out_cot, seg, row, col, wqkv, wo, w1, w2, small):
    tabs, length = tables_in.shape[0] // 2, tables_in.shape[1] * 2
    width, hidden = w1.shape
    pairs, chunks, rows = width // (2 * HD), hidden // width, tabs * length
    shape = jax.ShapeDtypeStruct
    act = shape((tabs, length, width), BF)
    wide = shape((chunks, rows, width), BF)
    outs = [act] * 4 + [shape((tabs, pairs, length, 2 * length), BF)] + [act] * 4
    outs += [shape((tabs, length, 128), F32), wide, wide, shape(act.shape, F32), act]
    outs += [shape((8, width), F32)]
    ins = (tables_in, out_cot, seg, row, col, wqkv, wo, w1, w2, small)
    like = lambda array: pltpu.VMEM(array.shape, array.dtype)
    scratch = [like(act), like(act)] + [like(array) for array in ins[2:]]
    scratch += [pltpu.VMEM((tabs, length, length), BF), pltpu.VMEM((1, hidden), F32)]
    scratch += [like(array) for array in outs[1:4]] + [pltpu.VMEM((2, length, 2 * length), BF)]
    scratch += [like(array) for array in outs[5:]] + [pltpu.VMEM((length, width), F32)]
    dma = pltpu.SemaphoreType.DMA
    return pl.pallas_call(
        forward_kernel,
        out_shape=outs,
        in_specs=anywhere(len(ins)),
        out_specs=anywhere(len(outs)),
        scratch_shapes=scratch + [dma((16,)), dma((16 * tabs,)), dma((2,)), dma((8,)), dma((8,))],
        compiler_params=pltpu.CompilerParams(
            vmem_limit_bytes=VMEM_BYTES, collective_id=0, has_side_effects=True
        ),
        name="layer_forward",
    )(*ins)


class Link:
    FIRST_Y = ("core", "y", "z", "w", "x")
    FIRST_Z = ("core", "z", "w", "y", "x")

    def __init__(self, rest, g2, g1, full, sm, grad, lo_h, outs):
        (self.half2, self.z2, self.w2, self.y2, self.x2, self.half, self.two, self.one, self.last) = rest[:9]
        (self.x_send, self.x_get, self.final2, self.final, self.slots8, self.slots4) = rest[9:15]
        (self.square8, self.square4, self.send_sem, self.recv_sem, self.own_sem) = rest[15:]
        self.g2, self.g1, self.full, self.sm, self.grad = g2, g1, full, sm, grad
        self.lo_h, self.outs = lo_h, outs
        batch, seq = lax.axis_index("batch"), lax.axis_index("seq")
        self.batch, self.seq = batch, seq
        self.bit = {
            "core": lax.rem(batch, 2),
            "y": lax.rem(batch // 2, 2),
            "z": lax.rem(batch // 4, 2),
            "w": batch // 8,
            "x": seq,
        }
        self.jump = {"core": 1, "y": 2, "z": 4, "w": 8}
        count = g1.shape[0] + 4
        self.state = [0] * count
        self.memo = None
        self.order = [self.FIRST_Y] * count
        self.held = [["w", "z", "y"] for _ in range(count)]
        self.near = [None] + [tuple(n for b, n in ((1, "x"), (2, "core"), (4, "y")) if m & b) for m in range(1, 8)]
        self.far = [None] + [tuple(n for b, n in ((1, "z"), (2, "w")) if m & b) for m in range(1, 4)]

    def device(self, names):
        batch, seq = self.batch, self.seq
        for name in names:
            if name == "x":
                seq = 1 - seq
            else:
                batch = batch + self.jump[name] * (1 - 2 * self.bit[name])
        return (batch, seq)

    def remote(self, index, src, dst, names):
        return pltpu.make_async_remote_copy(
            src_ref=src,
            dst_ref=dst,
            send_sem=self.send_sem.at[index],
            recv_sem=self.recv_sem.at[index],
            device_id=self.device(names),
            device_id_type=MESH,
        )

    def source(self, chunk):
        kept = self.g1.shape[0]
        other = 1 - self.bit["core"]
        if chunk < kept:
            return self.g1.at[chunk, :, :, :, other]
        return self.full.at[(chunk + 3) % 4, :, :, :, other, pl.ds(0, self.g1.shape[-2])]

    def own(self, chunk):
        kept = self.g1.shape[0]
        core = self.bit["core"]
        if chunk < kept:
            return self.g1[chunk, :, :, :, core]
        return self.full[(chunk + 3) % 4, :, :, :, core, 0 : self.g1.shape[-2]]

    def pick(self, chunk, name, other):
        value = 1 - self.bit[name] if other else self.bit[name]
        return tuple(value if axis == name else slice(None) for axis in self.held[chunk])

    def phase(self, chunk, number):
        name = self.order[chunk][number]
        index = chunk * 5 + number
        if name == "core":
            return self.remote(index, self.source(chunk), self.half.at[chunk], (name,))
        if name == "x":
            return self.remote(index, self.x_send.at[chunk], self.x_get.at[chunk], (name,))
        stages = [self.half, self.two, self.one, self.last]
        src = stages[number - 1].at[(chunk,) + self.pick(chunk, name, True)]
        return self.remote(index, src, stages[number].at[chunk], (name,))

    def begin(self, chunk):
        self.phase(chunk, 0).start()

    def advance(self, *chunks):
        for chunk in chunks:
            number = self.state[chunk]
            name = self.order[chunk][number]
            stages = [self.half, self.two, self.one, self.last]
            self.phase(chunk, number).wait_recv()
            if name == "x":
                rows = self.final.shape[1]
                total = self.final[chunk] + self.x_get[chunk].astype(F32)[0:rows]
                self.final[chunk] = total
                self.state[chunk] = 5
                continue
            if name == "core":
                kept = self.own(chunk)
            else:
                kept = stages[number - 1][(chunk,) + self.pick(chunk, name, False)]
                self.held[chunk].remove(name)
            total = stages[number][chunk].astype(F32) + kept.astype(F32)
            if number < 3:
                stages[number][chunk] = total.astype(BF)
            else:
                rows = total.shape[0] // 2
                low, high = total[0:rows], total[rows:]
                upper = self.seq == 1
                self.final[chunk] = jnp.where(upper, high, low)
                pad = jnp.zeros((self.x_send.shape[1] - rows, low.shape[1]), F32)
                gone = jnp.concatenate([jnp.where(upper, low, high), pad], axis=0)
                self.x_send[chunk] = gone.astype(BF)
            self.state[chunk] = number + 1
            self.phase(chunk, number + 1).start()

    def core2(self, j):
        src = self.g2.at[j, :, 1 - self.bit["core"]]
        return self.remote(40 + j, src, self.half2.at[j // 2, j % 2], ("core",))

    def core2_done(self, *which):
        for j in which:
            self.core2(j).wait_recv()
            kept = self.g2[j, :, self.bit["core"]].astype(F32)
            self.half2[j // 2, j % 2] = (self.half2[j // 2, j % 2].astype(F32) + kept).astype(BF)

    def copy_z2(self, y):
        src = self.half2.at[:, 1 - self.bit["z"], y]
        return self.remote(44 + y, src, self.z2.at[y], ("z",))

    def copy_w2(self, y):
        return self.remote(46 + y, self.z2.at[y, 1 - self.bit["w"]], self.w2.at[y], ("w",))

    def copy_y2(self):
        return self.remote(48, self.w2.at[1 - self.bit["y"]], self.y2, ("y",))

    def copy_x2(self):
        rows = self.x2.shape[0]
        there = pl.ds(pl.multiple_of((1 - self.seq) * rows, rows), rows)
        return self.remote(49, self.y2.at[there], self.x2, ("x",))

    def z2_done(self, y):
        self.copy_z2(y).wait_recv()
        kept = self.half2[:, self.bit["z"], y].astype(F32)
        self.z2[y] = (self.z2[y].astype(F32) + kept).astype(BF)
        self.copy_w2(y).start()

    def w2_done(self, y):
        self.copy_w2(y).wait_recv()
        kept = self.z2[y, self.bit["w"]].astype(F32)
        self.w2[y] = (self.w2[y].astype(F32) + kept).astype(BF)

    def y2_done(self):
        self.copy_y2().wait_recv()
        kept = self.w2[self.bit["y"]].astype(F32)
        self.y2[...] = (self.y2[...].astype(F32) + kept).astype(BF)
        self.copy_x2().start()

    def x2_done(self):
        self.copy_x2().wait_recv()
        rows = self.x2.shape[0]
        here = pl.ds(pl.multiple_of(self.seq * rows, rows), rows)
        self.final2[...] = self.y2[here, :].astype(F32) + self.x2[...].astype(F32)

    def back(self, index, src, table, tabs):
        block = self.outs[0].shape[1]
        there = pl.ds(pl.multiple_of((1 - self.seq) * block, block), block)
        dst = self.outs[1 if index == 50 else 0]
        if index == 50:
            return self.remote(50, src.at[:, there], dst.at[pl.ds(self.seq * tabs, tabs)], ("x",))
        rows = pl.ds(pl.multiple_of(table * 2 * block + (1 - self.seq) * block, block), block)
        return self.remote(index, src.at[rows], dst.at[self.seq * tabs + table], ("x",))

    def keep(self, index, src, table, tabs):
        block = self.outs[0].shape[1]
        sem = self.own_sem.at[index - 50]
        dst = self.outs[1 if index == 50 else 0]
        here = pl.ds(pl.multiple_of(self.seq * block, block), block)
        if index == 50:
            return pltpu.make_async_copy(src.at[:, here], dst.at[pl.ds(self.seq * tabs, tabs)], sem)
        rows = pl.ds(pl.multiple_of(table * 2 * block + self.seq * block, block), block)
        return pltpu.make_async_copy(src.at[rows], dst.at[self.seq * tabs + table], sem)

    def spread(self, base, slots, groups):
        return [
            self.remote(base + m, slots.at[0], slots.at[m], groups[m])
            for m in range(1, len(groups))
        ]

    def gathered(self, base, slots, groups):
        for sent in self.spread(base, slots, groups):
            sent.wait_recv()
        terms = [slots[m] for m in range(len(groups))]
        while len(terms) > 1:
            terms = [terms[i] + terms[i + 1] for i in range(0, len(terms), 2)]
        return terms[0]

    def quiet(self, act):
        act()

    def start_all(self, copies):
        for each in copies:
            each.start()

    def at(self, name, n=None):
        tabs = self.lo_h.shape[0]
        if name == "enter":
            barrier = pltpu.get_barrier_semaphore()
            for names in self.near[1:] + self.far[1:]:
                pl.semaphore_signal(barrier, inc=1, device_id=self.device(names), device_id_type=MESH)
        elif name == "outer":
            if n == 0:
                pl.semaphore_wait(pltpu.get_barrier_semaphore(), len(self.near) + len(self.far) - 2)
            self.core2(n).start()
            if n == 0:
                self.back(50, self.lo_h, 0, tabs).start()
                self.keep(50, self.lo_h, 0, tabs).start()
        elif name == "slope":
            if n == 0:
                self.core2_done(0, 1)
            if n == 1:
                self.core2_done(2, 3)
                for y in range(2):
                    self.copy_z2(y).start()
        elif name == "inner":
            self.begin(n)
            if n:
                self.advance(n - 1)
        elif name == "norm":
            if n == 0:
                self.advance(3)
            else:
                self.z2_done(0)
                self.advance(0)
        elif name == "attn":
            self.begin(4)
        elif name == "context":
            self.advance(4, 1, 0)
        elif name == "attend":
            plan = {
                1: lambda: self.z2_done(1),
                3: lambda: (self.begin(5), self.advance(2, 1, 0)),
                4: lambda: self.advance(5),
                6: lambda: (self.w2_done(0), self.advance(3, 2, 1)),
                7: lambda: self.begin(6),
                8: lambda: self.advance(6, 0),
                9: lambda: (self.w2_done(1), self.copy_y2().start(), self.advance(4, 3, 2)),
                11: lambda: self.begin(7),
            }
            if self.memo is None:
                self.memo = (list(self.state), [list(held) for held in self.held])
            self.state, self.held = list(self.memo[0]), [list(held) for held in self.memo[1]]
            for k, act in plan.items():
                pl.when(n == k)(functools.partial(self.quiet, act))
        elif name == "attended":
            self.slots8[0] = self.sm[...]
            self.start_all(self.spread(53, self.slots8, self.near))
            self.advance(7, 5, 4, 3)
        elif name == "input":
            src = self.grad
            self.back(51 + n, src, n, tabs).start()
            self.keep(51 + n, src, n, tabs).start()
            if n == 0:
                total = self.gathered(53, self.slots8, self.near)
                self.slots4[0] = total
                self.start_all(self.spread(60, self.slots4, self.far))
            else:
                self.sm[...] = self.gathered(60, self.slots4, self.far)
        elif name == "leave":
            self.finish(tabs)

    def finish(self, tabs):
        self.y2_done()
        left = [c for c in range(len(self.state)) if self.state[c] < 5]
        while left:
            left.sort(key=lambda c: -self.state[c])
            self.advance(*left)
            left = [c for c in range(len(self.state)) if self.state[c] < 5]
        self.x2_done()
        fold = lambda values: sum(
            (values * values)[:, i * 128 : (i + 1) * 128] for i in range(values.shape[1] // 128)
        )
        tile = lambda rows: jnp.sum(rows.reshape(rows.shape[0] // 8, 8, 128), axis=0)
        square = tile(fold(self.final2[...]))
        for chunk in range(len(self.state)):
            square = square + tile(fold(self.final[chunk]))
        ends = [(self.final2, self.outs[2]), (self.final, self.outs[3]), (self.sm, self.outs[4])]
        ends = [pltpu.make_async_copy(src, dst, self.own_sem.at[3 + i]) for i, (src, dst) in enumerate(ends)]
        self.start_all(ends)
        self.square8[0] = square
        self.start_all(self.spread(64, self.square8, self.near))
        self.square4[0] = self.gathered(64, self.square8, self.near)
        self.start_all(self.spread(71, self.square4, self.far))
        small = tile(fold(self.sm[...]))
        whole = self.gathered(71, self.square4, self.far) + small
        end = pltpu.make_async_copy(self.square8.at[0], self.outs[5], self.own_sem.at[6])
        for chunk in range(len(self.state)):
            self.held[chunk] = ["w", "z", "y"]
            for number in range(5):
                self.phase(chunk, number).wait_send()
                name = self.order[chunk][number]
                if name in self.held[chunk]:
                    self.held[chunk].remove(name)
        sent = [self.core2(j) for j in range(4)] + [self.copy_z2(y) for y in range(2)]
        sent += [self.copy_w2(y) for y in range(2)] + [self.copy_y2(), self.copy_x2()]
        sent += [self.back(50, self.lo_h, 0, tabs)]
        sent += [self.back(51 + t, self.grad, t, tabs) for t in range(tabs)]
        sent += self.spread(53, self.slots8, self.near) + self.spread(60, self.slots4, self.far)
        for each in sent:
            each.wait_send()
        for each in self.spread(64, self.square8, self.near) + self.spread(71, self.square4, self.far):
            each.wait_send()
        self.square8[0] = whole
        end.start()
        self.back(50, self.lo_h, 0, tabs).wait_recv()
        self.keep(50, self.lo_h, 0, tabs).wait()
        for t in range(tabs):
            self.back(51 + t, self.grad, t, tabs).wait_recv()
            self.keep(51 + t, self.grad, t, tabs).wait()
        for each in ends:
            each.wait()
        end.wait()


def backward_kernel(
    count, a_h, g_h, dr2_h, h1_h, xh_h, rstd_h, rinv_h, ctx_h, q_h, k_h, v_h, x_h, e_h, lo_h,
    wqkv_h, wo_h, w1_h, w2_h, small_h, sg_h,
    *rest,
):
    outs, rest = rest[:count], rest[count:]
    A, U, W, WO, dr, df, h1, rstd, ctx, e, small, sm, g2, g1 = rest[:14]
    in_sem, e_sem, out_sem = rest[14:17]
    chunks, rows, width = A.shape
    tabs, pairs, length, _ = e_h.shape
    share = g1.shape[-2]
    corner = (slice(None),) * (len(U.shape) - 3) + (slice(0, share),)
    copy = pltpu.make_async_copy
    link = Link(rest[17:], g2, g1, U, sm, h1, lo_h, outs) if len(rest) > 17 else None
    loads = {}
    used = [0]

    def load(name, *both):
        loads[name] = []
        for src, dst in both:
            loads[name].append(copy(src, dst, in_sem.at[used[0]]))
            used[0] += 1
            loads[name][-1].start()

    def need(*names):
        for name in names:
            for loaded in loads[name]:
                loaded.wait()

    load("dr2", (dr2_h, dr))
    load("a", *[(a_h.at[j], A.at[j]) for j in range(chunks)])
    load("small", (small_h, small), (sg_h, sm.at[pl.ds(0, 8)]))
    load("w2", (w2_h, W))
    load("g", *[(g_h.at[j], U.at[j]) for j in range(chunks)])
    load("h1", (h1_h, h1))
    load("rstd", (rstd_h, rstd))
    load("wo", (wo_h, WO))
    load("ctx", (ctx_h, ctx))
    at = link.at if link else (lambda *key: None)
    at("enter")
    half = rows // 2
    halves = [slice(i * half, (i + 1) * half) for i in range(2)]
    inside = U.shape[2:]
    take = lambda j, i: U[j, i].reshape(half, width)
    need("small", "dr2")
    first = sm[0:8, :]
    blank = jnp.zeros((1, width), F32)
    order = [blank, first[0:1], blank, first[1:2], blank, blank, blank, first[2:3]]
    sm[...] = jnp.concatenate(order + [jnp.zeros((8, width), F32)], axis=0)
    gain1 = small_row(small, 0, width)
    df[...] = dr[...].astype(BF)

    for j in range(chunks):
        loads["a"][j].wait()
        g2[j] = tn(A[j], df[...]).astype(BF).reshape(g2.shape[1:])
        at("outer", j)
    load("qkv", *[(src, A.at[i]) for i, src in enumerate((q_h, k_h, v_h))])
    load("unit", (xh_h, A.at[3]))

    need("w2")
    for j in range(chunks):
        loads["g"][j].wait()
        total = blank
        for i, half_rows in enumerate(halves):
            d_active = nt(df[half_rows, :], W[j * width : (j + 1) * width, :])
            d_inner = (d_active * take(j, i).astype(F32)).astype(BF)
            U[j, i] = d_inner.reshape(inside)
            total = total + column_sum(d_inner.astype(F32))
        sm[8 + j : 9 + j, :] = total
        at("slope", j)
    load("w1", *[(w1_h.at[:, pl.ds(j * width, width)], W.at[pl.ds(j * width, width)]) for j in range(chunks)])

    need("h1")
    for j in range(chunks):
        g1[j] = tn(h1[...], U[j].reshape(rows, width)).astype(BF).reshape(g1.shape[1:])
        at("inner", j)

    load("rinv", (rinv_h, h1))
    need("w1", "rstd", "unit")
    d_gain, d_shift, d_bias = blank, blank, blank
    for i, half_rows in enumerate(halves):
        d_normed = dr[half_rows, :]
        for j in range(chunks):
            d_normed = d_normed + nt(take(j, i), W[j * width : (j + 1) * width, :])
        unit = A[3, half_rows, :].astype(F32)
        d_shift = d_shift + column_sum(d_normed)
        d_gain = d_gain + column_sum(d_normed * unit)
        d_unit = d_normed * gain1
        d_sum1 = d_unit - row_mean(d_unit) - unit * row_mean(d_unit * unit)
        d_sum1 = rstd[half_rows, 0:1] * d_sum1
        dr[half_rows, :] = d_sum1
        d_attn = d_sum1.astype(BF)
        df[half_rows, :] = d_attn
        d_bias = d_bias + column_sum(d_attn.astype(F32))
        at("norm", i)
    load("wqkv", (wqkv_h, W.at[pl.ds(0, 3 * width)]))
    load("x", (x_h, A.at[3]))
    sm[0:1, :] = d_gain
    sm[2:3, :] = d_shift
    sm[6:7, :] = d_bias

    need("ctx", "wo")
    U[(3,) + corner] = tn(ctx[...], df[...]).astype(BF).reshape(g1.shape[1:])
    at("attn")
    need("rinv")
    for half_rows in halves:
        d_ctx = nt(df[half_rows, :], WO[...]) * h1[half_rows, :].astype(F32)
        df[half_rows, :] = d_ctx.astype(BF)
    at("context")

    need("qkv", "x")
    masks = head_masks()
    zero = jnp.zeros((), BF)
    groups = 3
    wide = width // groups
    per_table = wide // (2 * HD)
    per_group = tabs * per_table
    steps = groups * per_group

    def place(n):
        table = lax.rem(n, per_group) // per_table
        return table, (n // per_group) * per_table + lax.rem(n, per_table)

    def fetch(n, slot):
        table, hp = place(n)
        copy(e_h.at[table, hp], e.at[slot], e_sem.at[slot]).start()

    fetch(0, 0)

    def attend(n, carry):
        table, hp = place(n)
        slot = lax.rem(n, 2)

        @pl.when(n + 1 < steps)
        def _():
            fetch(n + 1, 1 - slot)

        lanes = pl.ds(pl.multiple_of(hp * 2 * HD, 2 * HD), 2 * HD)
        here = pl.ds(pl.multiple_of(table * length, length), length)
        q2, k2, v2 = (A[i, here, lanes] for i in range(3))
        d_ctx = df[here, lanes]
        less = (-(ctx[here, lanes].astype(F32) * d_ctx.astype(F32))).astype(BF)
        right = jnp.concatenate([v2, jnp.ones((length, 2 * HD), BF)], axis=1)
        copy(e_h.at[0, 0], e.at[slot], e_sem.at[slot]).wait()
        d_query = d_key = d_value = None
        for h in range(2):
            mine = lambda values: jnp.where(masks[h], values, zero)
            d_head = mine(d_ctx)
            weights = e[slot, :, h * length : (h + 1) * length]
            d_raw = nt(jnp.concatenate([d_head, mine(less)], axis=1), right)
            d_scores = (weights.astype(F32) * d_raw).astype(BF)
            add = lambda held, new: new if held is None else held + new
            d_value = add(d_value, tn(weights, d_head))
            d_key = add(d_key, tn(d_scores, mine(q2)))
            d_query = add(d_query, nn(d_scores, mine(k2)))
        d_query = (d_query * (HD**-0.5)).astype(BF)
        d_value = d_value.astype(BF)
        A[0, here, lanes] = d_query
        A[1, here, lanes] = d_key.astype(BF)
        A[2, here, lanes] = d_value
        sm[4:5, lanes] = sm[4:5, lanes] + column_sum(d_query.astype(F32))
        sm[5:6, lanes] = sm[5:6, lanes] + column_sum(d_value.astype(F32))

        @pl.when(lax.rem(n, per_group) == per_group - 1)
        def _():
            g = n // per_group
            cols = pl.ds(pl.multiple_of(g * wide, wide), wide)
            grads = jnp.concatenate([A[i, :, cols] for i in range(3)], axis=1)
            U[(g,) + corner] = tn(A[3], grads).astype(BF).reshape(g1.shape[1:])

        at("attend", n)
        return carry

    lax.fori_loop(0, steps, attend, 0)
    at("attended")
    need("wqkv")
    for i, half_rows in enumerate(halves):
        d_input = dr[half_rows, :]
        for j in range(3):
            d_input = d_input + nt(A[j, half_rows, :], W[j * width : (j + 1) * width, :])
        h1[half_rows, :] = d_input.astype(BF)
        at("input", i)
    if link:
        at("leave")
        return
    pieces = [(h1, outs[0]), (g2, outs[1]), (g1, outs[2]), (U.at[3, :, pl.ds(0, share)], outs[3]), (sm, outs[4])]
    pieces += [(U.at[i, :, pl.ds(0, share)], outs[5].at[i]) for i in range(3)]
    ends = [copy(src, dst, out_sem.at[i]) for i, (src, dst) in enumerate(pieces)]
    for end in ends:
        end.start()
    for end in ends:
        end.wait()


def backward(saved, weights, small, mesh_bits):
    (x, q, k, v, e, rinv, ctx, h1, xh, rstd, a, g, dr2, lo, sg) = saved
    wqkv, wo, w1, w2 = weights
    chunks, rows, width = a.shape
    hidden = w1.shape[1]
    tabs, length = x.shape[:2]
    shape = jax.ShapeDtypeStruct
    linked = mesh_bits == (4, 1) and width % 256 == 0 and chunks == 4
    lead = (2, 2, 2, 2) if linked else (2,)
    share, part = width // math.prod(lead), rows // math.prod(lead)
    flat = lambda array: array.reshape(rows, array.shape[-1])
    g2 = shape((chunks, 2, 2, width // 4, width) if linked else (chunks, width, width), BF)
    g1 = shape((chunks,) + lead + (share, width), BF)
    go = shape(lead + (share, width), BF)
    small_sum = shape((16, width), F32)
    ins = (a, g.reshape((chunks,) + lead + (part, width)))
    ins += tuple(flat(array) for array in (dr2, h1, xh, rstd, rinv, ctx, q, k, v, x))
    ins += (e, lo, wqkv.reshape(3 * width, width), wo, w1, w2, small, sg)
    mem, dma = pltpu.VMEM, pltpu.SemaphoreType.DMA
    act = mem((rows, width), BF)
    scratch = [mem(a.shape, BF), mem(ins[1].shape, BF), mem(w2.shape, BF), mem(wo.shape, BF)]
    scratch += [mem((rows, width), F32), act, act, mem((rows, 128), F32), act]
    scratch += [mem((2,) + e.shape[2:], BF), mem(small.shape, F32), mem(small_sum.shape, F32)]
    scratch += [mem(array.shape, BF) for array in (g2, g1)]
    scratch += [dma((32,)), dma((2,)), dma((8,))]
    if linked:
        blocks = shape((2 * tabs, length // 2, width), BF)
        quarter, count, half = width // 4, chunks + 4, share // 2
        outs = [blocks, blocks, shape((quarter // 2, width), F32), shape((count, half, width), F32)]
        outs += [small_sum, shape((8, 128), F32)]
        scratch += [mem((2, 2, 2, quarter, width), BF), mem((2, 2, quarter, width), BF)]
        scratch += [mem((2, quarter, width), BF), mem((quarter, width), BF), mem((quarter // 2, width), BF)]
        scratch += [mem((count,) + (2,) * i + (share, width), BF) for i in (3, 2, 1, 0)]
        scratch += [mem((count, 32, width), BF)] * 2
        scratch += [mem(outs[2].shape, F32), mem(outs[3].shape, F32)]
        scratch += [mem((8,) + small_sum.shape, F32), mem((4,) + small_sum.shape, F32)]
        scratch += [mem((8, 8, 128), F32), mem((4, 8, 128), F32)]
        scratch += [dma((80,)), dma((80,)), dma((8,))]
        params = pltpu.CompilerParams(
            vmem_limit_bytes=VMEM_BYTES, collective_id=1, has_side_effects=True
        )
    else:
        outs = [shape((rows, width), BF), g2, g1, go, small_sum, shape((3,) + go.shape, BF)]
        params = pltpu.CompilerParams(vmem_limit_bytes=VMEM_BYTES)
    return linked, pl.pallas_call(
        functools.partial(backward_kernel, len(outs)),
        out_shape=outs,
        in_specs=anywhere(len(ins)),
        out_specs=anywhere(len(outs)),
        scratch_shapes=scratch,
        compiler_params=params,
        name="layer_backward",
    )(*ins)


def adam_update(grad_new, first, second, master, ema_old, rate):
    first_new = BETA_ONE * first + (1.0 - BETA_ONE) * grad_new
    second_new = BETA_TWO * second + (1.0 - BETA_TWO) * grad_new * grad_new
    fix_one = 1.0 - BETA_ONE**STEP
    fix_two = 1.0 - BETA_TWO**STEP
    master_new = master - rate * (
        first_new / fix_one / (jnp.sqrt(second_new / fix_two) + ADAM_EPS) + DECAY * master
    )
    ema_new = EMA_KEEP * ema_old + (1.0 - EMA_KEEP) * master_new
    return (first_new, second_new, master_new, ema_new)


def update_kernel(rates, clip_limit, names, *refs):
    total_in, outer_in, final_in, sum_in = refs[:4]
    states_in = [refs[4 + 4 * i : 8 + 4 * i] for i in range(5)]
    count_out = 6 * 4 + 5 + 1
    outs = refs[24 : 24 + count_out]
    refs = refs[24 + count_out :]
    total, outer, final, sums = refs[:4]
    states = [refs[4 + 4 * i : 8 + 4 * i] for i in range(5)]
    held = refs[24 : 24 + count_out]
    in_sem, out_sem = refs[24 + count_out :]
    copy = pltpu.make_async_copy
    loads = []

    def load(src, dst):
        loads.append(copy(src, dst, in_sem.at[len(loads)]))
        loads[-1].start()

    for src, dst in zip((total_in, outer_in, final_in, sum_in), (total, outer, final, sums)):
        load(src, dst)
    for group in range(5):
        for src, dst in zip(states_in[group], states[group]):
            load(src, dst)
    ends = []

    def end(index):
        ends.append(copy(held[index], outs[index], out_sem.at[index]))
        ends[-1].start()

    width = outer.shape[-1]
    for i in range(4):
        loads[i].wait()
    norm = jnp.sqrt(jnp.sum(jnp.sum(total[...], axis=0, keepdims=True), axis=1, keepdims=True))
    scale = jnp.minimum(1.0, clip_limit / norm)
    held[29][...] = norm
    end(29)
    third = width // 3
    for group in range(5):
        for i in range(4):
            loads[4 + 4 * group + i].wait()
        state = states[group]
        base = 6 * group
        kinds = held[base : base + (5 if group == 4 else 6)]
        if group == 0:
            spots = [(outer[...], (slice(None),))]
        elif group == 1:
            spots = [(final[j], (slice(None), slice(j * width, (j + 1) * width))) for j in range(4)]
        elif group == 2:
            spots = [(final[4], (slice(None),))]
        elif group == 3:
            spots = [
                (final[5 + j][:, i * third : (i + 1) * third], (i, slice(None), slice(j * third, (j + 1) * third)))
                for i in range(3)
                for j in range(3)
            ]
        else:
            lines = width // 128
            packed = [
                sums[r : r + 1, i * 128 : (i + 1) * 128]
                for r in range(kinds[0].shape[0] // lines)
                for i in range(lines)
            ]
            spots = [(jnp.concatenate(packed, axis=0), (slice(None),))]
        for summed, spot in spots:
            grad = summed * scale
            first, second, master, ema = adam_update(
                grad, state[1][spot], state[2][spot], state[0][spot], state[3][spot], rates[group]
            )
            if group == 4:
                results = (grad, first, second, master, ema)
            else:
                results = (grad, first, second, master, master.astype(BF), ema)
            for kind, result in zip(kinds, results):
                kind[spot] = result
        for i in range(len(kinds)):
            end(base + i)
    for each in ends:
        each.wait()


def update(total, outer, final, sums, states, rates, clip_limit):
    shape = jax.ShapeDtypeStruct
    outs = []
    for master, *_ in states[:4]:
        kind = shape(master.shape, F32)
        outs += [kind, kind, kind, kind, shape(master.shape, BF), kind]
    outs += [shape(states[4][0].shape, F32)] * 5 + [shape((1, 1), F32)]
    ins = (total, outer, final, sums) + tuple(array for group in states for array in group)
    mem, dma = pltpu.VMEM, pltpu.SemaphoreType.DMA
    return pl.pallas_call(
        functools.partial(update_kernel, rates, clip_limit, None),
        out_shape=outs,
        in_specs=anywhere(len(ins)),
        out_specs=anywhere(len(outs)),
        scratch_shapes=[mem(array.shape, array.dtype) for array in ins + tuple(outs)]
        + [dma((len(ins),)), dma((len(outs),))],
        compiler_params=pltpu.CompilerParams(vmem_limit_bytes=VMEM_BYTES),
        name="update",
    )(*ins)


def partner_swap(values, bit):
    count = lax.axis_size(AXES)
    return lax.ppermute(values, AXES, [(place, place ^ (1 << bit)) for place in range(count)])


def bit_order():
    bits = lax.axis_size(AXES).bit_length() - 1
    return list(range(1, bits)) + [0]


def scatter_sum(rows):
    order = bit_order()
    place = lax.axis_index(AXES)
    left = list(reversed(range(len(order))))
    held = rows.reshape((2,) * len(order) + rows.shape[1:])
    for bit in order:
        axis = left.index(bit)
        mine = (place >> bit) & 1
        keep = lax.dynamic_index_in_dim(held, mine, axis, keepdims=False)
        send = lax.dynamic_index_in_dim(held, 1 - mine, axis, keepdims=False)
        total = keep.astype(F32) + partner_swap(send, bit).astype(F32)
        left.remove(bit)
        held = total.astype(BF) if left else total
    return held


def butterfly_sum(values):
    for bit in bit_order():
        values = values + partner_swap(values, bit)
    return values


def sums_by_permutes(outs, width, tabs):
    grad, g2, g1, go, sums, gq = outs
    shards = lax.axis_size(AXES)
    outer = scatter_sum(g2.reshape(shards, -1)).reshape(-1, width)
    pieces = [g1.reshape(-1, shards, width // shards, width), go.reshape(1, shards, -1, width)]
    pieces = jnp.concatenate(pieces + [gq.reshape(-1, shards, width // shards, width)], axis=0)
    pieces = pieces.swapaxes(0, 1)
    final = scatter_sum(pieces.reshape(shards, -1)).reshape(pieces.shape[1:])
    sums = butterfly_sum(sums)
    total = butterfly_sum((jnp.sum(outer * outer) + jnp.sum(final * final)).reshape(1))
    total = jnp.zeros((8, 128), F32).at[0, 0].set(total[0] + jnp.sum(sums * sums))
    return grad, total, outer, final, sums


def unswap(rows, length):
    blocks = rows.reshape(-1, length, rows.shape[-1])
    return lax.all_to_all(blocks, "seq", split_axis=1, concat_axis=0, tiled=True)


def body(
    tables_in, out_cot, segment_ids, row_ids, col_ids,
    qkv_weight, out_weight, ffn_in_weight, ffn_out_weight, small_params,
    qkv_master, qkv_first, qkv_second, qkv_ema,
    out_master, out_first, out_second, out_ema,
    ffn_in_master, ffn_in_first, ffn_in_second, ffn_in_ema,
    ffn_out_master, ffn_out_first, ffn_out_second, ffn_out_ema,
    small_first, small_second, small_ema,
):
    width, hidden = ffn_in_weight.shape
    pack = lambda values: values.reshape(-1, 128)
    small = pack(small_params)
    weights = (qkv_weight, out_weight, ffn_in_weight, ffn_out_weight)
    saved = forward(tables_in, out_cot, segment_ids, row_ids, col_ids, *weights, small)
    bits = tuple(lax.axis_size(axis).bit_length() - 1 for axis in AXES)
    linked, outs = backward(saved, weights, small, bits)
    if linked:
        input_grad, layer_out, outer, final, sums, total = outs
    else:
        length = 2 * tables_in.shape[1]
        grad, total, outer, final, sums = sums_by_permutes(outs, width, tables_in.shape[0])
        input_grad, layer_out = unswap(grad, length), unswap(saved[13], length)
    states = [
        (ffn_out_master, ffn_out_first, ffn_out_second, ffn_out_ema),
        (ffn_in_master, ffn_in_first, ffn_in_second, ffn_in_ema),
        (out_master, out_first, out_second, out_ema),
        (qkv_master, qkv_first, qkv_second, qkv_ema),
        (small, pack(small_first), pack(small_second), pack(small_ema)),
    ]
    rates = (hidden**-0.5, width**-0.5, max(width // 128, 1) ** -0.5, width**-0.5, SMALL_RATE)
    entries = 4 * width * width + 2 * width * hidden + 8 * width + hidden
    new = update(total, outer, final, sums, states, rates, math.sqrt(float(entries)))
    wo_new, wi_new, o_new, qkv_new = (new[6 * i : 6 * i + 6] for i in range(4))
    sm_new = [values.reshape(-1) for values in new[24:29]]
    groups = (qkv_new, o_new, wi_new, wo_new)
    return (
        layer_out,
        input_grad,
        *[group[0] for group in groups],
        sm_new[0],
        new[29].reshape(()),
        *[values for group in groups for values in group[1:]],
        sm_new[1],
        sm_new[2],
        sm_new[3],
        sm_new[4],
    )


def solution(mesh):
    rows = P("batch", "seq", None)
    ids = P("batch", None)
    shard3 = P(None, AXES, None)
    shard2 = P(AXES, None)
    in_specs = (rows, rows, ids, ids, ids) + (P(),) * 5 + (shard3,) * 4 + (shard2,) * 12 + (P(),) * 3
    out_specs = (rows, rows, shard3, shard2, shard2, shard2, P(), P())
    out_specs += (shard3,) * 5 + (shard2,) * 15 + (P(),) * 4
    return jax.shard_map(body, mesh=mesh, in_specs=in_specs, out_specs=out_specs, check_vma=False)
```

```python
import functools
import math

import jax
import jax.numpy as jnp
from jax import lax
from jax.experimental import pallas as pl
from jax.experimental.pallas import tpu as pltpu
from jax.sharding import PartitionSpec as P

HD = 64
STEP = 10
EPS_NORM = 1e-06
NEG_BIG = -1e30
BETA_ONE = 0.9
BETA_TWO = 0.999
ADAM_EPS = 1e-08
DECAY = 0.01
EMA_KEEP = 0.8
SMALL_RATE = 0.1
AXES = ("batch", "seq")
MESH = pl.DeviceIdType.MESH
VMEM_BYTES = 61 << 20
BF = jnp.bfloat16
F32 = jnp.float32


def nn(left, right):
    return lax.dot_general(left, right, (((1,), (0,)), ((), ())), preferred_element_type=F32)


def nt(left, right):
    return lax.dot_general(left, right, (((1,), (1,)), ((), ())), preferred_element_type=F32)


def tn(left, right):
    return lax.dot_general(left, right, (((0,), (0,)), ((), ())), preferred_element_type=F32)


def row_mean(values):
    return jnp.mean(values, axis=1, keepdims=True)


def column_sum(values):
    return jnp.sum(values, axis=0, keepdims=True)


def gelu_pair(inner):
    size = jnp.abs(inner) * 0.7071067811865476
    t = 1.0 / (1.0 + 0.3275911 * size)
    bell = jnp.exp(inner * inner * -0.5)
    series = (((1.061405429 * t - 1.453152027) * t + 1.421413741) * t - 0.284496736) * t
    half = (series + 0.254829592) * t * (0.5 * bell)
    share = jnp.where(inner > 0, 1.0 - half, half)
    return inner * share, share + inner * bell * 0.3989422804014327


def small_row(packed, index, width):
    lines = width // 128
    return jnp.concatenate([packed[index * lines + i : index * lines + i + 1, :] for i in range(lines)], axis=1)


def head_masks():
    lane = lax.broadcasted_iota(jnp.int32, (1, 2 * HD), 1)
    return (lane < HD, lane >= HD)


def forward_kernel(
    tables_h, cot_h, seg_h, row_h, col_h, wqkv_h, wo_h, w1_h, w2_h, small_h,
    x_o, q_o, k_o, v_o, e_o, rinv_o, ctx_o, h1_o, xh_o, rstd_o, a_o, g_o, dr2_o, lo_o, sg_o,
    x, cot, seg, row, col, wqkv, wo, w1, w2, small, bias, inner_bias,
    q, k, v, e, rinv, ctx, h1, xh, rstd, a, g, dr2, lo, sg, h1f,
    in_sem, out_sem, e_sem, send_sem, recv_sem,
):
    tabs, length, width = x.shape
    block = length // 2
    hidden = w1.shape[1]
    pairs = width // (2 * HD)
    batch, me = lax.axis_index("batch"), lax.axis_index("seq")
    peer = (batch, 1 - me)
    copy = pltpu.make_async_copy
    barrier = pltpu.get_barrier_semaphore()
    pl.semaphore_signal(barrier, inc=1, device_id=peer, device_id_type=MESH)
    own_rows = pl.ds(pl.multiple_of(me * block, block), block)
    peer_rows = pl.ds(pl.multiple_of((1 - me) * block, block), block)

    sources = [(small_h, small), (wqkv_h, wqkv), (seg_h, seg), (row_h, row), (col_h, col)]
    sources += [(wo_h, wo), (w1_h, w1), (w2_h, w2)]
    sources += [(tables_h.at[me * tabs + t], x.at[t, own_rows]) for t in range(tabs)]
    sources += [(cot_h.at[me * tabs + t], cot.at[t, own_rows]) for t in range(tabs)]
    loads = [copy(src, dst, in_sem.at[i]) for i, (src, dst) in enumerate(sources)]
    for i in (8, 9, 1, 0, 2, 3, 4, 5, 6, 7, 10, 11):
        loads[i].start()

    def swap(index):
        source, place = (tables_h, x) if index < tabs else (cot_h, cot)
        t = index % tabs
        return pltpu.make_async_remote_copy(
            src_ref=source.at[(1 - me) * tabs + t],
            dst_ref=place.at[t, own_rows],
            send_sem=send_sem.at[index],
            recv_sem=recv_sem.at[index],
            device_id=peer,
            device_id_type=MESH,
        )

    pl.semaphore_wait(barrier, 1)
    for index in range(2 * tabs):
        swap(index).start()

    stores = []

    def store(index, src, dst):
        stores.append(copy(src, dst, out_sem.at[index]))
        stores[-1].start()

    for i in (0, 1, 8, 9):
        loads[i].wait()
    gain1, gain2, shift1, shift2, bias_q, bias_v, bias_o, bias_f2 = (
        small_row(small, i, width) for i in range(8)
    )
    inner_bias[...] = small_row(small[8 * (width // 128) :, :], 0, hidden)
    masks = head_masks()
    zero = jnp.zeros((), BF)

    def project(t, rows):
        block_x = x[t, rows, :]
        q[t, rows, :] = ((nn(block_x, wqkv[0]) + bias_q) * (HD**-0.5)).astype(BF)
        k[t, rows, :] = nn(block_x, wqkv[1]).astype(BF)
        v[t, rows, :] = (nn(block_x, wqkv[2]) + bias_v).astype(BF)

    for t in range(tabs):
        project(t, own_rows)
    for i in (2, 3, 4):
        loads[i].wait()
    for t in range(tabs):
        keys = [ids[pl.ds(me * tabs + t, 1), :].astype(F32) for ids in (seg, row, col)]
        wide = [jnp.transpose(jnp.broadcast_to(ids, (128, length)))[:, 0:1] for ids in keys]
        seen = (wide[0] == 0.0) | (keys[0] == 0.0)
        seen = seen | (wide[1] == keys[1]) | (wide[2] == keys[2])
        bias[t] = jnp.where(seen, 0.0, NEG_BIG)

    for t in range(tabs):
        swap(t).wait_recv()
        project(t, peer_rows)
        store(16 * t + 14, x.at[t], x_o.at[t])

        def pair(hp, carry):
            lanes = pl.ds(pl.multiple_of(hp * 2 * HD, 2 * HD), 2 * HD)
            slot = lax.rem(hp, 2)

            @pl.when(t * pairs + hp >= 2)
            def _():
                copy(e.at[slot], e_o.at[0, 0], e_sem.at[slot]).wait()

            q2, k2, v2 = q[t, :, lanes], k[t, :, lanes], v[t, :, lanes]
            one = jnp.ones((length, 2 * HD), BF)
            rows = 256
            for start in range(0, length, rows):
                here = slice(start, start + rows)
                for h in range(2):
                    scores = nt(jnp.where(masks[h], q2[here], zero), k2) + bias[t, here, :]
                    top = jnp.max(scores, axis=1, keepdims=True)
                    e[slot, here, h * length : (h + 1) * length] = jnp.exp(scores - top).astype(BF)
            right = [
                jnp.concatenate([jnp.where(m, v2, zero), jnp.where(m, one, zero)], axis=1)
                for m in masks
            ]
            both = nn(e[slot], jnp.concatenate(right, axis=0))
            inverse = 1.0 / both[:, 2 * HD :]
            rinv[t, :, lanes] = inverse.astype(BF)
            ctx[t, :, lanes] = (both[:, : 2 * HD] * inverse).astype(BF)
            copy(e.at[slot], e_o.at[t, hp], e_sem.at[slot]).start()
            return carry

        lax.fori_loop(0, pairs, pair, 0)
        for i, (src, dst) in enumerate(((q, q_o), (k, k_o), (v, v_o), (rinv, rinv_o), (ctx, ctx_o))):
            store(16 * t + i, src.at[t], dst.at[t])
        if t == 0:
            loads[5].wait()
        sum1 = x[t].astype(F32) + nn(ctx[t], wo[...]) + bias_o
        centre = sum1 - row_mean(sum1)
        scale = lax.rsqrt(row_mean(centre * centre) + EPS_NORM)
        unit = centre * scale
        xh[t] = unit.astype(BF)
        rstd[t] = jnp.broadcast_to(scale, (length, 128))
        normed = unit * gain1 + shift1
        h1f[...] = normed
        h1[t] = normed.astype(BF)
        for i, (src, dst) in enumerate(((h1, h1_o), (xh, xh_o), (rstd, rstd_o))):
            store(16 * t + 5 + i, src.at[t], dst.at[t])
        if t == 0:
            loads[6].wait()
        rows = pl.ds(t * length, length)
        step = 256

        def inner(j, carry):
            for sub in range(width // step):
                here = slice(sub * step, (sub + 1) * step)
                there = pl.ds(pl.multiple_of(j * width + sub * step, step), step)
                active, slope = gelu_pair(nn(h1[t], w1[:, there]) + inner_bias[0:1, there])
                a[j, rows, here] = active.astype(BF)
                g[j, rows, here] = slope.astype(BF)
            return carry

        lax.fori_loop(0, hidden // width, inner, 0)
        store(16 * t + 8, a.at[:, rows], a_o.at[:, rows])
        store(16 * t + 9, g.at[:, rows], g_o.at[:, rows])
        if t == 0:
            loads[7].wait()
        sum2 = h1f[...] + bias_f2
        for j in range(hidden // width):
            sum2 = sum2 + nn(a[j, rows, :], w2[j * width : (j + 1) * width, :])
        centre = sum2 - row_mean(sum2)
        scale = lax.rsqrt(row_mean(centre * centre) + EPS_NORM)
        unit = centre * scale
        lo[t] = (unit * gain2 + shift2).astype(BF)
        loads[10 + t].wait()
        swap(tabs + t).wait_recv()
        back = cot[t].astype(F32)
        d_unit = back * gain2
        d_sum2 = scale * (d_unit - row_mean(d_unit) - unit * row_mean(d_unit * unit))
        dr2[t] = d_sum2
        parts = [column_sum(back * unit), column_sum(back), column_sum(d_sum2.astype(BF).astype(F32))]
        parts = jnp.concatenate(parts + [jnp.zeros((5, width), F32)], axis=0)
        sg[...] = parts if t == 0 else sg[...] + parts
        store(16 * t + 10, dr2.at[t], dr2_o.at[t])
        store(16 * t + 11, lo.at[t], lo_o.at[t])
    store(12, sg, sg_o)
    for stored in stores:
        stored.wait()
    for slot in range(2):
        copy(e.at[slot], e_o.at[0, 0], e_sem.at[slot]).wait()
    for index in range(2 * tabs):
        swap(index).wait_send()


def anywhere(count):
    return [pl.BlockSpec(memory_space=pl.ANY)] * count


def forward(tables_in, out_cot, seg, row, col, wqkv, wo, w1, w2, small):
    tabs, length = tables_in.shape[0] // 2, tables_in.shape[1] * 2
    width, hidden = w1.shape
    pairs, chunks, rows = width // (2 * HD), hidden // width, tabs * length
    shape = jax.ShapeDtypeStruct
    act = shape((tabs, length, width), BF)
    wide = shape((chunks, rows, width), BF)
    outs = [act] * 4 + [shape((tabs, pairs, length, 2 * length), BF)] + [act] * 4
    outs += [shape((tabs, length, 128), F32), wide, wide, shape(act.shape, F32), act]
    outs += [shape((8, width), F32)]
    ins = (tables_in, out_cot, seg, row, col, wqkv, wo, w1, w2, small)
    like = lambda array: pltpu.VMEM(array.shape, array.dtype)
    scratch = [like(act), like(act)] + [like(array) for array in ins[2:]]
    scratch += [pltpu.VMEM((tabs, length, length), F32), pltpu.VMEM((1, hidden), F32)]
    scratch += [like(array) for array in outs[1:4]] + [pltpu.VMEM((2, length, 2 * length), BF)]
    scratch += [like(array) for array in outs[5:]] + [pltpu.VMEM((length, width), F32)]
    dma = pltpu.SemaphoreType.DMA
    return pl.pallas_call(
        forward_kernel,
        out_shape=outs,
        in_specs=anywhere(len(ins)),
        out_specs=anywhere(len(outs)),
        scratch_shapes=scratch + [dma((16,)), dma((16 * tabs,)), dma((2,)), dma((8,)), dma((8,))],
        compiler_params=pltpu.CompilerParams(
            vmem_limit_bytes=VMEM_BYTES, collective_id=0, has_side_effects=True
        ),
        name="layer_forward",
    )(*ins)


PLAN = {
    ("slope", 1): (("core2", 1),),
    ("inner", 0): (("begin", 0),),
    ("inner", 1): (("begin", 1),),
    ("inner", 2): (("begin", 2), ("advance", 0), ("core2", 0),),
    ("inner", 3): (("begin", 3), ("advance", 1),),
    ("norm", 0): (("advance", 3), ("advance", 2),),
    ("norm", 1): (("advance", 0),),
    ("attn", None): (("begin", 4),),
    ("context", None): (("advance", 1),),
    ("attend", 0): (("x2", 1),),
    ("attend", 1): (("rows", 0), ("advance", 3),),
    ("attend", 2): (("advance", 2),),
    ("attend", 3): (("begin", 5), ("x2", 0),),
    ("attend", 4): (("advance", 1), ("advance", 4),),
    ("attend", 5): (("advance", 0),),
    ("attend", 6): (("advance", 5),),
    ("attend", 7): (("begin", 6), ("advance", 1), ("advance", 2), ("y2", 1),),
    ("attend", 9): (("advance", 4), ("advance", 6), ("y2", 0),),
    ("attend", 10): (("begin", 7), ("advance", 1),),
    ("attend", 11): (("begin", 8), ("advance", 5), ("advance", 7), ("advance", 6),),
    ("attended", None): (("advance", 8), ("advance", 0), ("z2", 1),),
    ("input", 1): (("advance", 5),),
    ("leave", None): (("advance", 7), ("advance", 6), ("advance", 4), ("advance", 2), ("z2", 0), ("advance", 8), ("advance", 7), ("advance", 4), ("advance", 3), ("advance", 2), ("near", 0), ("advance", 6), ("advance", 5), ("advance", 3), ("advance", 7), ("advance", 4), ("w2", 0), ("advance", 8), ("advance", 3), ("advance", 5), ("advance", 0), ("advance", 6), ("advance", 7), ("far", 0),),
}


class Link:
    FIRST_Y = ("core", "y", "z", "w", "x")
    FIRST_Z = ("core", "z", "w", "y", "x")

    def __init__(self, rest, g2, g1, full, sm, grad, lo_h, outs):
        (self.half2, self.x2, self.y2, self.z2, self.w2, self.half, self.two, self.one, self.last) = rest[:9]
        (self.x_send, self.x_get, self.final2, self.final, self.slots8, self.slots4) = rest[9:15]
        (self.square8, self.square4, self.plane_out, self.plane_get, self.line_out, self.line_get) = rest[15:21]
        self.send_sem, self.recv_sem, self.own_sem = rest[21:]
        self.g2, self.g1, self.full, self.sm, self.grad = g2, g1, full, sm, grad
        self.lo_h, self.outs = lo_h, outs
        batch, seq = lax.axis_index("batch"), lax.axis_index("seq")
        self.batch, self.seq = batch, seq
        self.bit = {
            "core": lax.rem(batch, 2),
            "y": lax.rem(batch // 2, 2),
            "z": lax.rem(batch // 4, 2),
            "w": batch // 8,
            "x": seq,
        }
        self.jump = {"core": 1, "y": 2, "z": 4, "w": 8}
        width = g1.shape[-1]
        whole = pl.ds(0, width)
        self.chunks = [(c, whole) for c in range(7)]
        self.chunks += [(7, pl.ds(0, width // 2)), (7, pl.ds(width // 2, width // 2))]
        y, z = self.FIRST_Y, self.FIRST_Z
        self.order = [z, y, y, z, z, y, y, y, y]
        count = len(self.chunks)
        self.state = [0] * count
        self.direct = count - 1
        self.memo = None
        self.halves2 = 0
        self.held = [["w", "z", "y"] for _ in range(count)]
        self.near = [None] + [tuple(n for b, n in ((1, "x"), (2, "core"), (4, "y")) if m & b) for m in range(1, 8)]
        self.far = [None] + [tuple(n for b, n in ((1, "z"), (2, "w")) if m & b) for m in range(1, 4)]

    def device(self, names):
        batch, seq = self.batch, self.seq
        for name in names:
            if name == "x":
                seq = 1 - seq
            else:
                batch = batch + self.jump[name] * (1 - 2 * self.bit[name])
        return (batch, seq)

    def remote(self, index, src, dst, names):
        return pltpu.make_async_remote_copy(
            src_ref=src,
            dst_ref=dst,
            send_sem=self.send_sem.at[index],
            recv_sem=self.recv_sem.at[index],
            device_id=self.device(names),
            device_id_type=MESH,
        )

    def full_part(self, chunk, core):
        buffer, cols = self.chunks[chunk]
        kept = self.g1.shape[0]
        rows = pl.ds(0, self.g1.shape[-2])
        ref, index = (self.g1, buffer) if buffer < kept else (self.full, (buffer + 3) % 4)
        return ref.at[index, :, :, :, core, rows, cols]

    def stage(self, chunk, number, where=()):
        buffer, cols = self.chunks[chunk]
        ref = (self.half, self.two, self.one, self.last)[number]
        where = tuple(where) + (slice(None),) * (len(ref.shape) - 3 - len(where))
        return ref.at[(buffer,) + where + (slice(None), cols)]

    def pick(self, chunk, name, other):
        value = 1 - self.bit[name] if other else self.bit[name]
        return tuple(value if axis == name else slice(None) for axis in self.held[chunk])

    def phase(self, chunk, number):
        name = self.order[chunk][number]
        buffer, cols = self.chunks[chunk]
        index = chunk * 5 + number
        if name == "core":
            src, dst = self.full_part(chunk, 1 - self.bit["core"]), self.stage(chunk, 0)
        elif name == "x":
            src, dst = self.x_send.at[buffer, :, cols], self.x_get.at[buffer, :, cols]
        else:
            src = self.stage(chunk, number - 1, self.pick(chunk, name, True))
            dst = self.stage(chunk, number)
        return self.remote(index, src, dst, (name,))

    def flips(self, names):
        values = [self.bit[name] for name in names]
        for m in range(4):
            flip = [(m >> i) & 1 for i in range(2)]
            low, high = (1 - v if f else v for v, f in zip(values, flip))
            yield m, 2 * high + low, tuple(n for n, f in zip(names, flip) if f)

    def plane(self):
        return [
            self.remote(40 + m, self.plane_out.at[place], self.plane_get.at[m - 1], names)
            for m, place, names in self.flips(("x", "y"))
            if m
        ]

    def line(self):
        return [
            self.remote(84 + m, self.line_out.at[place], self.line_get.at[m - 1], names)
            for m, place, names in self.flips(("z", "w"))
            if m
        ]

    def advance_direct(self):
        chunk = self.direct
        buffer, cols = self.chunks[chunk]
        number = self.state[chunk]
        if number == 0:
            self.phase(chunk, 0).wait_recv()
            total = self.stage(chunk, 0)[...].astype(F32) + self.full_part(chunk, self.bit["core"])[...].astype(F32)
            share = total.shape[3] // 2
            pad = jnp.zeros(total.shape[:2] + (self.plane_out.shape[3] - share, total.shape[4]), F32)
            for y in range(2):
                for x in range(2):
                    rows = total[:, :, y, x * share : (x + 1) * share]
                    self.plane_out[2 * y + x] = jnp.concatenate([rows, pad], axis=2).astype(BF)
            self.start_all(self.plane())
            self.state[chunk] = 1
            return
        sent = self.plane() if number == 1 else self.line()
        out, get = (self.plane_out, self.plane_get) if number == 1 else (self.line_out, self.line_get)
        for each in sent:
            each.wait_recv()
        names = ("x", "y") if number == 1 else ("z", "w")
        total = out[2 * self.bit[names[1]] + self.bit[names[0]]].astype(F32)
        for m in range(3):
            total = total + get[m].astype(F32)
        if number == 1:
            self.line_out[...] = total.reshape(self.line_out.shape).astype(BF)
            self.start_all(self.line())
            self.state[chunk] = 2
        else:
            self.final.at[buffer, :, cols][...] = total[0 : self.final.shape[1]]
            self.state[chunk] = 5

    def begin(self, chunk):
        self.phase(chunk, 0).start()

    def advance(self, *chunks):
        for chunk in chunks:
            if chunk == self.direct:
                self.advance_direct()
                continue
            number = self.state[chunk]
            name = self.order[chunk][number]
            buffer, cols = self.chunks[chunk]
            self.phase(chunk, number).wait_recv()
            if name == "x":
                rows = self.final.shape[1]
                here = self.x_get.at[buffer, :, cols][...].astype(F32)[0:rows]
                ref = self.final.at[buffer, :, cols]
                ref[...] = ref[...] + here
                self.state[chunk] = 5
                continue
            if name == "core":
                kept = self.full_part(chunk, self.bit["core"])
            else:
                kept = self.stage(chunk, number - 1, self.pick(chunk, name, False))
                self.held[chunk].remove(name)
            ref = self.stage(chunk, number)
            total = ref[...].astype(F32) + kept[...].astype(F32)
            if number < 3:
                ref[...] = total.astype(BF)
            else:
                rows = total.shape[0] // 2
                low, high = total[0:rows], total[rows:]
                upper = self.seq == 1
                self.final.at[buffer, :, cols][...] = jnp.where(upper, high, low)
                pad = jnp.zeros((self.x_send.shape[1] - rows, low.shape[1]), F32)
                gone = jnp.concatenate([jnp.where(upper, low, high), pad], axis=0)
                self.x_send.at[buffer, :, cols][...] = gone.astype(BF)
            self.state[chunk] = number + 1
            self.phase(chunk, number + 1).start()

    def core2(self, j):
        src = self.g2.at[j, :, 1 - self.bit["core"]]
        return self.remote(50 + j, src, self.half2.at[j // 2, j % 2], ("core",))

    def core2_done(self, *which):
        for j in which:
            self.core2(j).wait_recv()
            kept = self.g2[j, :, self.bit["core"]].astype(F32)
            self.half2[j // 2, j % 2] = (self.half2[j // 2, j % 2].astype(F32) + kept).astype(BF)

    def side2(self, seq):
        rows = self.x2.shape[3]
        return pl.ds(pl.multiple_of(seq * rows, rows), rows)

    def copy_x2(self, w):
        src = self.half2.at[w, :, :, self.side2(1 - self.seq)]
        return self.remote(54 + w, src, self.x2.at[w], ("x",))

    def copy_y2(self, w):
        return self.remote(56 + w, self.x2.at[w, :, 1 - self.bit["y"]], self.y2.at[w], ("y",))

    def copy_z2(self, w):
        return self.remote(58 + w, self.y2.at[w, 1 - self.bit["z"]], self.z2.at[w], ("z",))

    def copy_w2(self):
        return self.remote(60, self.z2.at[1 - self.bit["w"]], self.w2, ("w",))

    def x2_done(self, w):
        self.copy_x2(w).wait_recv()
        for z in range(2):
            kept = self.half2[w, z, :, self.side2(self.seq), :].astype(F32)
            self.x2[w, z] = (self.x2[w, z].astype(F32) + kept).astype(BF)
        self.copy_y2(w).start()

    def y2_done(self, w):
        self.copy_y2(w).wait_recv()
        kept = self.x2[w, :, self.bit["y"]].astype(F32)
        self.y2[w] = (self.y2[w].astype(F32) + kept).astype(BF)
        self.copy_z2(w).start()

    def z2_done(self, w):
        self.copy_z2(w).wait_recv()
        kept = self.y2[w, self.bit["z"]].astype(F32)
        self.z2[w] = (self.z2[w].astype(F32) + kept).astype(BF)

    def w2_done(self):
        self.copy_w2().wait_recv()
        self.final2[...] = self.z2[self.bit["w"]].astype(F32) + self.w2[...].astype(F32)

    def back(self, index, src, table, tabs):
        block = self.outs[0].shape[1]
        there = pl.ds(pl.multiple_of((1 - self.seq) * block, block), block)
        dst = self.outs[1 if index == 61 else 0]
        if index == 61:
            return self.remote(61, src.at[:, there], dst.at[pl.ds(self.seq * tabs, tabs)], ("x",))
        rows = pl.ds(pl.multiple_of(table * 2 * block + (1 - self.seq) * block, block), block)
        return self.remote(index, src.at[rows], dst.at[self.seq * tabs + table], ("x",))

    def keep(self, index, src, table, tabs):
        block = self.outs[0].shape[1]
        sem = self.own_sem.at[index - 61]
        dst = self.outs[1 if index == 61 else 0]
        here = pl.ds(pl.multiple_of(self.seq * block, block), block)
        if index == 61:
            return pltpu.make_async_copy(src.at[:, here], dst.at[pl.ds(self.seq * tabs, tabs)], sem)
        rows = pl.ds(pl.multiple_of(table * 2 * block + self.seq * block, block), block)
        return pltpu.make_async_copy(src.at[rows], dst.at[self.seq * tabs + table], sem)

    def spread(self, base, slots, groups):
        return [
            self.remote(base + m, slots.at[0], slots.at[m], groups[m])
            for m in range(1, len(groups))
        ]

    def gathered(self, base, slots, groups):
        for sent in self.spread(base, slots, groups):
            sent.wait_recv()
        terms = [slots[m] for m in range(len(groups))]
        while len(terms) > 1:
            terms = [terms[i] + terms[i + 1] for i in range(0, len(terms), 2)]
        return terms[0]

    def start_all(self, copies):
        for each in copies:
            each.start()

    def act(self, kind, index):
        if kind == "begin":
            self.begin(index)
        elif kind == "advance":
            self.advance(index)
        elif kind == "core2":
            self.core2_done(2 * index, 2 * index + 1)
            self.copy_x2(index).start()
        elif kind == "x2":
            self.x2_done(index)
        elif kind == "y2":
            self.y2_done(index)
        elif kind == "z2":
            self.z2_done(index)
            self.halves2 += 1
            if self.halves2 == 2:
                self.copy_w2().start()
        elif kind == "w2":
            self.w2_done()
        elif kind == "rows":
            self.back(61, self.lo_h, 0, self.lo_h.shape[0]).start()
        elif kind == "near":
            self.slots4[0] = self.gathered(64, self.slots8, self.near)
            self.start_all(self.spread(71, self.slots4, self.far))
        elif kind == "far":
            self.sm[...] = self.gathered(71, self.slots4, self.far)

    def act_all(self, moves):
        for move in moves:
            self.act(*move)

    def at(self, name, n=None):
        tabs = self.lo_h.shape[0]
        if name == "attend":
            if self.memo is None:
                self.memo = (list(self.state), [list(held) for held in self.held], self.halves2)
            self.state, self.held = list(self.memo[0]), [list(held) for held in self.memo[1]]
            self.halves2 = self.memo[2]
            for (when, k), moves in PLAN.items():
                if when == name:
                    pl.when(n == k)(functools.partial(self.act_all, moves))
            return
        if name == "enter":
            barrier = pltpu.get_barrier_semaphore()
            for names in self.near[1:] + self.far[1:]:
                pl.semaphore_signal(barrier, inc=1, device_id=self.device(names), device_id_type=MESH)
        elif name == "outer":
            if n == 0:
                pl.semaphore_wait(pltpu.get_barrier_semaphore(), len(self.near) + len(self.far) - 2)
                self.keep(61, self.lo_h, 0, tabs).start()
            self.core2(n).start()
        elif name == "attended":
            self.slots8[0] = self.sm[...]
            self.start_all(self.spread(64, self.slots8, self.near))
        elif name == "input":
            self.back(62 + n, self.grad, n, tabs).start()
            self.keep(62 + n, self.grad, n, tabs).start()
        if name != "input" or n == tabs - 1:
            self.act_all(PLAN.get((name, n), ()))
        if name == "leave":
            self.finish(tabs)

    def finish(self, tabs):
        fold = lambda values: sum(
            (values * values)[:, i * 128 : (i + 1) * 128] for i in range(values.shape[1] // 128)
        )
        tile = lambda rows: jnp.sum(rows.reshape(rows.shape[0] // 8, 8, 128), axis=0)
        square = tile(fold(self.final2[...]))
        for buffer in range(self.final.shape[0]):
            square = square + tile(fold(self.final[buffer]))
        self.square8[0] = square
        near = self.spread(74, self.square8, self.near)
        self.start_all(near)
        ends = [(self.final2, self.outs[2]), (self.final, self.outs[3]), (self.sm, self.outs[4])]
        ends = [pltpu.make_async_copy(src, dst, self.own_sem.at[3 + i]) for i, (src, dst) in enumerate(ends)]
        self.start_all(ends)
        for chunk in range(len(self.state)):
            self.held[chunk] = ["w", "z", "y"]
            for number in range(1 if chunk == self.direct else 5):
                self.phase(chunk, number).wait_send()
                name = self.order[chunk][number]
                if name in self.held[chunk]:
                    self.held[chunk].remove(name)
        self.square4[0] = self.gathered(74, self.square8, self.near)
        far = self.spread(81, self.square4, self.far)
        self.start_all(far)
        small = tile(fold(self.sm[...]))
        sent = [self.core2(j) for j in range(4)] + [self.copy_w2()]
        sent += [copy(w) for copy in (self.copy_x2, self.copy_y2, self.copy_z2) for w in range(2)]
        sent += [self.back(61, self.lo_h, 0, tabs)]
        sent += [self.back(62 + t, self.grad, t, tabs) for t in range(tabs)]
        sent += self.plane() + self.line()
        sent += self.spread(64, self.slots8, self.near) + self.spread(71, self.slots4, self.far) + near
        for each in sent:
            each.wait_send()
        self.back(61, self.lo_h, 0, tabs).wait_recv()
        self.keep(61, self.lo_h, 0, tabs).wait()
        for t in range(tabs):
            self.back(62 + t, self.grad, t, tabs).wait_recv()
            self.keep(62 + t, self.grad, t, tabs).wait()
        self.square8[0] = self.gathered(81, self.square4, self.far) + small
        end = pltpu.make_async_copy(self.square8.at[0], self.outs[5], self.own_sem.at[6])
        end.start()
        for each in far:
            each.wait_send()
        for each in ends:
            each.wait()
        end.wait()


def backward_kernel(
    count, a_h, g_h, dr2_h, h1_h, xh_h, rstd_h, rinv_h, ctx_h, q_h, k_h, v_h, x_h, e_h, lo_h,
    wqkv_h, wo_h, w1_h, w2_h, small_h, sg_h,
    *rest,
):
    outs, rest = rest[:count], rest[count:]
    A, U, W, WO, dr, df, h1, rstd, ctx, e, small, sm, g2, g1 = rest[:14]
    in_sem, e_sem, out_sem = rest[14:17]
    chunks, rows, width = A.shape
    tabs, pairs, length, _ = e_h.shape
    share = g1.shape[-2]
    corner = (slice(None),) * (len(U.shape) - 3) + (slice(0, share),)
    copy = pltpu.make_async_copy
    link = Link(rest[17:], g2, g1, U, sm, h1, lo_h, outs) if len(rest) > 17 else None
    loads = {}
    used = [0]

    def load(name, *both):
        loads[name] = []
        for src, dst in both:
            loads[name].append(copy(src, dst, in_sem.at[used[0]]))
            used[0] += 1
            loads[name][-1].start()

    def need(*names):
        for name in names:
            for loaded in loads[name]:
                loaded.wait()

    load("dr2", (dr2_h, dr))
    load("a", *[(a_h.at[j], A.at[j]) for j in range(chunks)])
    load("small", (small_h, small), (sg_h, sm.at[pl.ds(0, 8)]))
    load("w2", (w2_h, W))
    load("g", *[(g_h.at[j], U.at[j]) for j in range(chunks)])
    load("h1", (h1_h, h1))
    load("rstd", (rstd_h, rstd))
    load("wo", (wo_h, WO))
    load("ctx", (ctx_h, ctx))
    at = link.at if link else (lambda *key: None)
    at("enter")
    half = rows // 2
    halves = [slice(i * half, (i + 1) * half) for i in range(2)]
    inside = U.shape[2:]
    take = lambda j, i: U[j, i].reshape(half, width)
    need("small", "dr2")
    first = sm[0:8, :]
    blank = jnp.zeros((1, width), F32)
    order = [blank, first[0:1], blank, first[1:2], blank, blank, blank, first[2:3]]
    sm[...] = jnp.concatenate(order + [jnp.zeros((8, width), F32)], axis=0)
    gain1 = small_row(small, 0, width)
    df[...] = dr[...].astype(BF)

    for j in range(chunks):
        loads["a"][j].wait()
        g2[j] = tn(A[j], df[...]).astype(BF).reshape(g2.shape[1:])
        at("outer", j)
    load("qkv", *[(src, A.at[i]) for i, src in enumerate((q_h, k_h, v_h))])
    load("unit", (xh_h, A.at[3]))

    need("w2")
    for j in range(chunks):
        loads["g"][j].wait()
        total = blank
        for i, half_rows in enumerate(halves):
            d_active = nt(df[half_rows, :], W[j * width : (j + 1) * width, :])
            d_inner = (d_active * take(j, i).astype(F32)).astype(BF)
            U[j, i] = d_inner.reshape(inside)
            total = total + column_sum(d_inner.astype(F32))
        sm[8 + j : 9 + j, :] = total
        at("slope", j)
    load("w1", *[(w1_h.at[:, pl.ds(j * width, width)], W.at[pl.ds(j * width, width)]) for j in range(chunks)])

    need("h1")
    for j in range(chunks):
        g1[j] = tn(h1[...], U[j].reshape(rows, width)).astype(BF).reshape(g1.shape[1:])
        at("inner", j)

    load("rinv", (rinv_h, h1))
    need("w1", "rstd", "unit")
    d_gain, d_shift, d_bias = blank, blank, blank
    for i, half_rows in enumerate(halves):
        d_normed = dr[half_rows, :]
        for j in range(chunks):
            d_normed = d_normed + nt(take(j, i), W[j * width : (j + 1) * width, :])
        unit = A[3, half_rows, :].astype(F32)
        d_shift = d_shift + column_sum(d_normed)
        d_gain = d_gain + column_sum(d_normed * unit)
        d_unit = d_normed * gain1
        d_sum1 = d_unit - row_mean(d_unit) - unit * row_mean(d_unit * unit)
        d_sum1 = rstd[half_rows, 0:1] * d_sum1
        dr[half_rows, :] = d_sum1
        d_attn = d_sum1.astype(BF)
        df[half_rows, :] = d_attn
        d_bias = d_bias + column_sum(d_attn.astype(F32))
        at("norm", i)
    load("wqkv", (wqkv_h, W.at[pl.ds(0, 3 * width)]))
    load("x", (x_h, A.at[3]))
    sm[0:1, :] = d_gain
    sm[2:3, :] = d_shift
    sm[6:7, :] = d_bias

    need("ctx", "wo")
    U[(3,) + corner] = tn(ctx[...], df[...]).astype(BF).reshape(g1.shape[1:])
    at("attn")
    need("rinv")
    for half_rows in halves:
        d_ctx = nt(df[half_rows, :], WO[...]) * h1[half_rows, :].astype(F32)
        df[half_rows, :] = d_ctx.astype(BF)
    at("context")

    need("qkv", "x", "wqkv")
    masks = head_masks()
    zero = jnp.zeros((), BF)
    steps = tabs * pairs
    split = steps - 2 * tabs

    def place(n):
        late = n // split
        table = (1 - late) * lax.rem(n, tabs) + late * ((n - split) // 2)
        return table, (1 - late) * (n // tabs) + late * (pairs - 2 + lax.rem(n, 2))

    def weight_grad(buffer, first, last, side):
        cols = slice(first * 2 * HD, last * 2 * HD)
        grads = jnp.concatenate([A[i, :, cols] for i in range(3)], axis=1)
        spot = (buffer,) + corner + (slice(side, side + grads.shape[1]),)
        total = tn(A[3], grads).astype(BF)
        U[spot] = total.reshape(g1.shape[1:-1] + (grads.shape[1],))

    due = {3: (0, 0, 2, 0), 7: (1, 2, 4, 0), 10: (2, 4, 5, 0), 11: (2, 5, 6, width // 2)}

    def input_grad(table):
        half_rows = halves[table]
        d_input = dr[half_rows, :]
        for j in range(3):
            d_input = d_input + nt(A[j, half_rows, :], W[j * width : (j + 1) * width, :])
        h1[half_rows, :] = d_input.astype(BF)
        at("input", table)

    def fetch(n, slot):
        table, hp = place(n)
        copy(e_h.at[table, hp], e.at[slot], e_sem.at[slot]).start()

    fetch(0, 0)

    def attend(n, carry):
        table, hp = place(n)
        slot = lax.rem(n, 2)

        @pl.when(n + 1 < steps)
        def _():
            fetch(n + 1, 1 - slot)

        lanes = pl.ds(pl.multiple_of(hp * 2 * HD, 2 * HD), 2 * HD)
        here = pl.ds(pl.multiple_of(table * length, length), length)
        q2, k2, v2 = (A[i, here, lanes] for i in range(3))
        d_ctx = df[here, lanes]
        less = (-(ctx[here, lanes].astype(F32) * d_ctx.astype(F32))).astype(BF)
        right = jnp.concatenate([v2, jnp.ones((length, 2 * HD), BF)], axis=1)
        copy(e_h.at[0, 0], e.at[slot], e_sem.at[slot]).wait()
        d_query = d_key = d_value = None
        for h in range(2):
            mine = lambda values: jnp.where(masks[h], values, zero)
            d_head = mine(d_ctx)
            weights = e[slot, :, h * length : (h + 1) * length]
            d_raw = nt(jnp.concatenate([d_head, mine(less)], axis=1), right)
            d_scores = (weights.astype(F32) * d_raw).astype(BF)
            add = lambda held, new: new if held is None else held + new
            d_value = add(d_value, tn(weights, d_head))
            d_key = add(d_key, tn(d_scores, mine(q2)))
            d_query = add(d_query, nn(d_scores, mine(k2)))
        d_query = (d_query * (HD**-0.5)).astype(BF)
        d_value = d_value.astype(BF)
        A[0, here, lanes] = d_query
        A[1, here, lanes] = d_key.astype(BF)
        A[2, here, lanes] = d_value
        sm[4:5, lanes] = sm[4:5, lanes] + column_sum(d_query.astype(F32))
        sm[5:6, lanes] = sm[5:6, lanes] + column_sum(d_value.astype(F32))

        for step, what in due.items():
            pl.when(n == step)(functools.partial(weight_grad, *what))
        pl.when(n == steps - 3)(functools.partial(input_grad, 0))

        at("attend", n)
        return carry

    lax.fori_loop(0, steps, attend, 0)
    at("attended")
    input_grad(1)
    if link:
        at("leave")
        return
    pieces = [(h1, outs[0]), (g2, outs[1]), (g1, outs[2]), (U.at[3, :, pl.ds(0, share)], outs[3]), (sm, outs[4])]
    pieces += [(U.at[i, :, pl.ds(0, share)], outs[5].at[i]) for i in range(3)]
    ends = [copy(src, dst, out_sem.at[i]) for i, (src, dst) in enumerate(pieces)]
    for end in ends:
        end.start()
    for end in ends:
        end.wait()


def backward(saved, weights, small, mesh_bits):
    (x, q, k, v, e, rinv, ctx, h1, xh, rstd, a, g, dr2, lo, sg) = saved
    wqkv, wo, w1, w2 = weights
    chunks, rows, width = a.shape
    hidden = w1.shape[1]
    tabs, length = x.shape[:2]
    shape = jax.ShapeDtypeStruct
    linked = mesh_bits == (4, 1) and width % 256 == 0 and chunks == 4
    lead = (2, 2, 2, 2) if linked else (2,)
    share, part = width // math.prod(lead), rows // math.prod(lead)
    flat = lambda array: array.reshape(rows, array.shape[-1])
    g2 = shape((chunks, 2, 2, width // 4, width) if linked else (chunks, width, width), BF)
    g1 = shape((chunks,) + lead + (share, width), BF)
    go = shape(lead + (share, width), BF)
    small_sum = shape((16, width), F32)
    ins = (a, g.reshape((chunks,) + lead + (part, width)))
    ins += tuple(flat(array) for array in (dr2, h1, xh, rstd, rinv, ctx, q, k, v, x))
    ins += (e, lo, wqkv.reshape(3 * width, width), wo, w1, w2, small, sg)
    mem, dma = pltpu.VMEM, pltpu.SemaphoreType.DMA
    act = mem((rows, width), BF)
    scratch = [mem(a.shape, BF), mem(ins[1].shape, BF), mem(w2.shape, BF), mem(wo.shape, BF)]
    scratch += [mem((rows, width), F32), act, act, mem((rows, 128), F32), act]
    scratch += [mem((2,) + e.shape[2:], BF), mem(small.shape, F32), mem(small_sum.shape, F32)]
    scratch += [mem(array.shape, BF) for array in (g2, g1)]
    scratch += [dma((32,)), dma((2,)), dma((8,))]
    if linked:
        blocks = shape((2 * tabs, length // 2, width), BF)
        quarter, count, half = width // 4, chunks + 4, share // 2
        outs = [blocks, blocks, shape((quarter // 2, width), F32), shape((count, half, width), F32)]
        outs += [small_sum, shape((8, 128), F32)]
        scratch += [mem((2, 2, 2, quarter, width), BF)]
        scratch += [mem((2,) * i + (quarter // 2, width), BF) for i in (3, 2, 1, 0)]
        scratch += [mem((count,) + (2,) * i + (share, width), BF) for i in (3, 2, 1, 0)]
        scratch += [mem((count, 32, width), BF)] * 2
        scratch += [mem(outs[2].shape, F32), mem(outs[3].shape, F32)]
        scratch += [mem((8,) + small_sum.shape, F32), mem((4,) + small_sum.shape, F32)]
        scratch += [mem((8, 8, 128), F32), mem((4, 8, 128), F32)]
        side = (32, width // 2)
        scratch += [mem((4, 2, 2) + side, BF), mem((3, 2, 2) + side, BF), mem((4,) + side, BF), mem((3,) + side, BF)]
        scratch += [dma((88,)), dma((88,)), dma((8,))]
        params = pltpu.CompilerParams(
            vmem_limit_bytes=VMEM_BYTES, collective_id=1, has_side_effects=True
        )
    else:
        outs = [shape((rows, width), BF), g2, g1, go, small_sum, shape((3,) + go.shape, BF)]
        params = pltpu.CompilerParams(vmem_limit_bytes=VMEM_BYTES)
    return linked, pl.pallas_call(
        functools.partial(backward_kernel, len(outs)),
        out_shape=outs,
        in_specs=anywhere(len(ins)),
        out_specs=anywhere(len(outs)),
        scratch_shapes=scratch,
        compiler_params=params,
        name="layer_backward",
    )(*ins)


def adam_update(grad_new, first, second, master, ema_old, rate):
    first_new = BETA_ONE * first + (1.0 - BETA_ONE) * grad_new
    second_new = BETA_TWO * second + (1.0 - BETA_TWO) * grad_new * grad_new
    fix_one = 1.0 - BETA_ONE**STEP
    fix_two = 1.0 - BETA_TWO**STEP
    master_new = master - rate * (
        first_new / fix_one / (jnp.sqrt(second_new / fix_two) + ADAM_EPS) + DECAY * master
    )
    ema_new = EMA_KEEP * ema_old + (1.0 - EMA_KEEP) * master_new
    return (first_new, second_new, master_new, ema_new)


def update_kernel(rates, clip_limit, names, *refs):
    total_in, outer_in, final_in, sum_in = refs[:4]
    states_in = [refs[4 + 4 * i : 8 + 4 * i] for i in range(5)]
    count_out = 6 * 4 + 5 + 1
    passed = refs[24:26]
    outs = refs[26 : 26 + count_out]
    refs = refs[26 + count_out :]
    passed = tuple(zip(passed, refs[:2], refs[-2:]))
    refs = refs[2:-2]
    total, outer, final, sums = refs[:4]
    states = [refs[4 + 4 * i : 8 + 4 * i] for i in range(5)]
    held = refs[24 : 24 + count_out]
    in_sem, out_sem, pass_sem = refs[24 + count_out :]
    copy = pltpu.make_async_copy
    loads = []

    def load(src, dst):
        loads.append(copy(src, dst, in_sem.at[len(loads)]))
        loads[-1].start()

    for src, dst in zip((total_in, outer_in, final_in, sum_in), (total, outer, final, sums)):
        load(src, dst)
    for group in range(5):
        for src, dst in zip(states_in[group], states[group]):
            load(src, dst)
    ends = []
    through = [copy(src, mid, pass_sem.at[i, 0]) for i, (src, _, mid) in enumerate(passed)]
    for each in through:
        each.start()

    def end(index):
        ends.append(copy(held[index], outs[index], out_sem.at[index]))
        ends[-1].start()

    width = outer.shape[-1]
    for i in range(4):
        loads[i].wait()
    norm = jnp.sqrt(jnp.sum(jnp.sum(total[...], axis=0, keepdims=True), axis=1, keepdims=True))
    scale = jnp.minimum(1.0, clip_limit / norm)
    held[29][...] = norm
    end(29)
    third = width // 3
    for group in range(5):
        for i in range(4):
            loads[4 + 4 * group + i].wait()
        state = states[group]
        base = 6 * group
        kinds = held[base : base + (5 if group == 4 else 6)]
        if group == 0:
            spots = [(outer[...], (slice(None),))]
        elif group == 1:
            spots = [(final[j], (slice(None), slice(j * width, (j + 1) * width))) for j in range(4)]
        elif group == 2:
            spots = [(final[4], (slice(None),))]
        elif group == 3:
            spots = [
                (final[5 + j][:, i * third : (i + 1) * third], (i, slice(None), slice(j * third, (j + 1) * third)))
                for i in range(3)
                for j in range(2)
            ]
            half = third // 2
            for i in range(3):
                for j in range(2):
                    side = (3 * j + i) * half
                    there = slice(2 * third + j * half, 2 * third + (j + 1) * half)
                    spots.append((final[7][:, side : side + half], (i, slice(None), there)))
        else:
            lines = width // 128
            packed = [
                sums[r : r + 1, i * 128 : (i + 1) * 128]
                for r in range(kinds[0].shape[0] // lines)
                for i in range(lines)
            ]
            spots = [(jnp.concatenate(packed, axis=0), (slice(None),))]
        for summed, spot in spots:
            grad = summed * scale
            first, second, master, ema = adam_update(
                grad, state[1][spot], state[2][spot], state[0][spot], state[3][spot], rates[group]
            )
            if group == 4:
                results = (grad, first, second, master, ema)
            else:
                results = (grad, first, second, master, master.astype(BF), ema)
            for kind, result in zip(kinds, results):
                kind[spot] = result
        for i in range(len(kinds)):
            end(base + i)
        if group == 1:
            for i, (_, dst, mid) in enumerate(passed):
                through[i].wait()
                ends.append(copy(mid, dst, pass_sem.at[i, 1]))
                ends[-1].start()
    for each in ends:
        each.wait()


def update(total, outer, final, sums, states, rates, clip_limit, passed):
    shape = jax.ShapeDtypeStruct
    outs = []
    for master, *_ in states[:4]:
        kind = shape(master.shape, F32)
        outs += [kind, kind, kind, kind, shape(master.shape, BF), kind]
    outs += [shape(states[4][0].shape, F32)] * 5 + [shape((1, 1), F32)]
    ins = (total, outer, final, sums) + tuple(array for group in states for array in group)
    held = ins + tuple(outs)
    ins += passed
    outs += [shape(array.shape, array.dtype) for array in passed]
    mem, dma = pltpu.VMEM, pltpu.SemaphoreType.DMA
    return pl.pallas_call(
        functools.partial(update_kernel, rates, clip_limit, None),
        out_shape=outs,
        in_specs=anywhere(len(ins)),
        out_specs=anywhere(len(outs)),
        scratch_shapes=[mem(array.shape, array.dtype) for array in held]
        + [dma((len(ins),)), dma((len(outs),)), dma((2, 2))]
        + [mem(array.shape, array.dtype) for array in passed],
        compiler_params=pltpu.CompilerParams(vmem_limit_bytes=VMEM_BYTES),
        name="update",
    )(*ins)


def partner_swap(values, bit):
    count = lax.axis_size(AXES)
    return lax.ppermute(values, AXES, [(place, place ^ (1 << bit)) for place in range(count)])


def bit_order():
    bits = lax.axis_size(AXES).bit_length() - 1
    return list(range(1, bits)) + [0]


def scatter_sum(rows):
    order = bit_order()
    place = lax.axis_index(AXES)
    left = list(reversed(range(len(order))))
    held = rows.reshape((2,) * len(order) + rows.shape[1:])
    for bit in order:
        axis = left.index(bit)
        mine = (place >> bit) & 1
        keep = lax.dynamic_index_in_dim(held, mine, axis, keepdims=False)
        send = lax.dynamic_index_in_dim(held, 1 - mine, axis, keepdims=False)
        total = keep.astype(F32) + partner_swap(send, bit).astype(F32)
        left.remove(bit)
        held = total.astype(BF) if left else total
    return held


def butterfly_sum(values):
    for bit in bit_order():
        values = values + partner_swap(values, bit)
    return values


def sums_by_permutes(outs, width, tabs):
    grad, g2, g1, go, sums, gq = outs
    shards = lax.axis_size(AXES)
    outer = scatter_sum(g2.reshape(shards, -1)).reshape(-1, width)
    pieces = [g1.reshape(-1, shards, width // shards, width), go.reshape(1, shards, -1, width)]
    pieces = jnp.concatenate(pieces + [gq.reshape(-1, shards, width // shards, width)], axis=0)
    pieces = pieces.swapaxes(0, 1)
    final = scatter_sum(pieces.reshape(shards, -1)).reshape(pieces.shape[1:])
    sums = butterfly_sum(sums)
    total = butterfly_sum((jnp.sum(outer * outer) + jnp.sum(final * final)).reshape(1))
    total = jnp.zeros((8, 128), F32).at[0, 0].set(total[0] + jnp.sum(sums * sums))
    return grad, total, outer, final, sums


def unswap(rows, length):
    blocks = rows.reshape(-1, length, rows.shape[-1])
    return lax.all_to_all(blocks, "seq", split_axis=1, concat_axis=0, tiled=True)


def body(
    tables_in, out_cot, segment_ids, row_ids, col_ids,
    qkv_weight, out_weight, ffn_in_weight, ffn_out_weight, small_params,
    qkv_master, qkv_first, qkv_second, qkv_ema,
    out_master, out_first, out_second, out_ema,
    ffn_in_master, ffn_in_first, ffn_in_second, ffn_in_ema,
    ffn_out_master, ffn_out_first, ffn_out_second, ffn_out_ema,
    small_first, small_second, small_ema,
):
    width, hidden = ffn_in_weight.shape
    pack = lambda values: values.reshape(-1, 128)
    small = pack(small_params)
    weights = (qkv_weight, out_weight, ffn_in_weight, ffn_out_weight)
    saved = forward(tables_in, out_cot, segment_ids, row_ids, col_ids, *weights, small)
    bits = tuple(lax.axis_size(axis).bit_length() - 1 for axis in AXES)
    linked, outs = backward(saved, weights, small, bits)
    if linked:
        input_grad, layer_out, outer, final, sums, total = outs
    else:
        length = 2 * tables_in.shape[1]
        grad, total, outer, final, sums = sums_by_permutes(outs, width, tables_in.shape[0])
        input_grad, layer_out = unswap(grad, length), unswap(saved[13], length)
    states = [
        (ffn_out_master, ffn_out_first, ffn_out_second, ffn_out_ema),
        (ffn_in_master, ffn_in_first, ffn_in_second, ffn_in_ema),
        (out_master, out_first, out_second, out_ema),
        (qkv_master, qkv_first, qkv_second, qkv_ema),
        (small, pack(small_first), pack(small_second), pack(small_ema)),
    ]
    rates = (hidden**-0.5, width**-0.5, max(width // 128, 1) ** -0.5, width**-0.5, SMALL_RATE)
    entries = 4 * width * width + 2 * width * hidden + 8 * width + hidden
    new = update(total, outer, final, sums, states, rates, math.sqrt(float(entries)), (layer_out, input_grad))
    wo_new, wi_new, o_new, qkv_new = (new[6 * i : 6 * i + 6] for i in range(4))
    sm_new = [values.reshape(-1) for values in new[24:29]]
    groups = (qkv_new, o_new, wi_new, wo_new)
    return (
        *new[30:32],
        *[group[0] for group in groups],
        sm_new[0],
        new[29].reshape(()),
        *[values for group in groups for values in group[1:]],
        sm_new[1],
        sm_new[2],
        sm_new[3],
        sm_new[4],
    )


def solution(mesh):
    rows = P("batch", "seq", None)
    ids = P("batch", None)
    shard3 = P(None, AXES, None)
    shard2 = P(AXES, None)
    in_specs = (rows, rows, ids, ids, ids) + (P(),) * 5 + (shard3,) * 4 + (shard2,) * 12 + (P(),) * 3
    out_specs = (rows, rows, shard3, shard2, shard2, shard2, P(), P())
    out_specs += (shard3,) * 5 + (shard2,) * 15 + (P(),) * 4
    return jax.shard_map(body, mesh=mesh, in_specs=in_specs, out_specs=out_specs, check_vma=False)
```

```python
import functools
import math

import jax
import jax.numpy as jnp
from jax import lax
from jax.experimental import pallas as pl
from jax.experimental.pallas import tpu as pltpu
from jax.sharding import PartitionSpec as P

HD = 64
STEP = 10
EPS_NORM = 1e-06
NEG_BIG = -1e30
BETA_ONE = 0.9
BETA_TWO = 0.999
ADAM_EPS = 1e-08
DECAY = 0.01
EMA_KEEP = 0.8
SMALL_RATE = 0.1
AXES = ("batch", "seq")
MESH = pl.DeviceIdType.MESH
VMEM_BYTES = 61 << 20
BF = jnp.bfloat16
F32 = jnp.float32


def nn(left, right):
    return lax.dot_general(left, right, (((1,), (0,)), ((), ())), preferred_element_type=F32)


def nt(left, right):
    return lax.dot_general(left, right, (((1,), (1,)), ((), ())), preferred_element_type=F32)


def tn(left, right):
    return lax.dot_general(left, right, (((0,), (0,)), ((), ())), preferred_element_type=F32)


def row_mean(values):
    return jnp.mean(values, axis=1, keepdims=True)


def column_sum(values):
    return jnp.sum(values, axis=0, keepdims=True)


def gelu_pair(inner):
    size = jnp.abs(inner) * 0.7071067811865476
    t = pl.reciprocal(1.0 + 0.3275911 * size)
    bell = jnp.exp(inner * inner * -0.5)
    series = (((1.061405429 * t - 1.453152027) * t + 1.421413741) * t - 0.284496736) * t
    half = (series + 0.254829592) * t * (0.5 * bell)
    share = jnp.where(inner > 0, 1.0 - half, half)
    return inner * share, share + inner * bell * 0.3989422804014327


def small_row(packed, index, width):
    lines = width // 128
    return jnp.concatenate([packed[index * lines + i : index * lines + i + 1, :] for i in range(lines)], axis=1)


def head_masks():
    lane = lax.broadcasted_iota(jnp.int32, (1, 2 * HD), 1)
    return (lane < HD, lane >= HD)


def forward_kernel(
    tables_h, cot_h, seg_h, row_h, col_h, wqkv_h, wo_h, w1_h, w2_h, small_h,
    x_o, q_o, k_o, v_o, e_o, rinv_o, ctx_o, h1_o, xh_o, rstd_o, a_o, g_o, dr2_o, lo_o, sg_o,
    x, cot, seg, row, col, wqkv, wo, w1, w2, small, bias, inner_bias,
    q, k, v, e, rinv, ctx, h1, xh, rstd, a, g, dr2, lo, sg, h1f,
    in_sem, out_sem, e_sem, send_sem, recv_sem,
):
    tabs, length, width = x.shape
    block = length // 2
    hidden = w1.shape[1]
    pairs = width // (2 * HD)
    batch, me = lax.axis_index("batch"), lax.axis_index("seq")
    peer = (batch, 1 - me)
    copy = pltpu.make_async_copy
    barrier = pltpu.get_barrier_semaphore()
    pl.semaphore_signal(barrier, inc=1, device_id=peer, device_id_type=MESH)
    own_rows = pl.ds(pl.multiple_of(me * block, block), block)
    peer_rows = pl.ds(pl.multiple_of((1 - me) * block, block), block)

    sources = [(small_h, small), (wqkv_h, wqkv), (seg_h, seg), (row_h, row), (col_h, col)]
    sources += [(wo_h, wo), (w1_h, w1), (w2_h, w2)]
    sources += [(tables_h.at[me * tabs + t], x.at[t, own_rows]) for t in range(tabs)]
    sources += [(cot_h.at[me * tabs + t], cot.at[t, own_rows]) for t in range(tabs)]
    loads = [copy(src, dst, in_sem.at[i]) for i, (src, dst) in enumerate(sources)]
    for i in (8, 9, 1, 0, 2, 3, 4, 5, 6, 7, 10, 11):
        loads[i].start()

    def swap(index):
        source, place = (tables_h, x) if index < tabs else (cot_h, cot)
        t = index % tabs
        return pltpu.make_async_remote_copy(
            src_ref=source.at[(1 - me) * tabs + t],
            dst_ref=place.at[t, own_rows],
            send_sem=send_sem.at[index],
            recv_sem=recv_sem.at[index],
            device_id=peer,
            device_id_type=MESH,
        )

    pl.semaphore_wait(barrier, 1)
    for index in range(2 * tabs):
        swap(index).start()

    stores = []

    def store(index, src, dst):
        stores.append(copy(src, dst, out_sem.at[index]))
        stores[-1].start()

    for i in (0, 1, 8, 9):
        loads[i].wait()
    gain1, gain2, shift1, shift2, bias_q, bias_v, bias_o, bias_f2 = (
        small_row(small, i, width) for i in range(8)
    )
    inner_bias[...] = small_row(small[8 * (width // 128) :, :], 0, hidden)
    masks = head_masks()
    zero = jnp.zeros((), BF)

    def project(t, rows):
        block_x = x[t, rows, :]
        q[t, rows, :] = ((nn(block_x, wqkv[0]) + bias_q) * (HD**-0.5)).astype(BF)
        k[t, rows, :] = nn(block_x, wqkv[1]).astype(BF)
        v[t, rows, :] = (nn(block_x, wqkv[2]) + bias_v).astype(BF)

    for t in range(tabs):
        project(t, own_rows)
    for i in (2, 3, 4):
        loads[i].wait()
    for t in range(tabs):
        keys = [ids[pl.ds(me * tabs + t, 1), :].astype(F32) for ids in (seg, row, col)]
        wide = [jnp.transpose(jnp.broadcast_to(ids, (128, length)))[:, 0:1] for ids in keys]
        seen = (wide[0] == 0.0) | (keys[0] == 0.0)
        seen = seen | (wide[1] == keys[1]) | (wide[2] == keys[2])
        bias[t] = jnp.where(seen, 0.0, NEG_BIG)

    for t in range(tabs):
        swap(t).wait_recv()
        project(t, peer_rows)
        store(16 * t + 14, x.at[t], x_o.at[t])

        def pair(hp, carry):
            lanes = pl.ds(pl.multiple_of(hp * 2 * HD, 2 * HD), 2 * HD)
            slot = lax.rem(hp, 2)

            @pl.when(t * pairs + hp >= 2)
            def _():
                copy(e.at[slot], e_o.at[0, 0], e_sem.at[slot]).wait()

            q2, k2, v2 = q[t, :, lanes], k[t, :, lanes], v[t, :, lanes]
            one = jnp.ones((length, 2 * HD), BF)
            rows = 256
            for start in range(0, length, rows):
                here = slice(start, start + rows)
                for h in range(2):
                    scores = nt(jnp.where(masks[h], q2[here], zero), k2) + bias[t, here, :]
                    top = jnp.max(scores, axis=1, keepdims=True)
                    e[slot, here, h * length : (h + 1) * length] = jnp.exp(scores - top).astype(BF)
            right = [
                jnp.concatenate([jnp.where(m, v2, zero), jnp.where(m, one, zero)], axis=1)
                for m in masks
            ]
            both = nn(e[slot], jnp.concatenate(right, axis=0))
            inverse = pl.reciprocal(both[:, 2 * HD :])
            rinv[t, :, lanes] = inverse.astype(BF)
            ctx[t, :, lanes] = (both[:, : 2 * HD] * inverse).astype(BF)
            copy(e.at[slot], e_o.at[t, hp], e_sem.at[slot]).start()
            return carry

        lax.fori_loop(0, pairs, pair, 0)
        for i, (src, dst) in enumerate(((q, q_o), (k, k_o), (v, v_o), (rinv, rinv_o), (ctx, ctx_o))):
            store(16 * t + i, src.at[t], dst.at[t])
        if t == 0:
            loads[5].wait()
        sum1 = x[t].astype(F32) + nn(ctx[t], wo[...]) + bias_o
        centre = sum1 - row_mean(sum1)
        scale = lax.rsqrt(row_mean(centre * centre) + EPS_NORM)
        unit = centre * scale
        xh[t] = unit.astype(BF)
        rstd[t] = jnp.broadcast_to(scale, (length, 128))
        normed = unit * gain1 + shift1
        h1f[...] = normed
        h1[t] = normed.astype(BF)
        for i, (src, dst) in enumerate(((h1, h1_o), (xh, xh_o), (rstd, rstd_o))):
            store(16 * t + 5 + i, src.at[t], dst.at[t])
        if t == 0:
            loads[6].wait()
        rows = pl.ds(t * length, length)
        step = 768

        def inner(j, carry):
            for sub in range(width // step):
                here = slice(sub * step, (sub + 1) * step)
                there = pl.ds(pl.multiple_of(j * width + sub * step, step), step)
                active, slope = gelu_pair(nn(h1[t], w1[:, there]) + inner_bias[0:1, there])
                a[j, rows, here] = active.astype(BF)
                g[j, rows, here] = slope.astype(BF)
            return carry

        lax.fori_loop(0, hidden // width, inner, 0)
        store(16 * t + 8, a.at[:, rows], a_o.at[:, rows])
        store(16 * t + 9, g.at[:, rows], g_o.at[:, rows])
        if t == 0:
            loads[7].wait()
        sum2 = h1f[...] + bias_f2
        for j in range(hidden // width):
            sum2 = sum2 + nn(a[j, rows, :], w2[j * width : (j + 1) * width, :])
        centre = sum2 - row_mean(sum2)
        scale = lax.rsqrt(row_mean(centre * centre) + EPS_NORM)
        unit = centre * scale
        lo[t] = (unit * gain2 + shift2).astype(BF)
        loads[10 + t].wait()
        swap(tabs + t).wait_recv()
        back = cot[t].astype(F32)
        d_unit = back * gain2
        d_sum2 = scale * (d_unit - row_mean(d_unit) - unit * row_mean(d_unit * unit))
        dr2[t] = d_sum2
        parts = [column_sum(back * unit), column_sum(back), column_sum(d_sum2.astype(BF).astype(F32))]
        parts = jnp.concatenate(parts + [jnp.zeros((5, width), F32)], axis=0)
        sg[...] = parts if t == 0 else sg[...] + parts
        store(16 * t + 10, dr2.at[t], dr2_o.at[t])
        store(16 * t + 11, lo.at[t], lo_o.at[t])
    store(12, sg, sg_o)
    for stored in stores:
        stored.wait()
    for slot in range(2):
        copy(e.at[slot], e_o.at[0, 0], e_sem.at[slot]).wait()
    for index in range(2 * tabs):
        swap(index).wait_send()


def anywhere(count):
    return [pl.BlockSpec(memory_space=pl.ANY)] * count


def forward(tables_in, out_cot, seg, row, col, wqkv, wo, w1, w2, small):
    tabs, length = tables_in.shape[0] // 2, tables_in.shape[1] * 2
    width, hidden = w1.shape
    pairs, chunks, rows = width // (2 * HD), hidden // width, tabs * length
    shape = jax.ShapeDtypeStruct
    act = shape((tabs, length, width), BF)
    wide = shape((chunks, rows, width), BF)
    outs = [act] * 4 + [shape((tabs, pairs, length, 2 * length), BF)] + [act] * 4
    outs += [shape((tabs, length, 128), F32), wide, wide, shape(act.shape, F32), act]
    outs += [shape((8, width), F32)]
    ins = (tables_in, out_cot, seg, row, col, wqkv, wo, w1, w2, small)
    like = lambda array: pltpu.VMEM(array.shape, array.dtype)
    scratch = [like(act), like(act)] + [like(array) for array in ins[2:]]
    scratch += [pltpu.VMEM((tabs, length, length), F32), pltpu.VMEM((1, hidden), F32)]
    scratch += [like(array) for array in outs[1:4]] + [pltpu.VMEM((2, length, 2 * length), BF)]
    scratch += [like(array) for array in outs[5:]] + [pltpu.VMEM((length, width), F32)]
    dma = pltpu.SemaphoreType.DMA
    return pl.pallas_call(
        forward_kernel,
        out_shape=outs,
        in_specs=anywhere(len(ins)),
        out_specs=anywhere(len(outs)),
        scratch_shapes=scratch + [dma((16,)), dma((16 * tabs,)), dma((2,)), dma((8,)), dma((8,))],
        compiler_params=pltpu.CompilerParams(
            vmem_limit_bytes=VMEM_BYTES, collective_id=0, has_side_effects=True
        ),
        name="layer_forward",
    )(*ins)


PLAN = {
    ("slope", 1): (("core2", 1),),
    ("inner", 0): (("begin", 0),),
    ("inner", 1): (("begin", 1),),
    ("inner", 2): (("begin", 2), ("advance", 0), ("core2", 0),),
    ("inner", 3): (("begin", 3), ("advance", 1),),
    ("norm", 0): (("advance", 3), ("advance", 2),),
    ("norm", 1): (("advance", 0),),
    ("attn", None): (("begin", 4),),
    ("context", None): (("advance", 1),),
    ("attend", 0): (("x2", 1),),
    ("attend", 1): (("rows", 0), ("advance", 3),),
    ("attend", 2): (("advance", 2),),
    ("attend", 3): (("begin", 5), ("x2", 0),),
    ("attend", 4): (("advance", 1), ("advance", 4),),
    ("attend", 5): (("advance", 0),),
    ("attend", 6): (("advance", 5),),
    ("attend", 7): (("begin", 6), ("advance", 1), ("advance", 2), ("y2", 1),),
    ("attend", 9): (("advance", 4), ("advance", 6), ("y2", 0),),
    ("attend", 10): (("begin", 7), ("advance", 1),),
    ("attend", 11): (("begin", 8), ("advance", 5), ("advance", 7), ("advance", 6),),
    ("attended", None): (("advance", 8), ("advance", 0), ("z2", 1),),
    ("input", 1): (("advance", 5),),
    ("leave", None): (("advance", 7), ("advance", 6), ("advance", 4), ("advance", 2), ("z2", 0), ("advance", 8), ("advance", 7), ("advance", 4), ("advance", 3), ("advance", 2), ("near", 0), ("advance", 6), ("advance", 5), ("advance", 3), ("advance", 7), ("advance", 4), ("w2", 0), ("advance", 8), ("advance", 3), ("advance", 5), ("advance", 0), ("advance", 6), ("advance", 7), ("far", 0),),
}


class Link:
    FIRST_Y = ("core", "y", "z", "w", "x")
    FIRST_Z = ("core", "z", "w", "y", "x")

    def __init__(self, rest, g2, g1, full, sm, grad, lo_h, outs):
        (self.half2, self.x2, self.y2, self.z2, self.w2, self.half, self.two, self.one, self.last) = rest[:9]
        (self.x_send, self.x_get, self.final2, self.final, self.slots8, self.slots4) = rest[9:15]
        (self.square8, self.square4, self.plane_out, self.plane_get, self.line_out, self.line_get) = rest[15:21]
        self.send_sem, self.recv_sem, self.own_sem = rest[21:]
        self.g2, self.g1, self.full, self.sm, self.grad = g2, g1, full, sm, grad
        self.lo_h, self.outs = lo_h, outs
        batch, seq = lax.axis_index("batch"), lax.axis_index("seq")
        self.batch, self.seq = batch, seq
        self.bit = {
            "core": lax.rem(batch, 2),
            "y": lax.rem(batch // 2, 2),
            "z": lax.rem(batch // 4, 2),
            "w": batch // 8,
            "x": seq,
        }
        self.jump = {"core": 1, "y": 2, "z": 4, "w": 8}
        width = g1.shape[-1]
        whole = pl.ds(0, width)
        self.chunks = [(c, whole) for c in range(7)]
        self.chunks += [(7, pl.ds(0, width // 2)), (7, pl.ds(width // 2, width // 2))]
        y, z = self.FIRST_Y, self.FIRST_Z
        self.order = [z, y, y, z, z, y, y, y, y]
        count = len(self.chunks)
        self.state = [0] * count
        self.direct = count - 1
        self.memo = None
        self.halves2 = 0
        self.held = [["w", "z", "y"] for _ in range(count)]
        self.near = [None] + [tuple(n for b, n in ((1, "x"), (2, "core"), (4, "y")) if m & b) for m in range(1, 8)]
        self.far = [None] + [tuple(n for b, n in ((1, "z"), (2, "w")) if m & b) for m in range(1, 4)]

    def device(self, names):
        batch, seq = self.batch, self.seq
        for name in names:
            if name == "x":
                seq = 1 - seq
            else:
                batch = batch + self.jump[name] * (1 - 2 * self.bit[name])
        return (batch, seq)

    def remote(self, index, src, dst, names):
        return pltpu.make_async_remote_copy(
            src_ref=src,
            dst_ref=dst,
            send_sem=self.send_sem.at[index],
            recv_sem=self.recv_sem.at[index],
            device_id=self.device(names),
            device_id_type=MESH,
        )

    def full_part(self, chunk, core):
        buffer, cols = self.chunks[chunk]
        kept = self.g1.shape[0]
        rows = pl.ds(0, self.g1.shape[-2])
        ref, index = (self.g1, buffer) if buffer < kept else (self.full, (buffer + 3) % 4)
        return ref.at[index, :, :, :, core, rows, cols]

    def stage(self, chunk, number, where=()):
        buffer, cols = self.chunks[chunk]
        ref = (self.half, self.two, self.one, self.last)[number]
        where = tuple(where) + (slice(None),) * (len(ref.shape) - 3 - len(where))
        return ref.at[(buffer,) + where + (slice(None), cols)]

    def pick(self, chunk, name, other):
        value = 1 - self.bit[name] if other else self.bit[name]
        return tuple(value if axis == name else slice(None) for axis in self.held[chunk])

    def phase(self, chunk, number):
        name = self.order[chunk][number]
        buffer, cols = self.chunks[chunk]
        index = chunk * 5 + number
        if name == "core":
            src, dst = self.full_part(chunk, 1 - self.bit["core"]), self.stage(chunk, 0)
        elif name == "x":
            src, dst = self.x_send.at[buffer, :, cols], self.x_get.at[buffer, :, cols]
        else:
            src = self.stage(chunk, number - 1, self.pick(chunk, name, True))
            dst = self.stage(chunk, number)
        return self.remote(index, src, dst, (name,))

    def flips(self, names):
        values = [self.bit[name] for name in names]
        for m in range(4):
            flip = [(m >> i) & 1 for i in range(2)]
            low, high = (1 - v if f else v for v, f in zip(values, flip))
            yield m, 2 * high + low, tuple(n for n, f in zip(names, flip) if f)

    def plane(self):
        return [
            self.remote(40 + m, self.plane_out.at[place], self.plane_get.at[m - 1], names)
            for m, place, names in self.flips(("x", "y"))
            if m
        ]

    def line(self):
        return [
            self.remote(84 + m, self.line_out.at[place], self.line_get.at[m - 1], names)
            for m, place, names in self.flips(("z", "w"))
            if m
        ]

    def advance_direct(self):
        chunk = self.direct
        buffer, cols = self.chunks[chunk]
        number = self.state[chunk]
        if number == 0:
            self.phase(chunk, 0).wait_recv()
            total = self.stage(chunk, 0)[...].astype(F32) + self.full_part(chunk, self.bit["core"])[...].astype(F32)
            share = total.shape[3] // 2
            pad = jnp.zeros(total.shape[:2] + (self.plane_out.shape[3] - share, total.shape[4]), F32)
            for y in range(2):
                for x in range(2):
                    rows = total[:, :, y, x * share : (x + 1) * share]
                    self.plane_out[2 * y + x] = jnp.concatenate([rows, pad], axis=2).astype(BF)
            self.start_all(self.plane())
            self.state[chunk] = 1
            return
        sent = self.plane() if number == 1 else self.line()
        out, get = (self.plane_out, self.plane_get) if number == 1 else (self.line_out, self.line_get)
        for each in sent:
            each.wait_recv()
        names = ("x", "y") if number == 1 else ("z", "w")
        total = out[2 * self.bit[names[1]] + self.bit[names[0]]].astype(F32)
        for m in range(3):
            total = total + get[m].astype(F32)
        if number == 1:
            self.line_out[...] = total.reshape(self.line_out.shape).astype(BF)
            self.start_all(self.line())
            self.state[chunk] = 2
        else:
            self.final.at[buffer, :, cols][...] = total[0 : self.final.shape[1]]
            self.state[chunk] = 5

    def begin(self, chunk):
        self.phase(chunk, 0).start()

    def advance(self, *chunks):
        for chunk in chunks:
            if chunk == self.direct:
                self.advance_direct()
                continue
            number = self.state[chunk]
            name = self.order[chunk][number]
            buffer, cols = self.chunks[chunk]
            self.phase(chunk, number).wait_recv()
            if name == "x":
                rows = self.final.shape[1]
                here = self.x_get.at[buffer, :, cols][...].astype(F32)[0:rows]
                ref = self.final.at[buffer, :, cols]
                ref[...] = ref[...] + here
                self.state[chunk] = 5
                continue
            if name == "core":
                kept = self.full_part(chunk, self.bit["core"])
            else:
                kept = self.stage(chunk, number - 1, self.pick(chunk, name, False))
                self.held[chunk].remove(name)
            ref = self.stage(chunk, number)
            total = ref[...].astype(F32) + kept[...].astype(F32)
            if number < 3:
                ref[...] = total.astype(BF)
            else:
                rows = total.shape[0] // 2
                low, high = total[0:rows], total[rows:]
                upper = self.seq == 1
                self.final.at[buffer, :, cols][...] = jnp.where(upper, high, low)
                pad = jnp.zeros((self.x_send.shape[1] - rows, low.shape[1]), F32)
                gone = jnp.concatenate([jnp.where(upper, low, high), pad], axis=0)
                self.x_send.at[buffer, :, cols][...] = gone.astype(BF)
            self.state[chunk] = number + 1
            self.phase(chunk, number + 1).start()

    def core2(self, j):
        src = self.g2.at[j, :, 1 - self.bit["core"]]
        return self.remote(50 + j, src, self.half2.at[j // 2, j % 2], ("core",))

    def core2_done(self, *which):
        for j in which:
            self.core2(j).wait_recv()
            kept = self.g2[j, :, self.bit["core"]].astype(F32)
            self.half2[j // 2, j % 2] = (self.half2[j // 2, j % 2].astype(F32) + kept).astype(BF)

    def side2(self, seq):
        rows = self.x2.shape[3]
        return pl.ds(pl.multiple_of(seq * rows, rows), rows)

    def copy_x2(self, w):
        src = self.half2.at[w, :, :, self.side2(1 - self.seq)]
        return self.remote(54 + w, src, self.x2.at[w], ("x",))

    def copy_y2(self, w):
        return self.remote(56 + w, self.x2.at[w, :, 1 - self.bit["y"]], self.y2.at[w], ("y",))

    def copy_z2(self, w):
        return self.remote(58 + w, self.y2.at[w, 1 - self.bit["z"]], self.z2.at[w], ("z",))

    def copy_w2(self):
        return self.remote(60, self.z2.at[1 - self.bit["w"]], self.w2, ("w",))

    def x2_done(self, w):
        self.copy_x2(w).wait_recv()
        for z in range(2):
            kept = self.half2[w, z, :, self.side2(self.seq), :].astype(F32)
            self.x2[w, z] = (self.x2[w, z].astype(F32) + kept).astype(BF)
        self.copy_y2(w).start()

    def y2_done(self, w):
        self.copy_y2(w).wait_recv()
        kept = self.x2[w, :, self.bit["y"]].astype(F32)
        self.y2[w] = (self.y2[w].astype(F32) + kept).astype(BF)
        self.copy_z2(w).start()

    def z2_done(self, w):
        self.copy_z2(w).wait_recv()
        kept = self.y2[w, self.bit["z"]].astype(F32)
        self.z2[w] = (self.z2[w].astype(F32) + kept).astype(BF)

    def w2_done(self):
        self.copy_w2().wait_recv()
        self.final2[...] = self.z2[self.bit["w"]].astype(F32) + self.w2[...].astype(F32)

    def back(self, index, src, table, tabs):
        block = self.outs[0].shape[1]
        there = pl.ds(pl.multiple_of((1 - self.seq) * block, block), block)
        dst = self.outs[1 if index == 61 else 0]
        if index == 61:
            return self.remote(61, src.at[:, there], dst.at[pl.ds(self.seq * tabs, tabs)], ("x",))
        rows = pl.ds(pl.multiple_of(table * 2 * block + (1 - self.seq) * block, block), block)
        return self.remote(index, src.at[rows], dst.at[self.seq * tabs + table], ("x",))

    def keep(self, index, src, table, tabs):
        block = self.outs[0].shape[1]
        sem = self.own_sem.at[index - 61]
        dst = self.outs[1 if index == 61 else 0]
        here = pl.ds(pl.multiple_of(self.seq * block, block), block)
        if index == 61:
            return pltpu.make_async_copy(src.at[:, here], dst.at[pl.ds(self.seq * tabs, tabs)], sem)
        rows = pl.ds(pl.multiple_of(table * 2 * block + self.seq * block, block), block)
        return pltpu.make_async_copy(src.at[rows], dst.at[self.seq * tabs + table], sem)

    def spread(self, base, slots, groups):
        return [
            self.remote(base + m, slots.at[0], slots.at[m], groups[m])
            for m in range(1, len(groups))
        ]

    def gathered(self, base, slots, groups):
        for sent in self.spread(base, slots, groups):
            sent.wait_recv()
        terms = [slots[m] for m in range(len(groups))]
        while len(terms) > 1:
            terms = [terms[i] + terms[i + 1] for i in range(0, len(terms), 2)]
        return terms[0]

    def start_all(self, copies):
        for each in copies:
            each.start()

    def act(self, kind, index):
        if kind == "begin":
            self.begin(index)
        elif kind == "advance":
            self.advance(index)
        elif kind == "core2":
            self.core2_done(2 * index, 2 * index + 1)
            self.copy_x2(index).start()
        elif kind == "x2":
            self.x2_done(index)
        elif kind == "y2":
            self.y2_done(index)
        elif kind == "z2":
            self.z2_done(index)
            self.halves2 += 1
            if self.halves2 == 2:
                self.copy_w2().start()
        elif kind == "w2":
            self.w2_done()
        elif kind == "rows":
            self.back(61, self.lo_h, 0, self.lo_h.shape[0]).start()
        elif kind == "near":
            self.slots4[0] = self.gathered(64, self.slots8, self.near)
            self.start_all(self.spread(71, self.slots4, self.far))
        elif kind == "far":
            self.sm[...] = self.gathered(71, self.slots4, self.far)

    def act_all(self, moves):
        for move in moves:
            self.act(*move)

    def at(self, name, n=None):
        tabs = self.lo_h.shape[0]
        if name == "attend":
            if self.memo is None:
                self.memo = (list(self.state), [list(held) for held in self.held], self.halves2)
            self.state, self.held = list(self.memo[0]), [list(held) for held in self.memo[1]]
            self.halves2 = self.memo[2]
            for (when, k), moves in PLAN.items():
                if when == name:
                    pl.when(n == k)(functools.partial(self.act_all, moves))
            return
        if name == "enter":
            barrier = pltpu.get_barrier_semaphore()
            for names in self.near[1:] + self.far[1:]:
                pl.semaphore_signal(barrier, inc=1, device_id=self.device(names), device_id_type=MESH)
        elif name == "outer":
            if n == 0:
                pl.semaphore_wait(pltpu.get_barrier_semaphore(), len(self.near) + len(self.far) - 2)
                self.keep(61, self.lo_h, 0, tabs).start()
            self.core2(n).start()
        elif name == "attended":
            self.slots8[0] = self.sm[...]
            self.start_all(self.spread(64, self.slots8, self.near))
        elif name == "input":
            self.back(62 + n, self.grad, n, tabs).start()
            self.keep(62 + n, self.grad, n, tabs).start()
        if name != "input" or n == tabs - 1:
            self.act_all(PLAN.get((name, n), ()))
        if name == "leave":
            self.finish(tabs)

    def finish(self, tabs):
        fold = lambda values: sum(
            (values * values)[:, i * 128 : (i + 1) * 128] for i in range(values.shape[1] // 128)
        )
        tile = lambda rows: jnp.sum(rows.reshape(rows.shape[0] // 8, 8, 128), axis=0)
        square = tile(fold(self.final2[...]))
        for buffer in range(self.final.shape[0]):
            square = square + tile(fold(self.final[buffer]))
        self.square8[0] = square
        near = self.spread(74, self.square8, self.near)
        self.start_all(near)
        ends = [(self.final2, self.outs[2]), (self.final, self.outs[3]), (self.sm, self.outs[4])]
        ends = [pltpu.make_async_copy(src, dst, self.own_sem.at[3 + i]) for i, (src, dst) in enumerate(ends)]
        self.start_all(ends)
        for chunk in range(len(self.state)):
            self.held[chunk] = ["w", "z", "y"]
            for number in range(1 if chunk == self.direct else 5):
                self.phase(chunk, number).wait_send()
                name = self.order[chunk][number]
                if name in self.held[chunk]:
                    self.held[chunk].remove(name)
        self.square4[0] = self.gathered(74, self.square8, self.near)
        far = self.spread(81, self.square4, self.far)
        self.start_all(far)
        small = tile(fold(self.sm[...]))
        sent = [self.core2(j) for j in range(4)] + [self.copy_w2()]
        sent += [copy(w) for copy in (self.copy_x2, self.copy_y2, self.copy_z2) for w in range(2)]
        sent += [self.back(61, self.lo_h, 0, tabs)]
        sent += [self.back(62 + t, self.grad, t, tabs) for t in range(tabs)]
        sent += self.plane() + self.line()
        sent += self.spread(64, self.slots8, self.near) + self.spread(71, self.slots4, self.far) + near
        for each in sent:
            each.wait_send()
        self.back(61, self.lo_h, 0, tabs).wait_recv()
        self.keep(61, self.lo_h, 0, tabs).wait()
        for t in range(tabs):
            self.back(62 + t, self.grad, t, tabs).wait_recv()
            self.keep(62 + t, self.grad, t, tabs).wait()
        self.square8[0] = self.gathered(81, self.square4, self.far) + small
        end = pltpu.make_async_copy(self.square8.at[0], self.outs[5], self.own_sem.at[6])
        end.start()
        for each in far:
            each.wait_send()
        for each in ends:
            each.wait()
        end.wait()


def backward_kernel(
    count, a_h, g_h, dr2_h, h1_h, xh_h, rstd_h, rinv_h, ctx_h, q_h, k_h, v_h, x_h, e_h, lo_h,
    wqkv_h, wo_h, w1_h, w2_h, small_h, sg_h,
    *rest,
):
    outs, rest = rest[:count], rest[count:]
    A, U, W, WO, dr, df, h1, rstd, ctx, e, small, sm, g2, g1 = rest[:14]
    in_sem, e_sem, out_sem = rest[14:17]
    chunks, rows, width = A.shape
    tabs, pairs, length, _ = e_h.shape
    share = g1.shape[-2]
    corner = (slice(None),) * (len(U.shape) - 3) + (slice(0, share),)
    copy = pltpu.make_async_copy
    link = Link(rest[17:], g2, g1, U, sm, h1, lo_h, outs) if len(rest) > 17 else None
    loads = {}
    used = [0]

    def load(name, *both):
        loads[name] = []
        for src, dst in both:
            loads[name].append(copy(src, dst, in_sem.at[used[0]]))
            used[0] += 1
            loads[name][-1].start()

    def need(*names):
        for name in names:
            for loaded in loads[name]:
                loaded.wait()

    load("dr2", (dr2_h, dr))
    load("a", *[(a_h.at[j], A.at[j]) for j in range(chunks)])
    load("small", (small_h, small), (sg_h, sm.at[pl.ds(0, 8)]))
    load("w2", (w2_h, W))
    load("g", *[(g_h.at[j], U.at[j]) for j in range(chunks)])
    load("h1", (h1_h, h1))
    load("rstd", (rstd_h, rstd))
    load("wo", (wo_h, WO))
    load("ctx", (ctx_h, ctx))
    at = link.at if link else (lambda *key: None)
    at("enter")
    half = rows // 2
    halves = [slice(i * half, (i + 1) * half) for i in range(2)]
    inside = U.shape[2:]
    take = lambda j, i: U[j, i].reshape(half, width)
    need("small", "dr2")
    first = sm[0:8, :]
    blank = jnp.zeros((1, width), F32)
    order = [blank, first[0:1], blank, first[1:2], blank, blank, blank, first[2:3]]
    sm[...] = jnp.concatenate(order + [jnp.zeros((8, width), F32)], axis=0)
    gain1 = small_row(small, 0, width)
    df[...] = dr[...].astype(BF)

    for j in range(chunks):
        loads["a"][j].wait()
        g2[j] = tn(A[j], df[...]).astype(BF).reshape(g2.shape[1:])
        at("outer", j)
    load("qkv", *[(src, A.at[i]) for i, src in enumerate((q_h, k_h, v_h))])
    load("unit", (xh_h, A.at[3]))

    need("w2")
    for j in range(chunks):
        loads["g"][j].wait()
        total = blank
        for i, half_rows in enumerate(halves):
            d_active = nt(df[half_rows, :], W[j * width : (j + 1) * width, :])
            d_inner = (d_active * take(j, i).astype(F32)).astype(BF)
            U[j, i] = d_inner.reshape(inside)
            total = total + column_sum(d_inner.astype(F32))
        sm[8 + j : 9 + j, :] = total
        at("slope", j)
    load("w1", *[(w1_h.at[:, pl.ds(j * width, width)], W.at[pl.ds(j * width, width)]) for j in range(chunks)])

    need("h1")
    for j in range(chunks):
        g1[j] = tn(h1[...], U[j].reshape(rows, width)).astype(BF).reshape(g1.shape[1:])
        at("inner", j)

    load("rinv", (rinv_h, h1))
    need("w1", "rstd", "unit")
    d_gain, d_shift, d_bias = blank, blank, blank
    for i, half_rows in enumerate(halves):
        d_normed = dr[half_rows, :]
        for j in range(chunks):
            d_normed = d_normed + nt(take(j, i), W[j * width : (j + 1) * width, :])
        unit = A[3, half_rows, :].astype(F32)
        d_shift = d_shift + column_sum(d_normed)
        d_gain = d_gain + column_sum(d_normed * unit)
        d_unit = d_normed * gain1
        d_sum1 = d_unit - row_mean(d_unit) - unit * row_mean(d_unit * unit)
        d_sum1 = rstd[half_rows, 0:1] * d_sum1
        dr[half_rows, :] = d_sum1
        d_attn = d_sum1.astype(BF)
        df[half_rows, :] = d_attn
        d_bias = d_bias + column_sum(d_attn.astype(F32))
        at("norm", i)
    load("wqkv", (wqkv_h, W.at[pl.ds(0, 3 * width)]))
    load("x", (x_h, A.at[3]))
    sm[0:1, :] = d_gain
    sm[2:3, :] = d_shift
    sm[6:7, :] = d_bias

    need("ctx", "wo")
    U[(3,) + corner] = tn(ctx[...], df[...]).astype(BF).reshape(g1.shape[1:])
    at("attn")
    need("rinv")
    for half_rows in halves:
        d_ctx = nt(df[half_rows, :], WO[...]) * h1[half_rows, :].astype(F32)
        df[half_rows, :] = d_ctx.astype(BF)
    at("context")

    need("qkv", "x", "wqkv")
    masks = head_masks()
    zero = jnp.zeros((), BF)
    steps = tabs * pairs
    split = steps - 2 * tabs

    def place(n):
        late = n // split
        table = (1 - late) * lax.rem(n, tabs) + late * ((n - split) // 2)
        return table, (1 - late) * (n // tabs) + late * (pairs - 2 + lax.rem(n, 2))

    def weight_grad(buffer, first, last, side):
        cols = slice(first * 2 * HD, last * 2 * HD)
        grads = jnp.concatenate([A[i, :, cols] for i in range(3)], axis=1)
        spot = (buffer,) + corner + (slice(side, side + grads.shape[1]),)
        total = tn(A[3], grads).astype(BF)
        U[spot] = total.reshape(g1.shape[1:-1] + (grads.shape[1],))

    due = {3: (0, 0, 2, 0), 7: (1, 2, 4, 0), 10: (2, 4, 5, 0), 11: (2, 5, 6, width // 2)}

    def input_grad(table):
        half_rows = halves[table]
        d_input = dr[half_rows, :]
        for j in range(3):
            d_input = d_input + nt(A[j, half_rows, :], W[j * width : (j + 1) * width, :])
        h1[half_rows, :] = d_input.astype(BF)
        at("input", table)

    def fetch(n, slot):
        table, hp = place(n)
        copy(e_h.at[table, hp], e.at[slot], e_sem.at[slot]).start()

    fetch(0, 0)

    def attend(n, carry):
        table, hp = place(n)
        slot = lax.rem(n, 2)

        @pl.when(n + 1 < steps)
        def _():
            fetch(n + 1, 1 - slot)

        lanes = pl.ds(pl.multiple_of(hp * 2 * HD, 2 * HD), 2 * HD)
        here = pl.ds(pl.multiple_of(table * length, length), length)
        q2, k2, v2 = (A[i, here, lanes] for i in range(3))
        d_ctx = df[here, lanes]
        less = (-(ctx[here, lanes].astype(F32) * d_ctx.astype(F32))).astype(BF)
        right = jnp.concatenate([v2, jnp.ones((length, 2 * HD), BF)], axis=1)
        copy(e_h.at[0, 0], e.at[slot], e_sem.at[slot]).wait()
        d_query = d_key = d_value = None
        for h in range(2):
            mine = lambda values: jnp.where(masks[h], values, zero)
            d_head = mine(d_ctx)
            weights = e[slot, :, h * length : (h + 1) * length]
            d_raw = nt(jnp.concatenate([d_head, mine(less)], axis=1), right)
            d_scores = (weights.astype(F32) * d_raw).astype(BF)
            add = lambda held, new: new if held is None else held + new
            d_value = add(d_value, tn(weights, d_head))
            d_key = add(d_key, tn(d_scores, mine(q2)))
            d_query = add(d_query, nn(d_scores, mine(k2)))
        d_query = (d_query * (HD**-0.5)).astype(BF)
        d_value = d_value.astype(BF)
        A[0, here, lanes] = d_query
        A[1, here, lanes] = d_key.astype(BF)
        A[2, here, lanes] = d_value
        sm[4:5, lanes] = sm[4:5, lanes] + column_sum(d_query.astype(F32))
        sm[5:6, lanes] = sm[5:6, lanes] + column_sum(d_value.astype(F32))

        for step, what in due.items():
            pl.when(n == step)(functools.partial(weight_grad, *what))
        pl.when(n == steps - 3)(functools.partial(input_grad, 0))

        at("attend", n)
        return carry

    lax.fori_loop(0, steps, attend, 0)
    at("attended")
    input_grad(1)
    if link:
        at("leave")
        return
    pieces = [(h1, outs[0]), (g2, outs[1]), (g1, outs[2]), (U.at[3, :, pl.ds(0, share)], outs[3]), (sm, outs[4])]
    pieces += [(U.at[i, :, pl.ds(0, share)], outs[5].at[i]) for i in range(3)]
    ends = [copy(src, dst, out_sem.at[i]) for i, (src, dst) in enumerate(pieces)]
    for end in ends:
        end.start()
    for end in ends:
        end.wait()


def backward(saved, weights, small, mesh_bits):
    (x, q, k, v, e, rinv, ctx, h1, xh, rstd, a, g, dr2, lo, sg) = saved
    wqkv, wo, w1, w2 = weights
    chunks, rows, width = a.shape
    hidden = w1.shape[1]
    tabs, length = x.shape[:2]
    shape = jax.ShapeDtypeStruct
    linked = mesh_bits == (4, 1) and width % 256 == 0 and chunks == 4
    lead = (2, 2, 2, 2) if linked else (2,)
    share, part = width // math.prod(lead), rows // math.prod(lead)
    flat = lambda array: array.reshape(rows, array.shape[-1])
    g2 = shape((chunks, 2, 2, width // 4, width) if linked else (chunks, width, width), BF)
    g1 = shape((chunks,) + lead + (share, width), BF)
    go = shape(lead + (share, width), BF)
    small_sum = shape((16, width), F32)
    ins = (a, g.reshape((chunks,) + lead + (part, width)))
    ins += tuple(flat(array) for array in (dr2, h1, xh, rstd, rinv, ctx, q, k, v, x))
    ins += (e, lo, wqkv.reshape(3 * width, width), wo, w1, w2, small, sg)
    mem, dma = pltpu.VMEM, pltpu.SemaphoreType.DMA
    act = mem((rows, width), BF)
    scratch = [mem(a.shape, BF), mem(ins[1].shape, BF), mem(w2.shape, BF), mem(wo.shape, BF)]
    scratch += [mem((rows, width), F32), act, act, mem((rows, 128), F32), act]
    scratch += [mem((2,) + e.shape[2:], BF), mem(small.shape, F32), mem(small_sum.shape, F32)]
    scratch += [mem(array.shape, BF) for array in (g2, g1)]
    scratch += [dma((32,)), dma((2,)), dma((8,))]
    if linked:
        blocks = shape((2 * tabs, length // 2, width), BF)
        quarter, count, half = width // 4, chunks + 4, share // 2
        outs = [blocks, blocks, shape((quarter // 2, width), F32), shape((count, half, width), F32)]
        outs += [small_sum, shape((8, 128), F32)]
        scratch += [mem((2, 2, 2, quarter, width), BF)]
        scratch += [mem((2,) * i + (quarter // 2, width), BF) for i in (3, 2, 1, 0)]
        scratch += [mem((count,) + (2,) * i + (share, width), BF) for i in (3, 2, 1, 0)]
        scratch += [mem((count, 32, width), BF)] * 2
        scratch += [mem(outs[2].shape, F32), mem(outs[3].shape, F32)]
        scratch += [mem((8,) + small_sum.shape, F32), mem((4,) + small_sum.shape, F32)]
        scratch += [mem((8, 8, 128), F32), mem((4, 8, 128), F32)]
        side = (32, width // 2)
        scratch += [mem((4, 2, 2) + side, BF), mem((3, 2, 2) + side, BF), mem((4,) + side, BF), mem((3,) + side, BF)]
        scratch += [dma((88,)), dma((88,)), dma((8,))]
        params = pltpu.CompilerParams(
            vmem_limit_bytes=VMEM_BYTES, collective_id=1, has_side_effects=True
        )
    else:
        outs = [shape((rows, width), BF), g2, g1, go, small_sum, shape((3,) + go.shape, BF)]
        params = pltpu.CompilerParams(vmem_limit_bytes=VMEM_BYTES)
    return linked, pl.pallas_call(
        functools.partial(backward_kernel, len(outs)),
        out_shape=outs,
        in_specs=anywhere(len(ins)),
        out_specs=anywhere(len(outs)),
        scratch_shapes=scratch,
        compiler_params=params,
        name="layer_backward",
    )(*ins)


def adam_update(grad_new, first, second, master, ema_old, rate):
    first_new = BETA_ONE * first + (1.0 - BETA_ONE) * grad_new
    second_new = BETA_TWO * second + (1.0 - BETA_TWO) * grad_new * grad_new
    fix_one = 1.0 - BETA_ONE**STEP
    fix_two = 1.0 - BETA_TWO**STEP
    master_new = master - rate * (
        first_new / fix_one / (jnp.sqrt(second_new / fix_two) + ADAM_EPS) + DECAY * master
    )
    ema_new = EMA_KEEP * ema_old + (1.0 - EMA_KEEP) * master_new
    return (first_new, second_new, master_new, ema_new)


def update_kernel(rates, clip_limit, names, *refs):
    total_in, outer_in, final_in, sum_in = refs[:4]
    states_in = [refs[4 + 4 * i : 8 + 4 * i] for i in range(5)]
    count_out = 6 * 4 + 5 + 1
    passed = refs[24:26]
    outs = refs[26 : 26 + count_out]
    refs = refs[26 + count_out :]
    passed = tuple(zip(passed, refs[:2], refs[-2:]))
    refs = refs[2:-2]
    total, outer, final, sums = refs[:4]
    states = [refs[4 + 4 * i : 8 + 4 * i] for i in range(5)]
    held = refs[24 : 24 + count_out]
    in_sem, out_sem, pass_sem = refs[24 + count_out :]
    copy = pltpu.make_async_copy
    loads = []

    def load(src, dst):
        loads.append(copy(src, dst, in_sem.at[len(loads)]))
        loads[-1].start()

    for src, dst in zip((total_in, outer_in, final_in, sum_in), (total, outer, final, sums)):
        load(src, dst)
    for group in range(5):
        for src, dst in zip(states_in[group], states[group]):
            load(src, dst)
    ends = []
    through = [copy(src, mid, pass_sem.at[i, 0]) for i, (src, _, mid) in enumerate(passed)]
    for each in through:
        each.start()

    def end(index):
        ends.append(copy(held[index], outs[index], out_sem.at[index]))
        ends[-1].start()

    width = outer.shape[-1]
    for i in range(4):
        loads[i].wait()
    norm = jnp.sqrt(jnp.sum(jnp.sum(total[...], axis=0, keepdims=True), axis=1, keepdims=True))
    scale = jnp.minimum(1.0, clip_limit / norm)
    held[29][...] = norm
    end(29)
    third = width // 3
    for group in range(5):
        for i in range(4):
            loads[4 + 4 * group + i].wait()
        state = states[group]
        base = 6 * group
        kinds = held[base : base + (5 if group == 4 else 6)]
        if group == 0:
            spots = [(outer[...], (slice(None),))]
        elif group == 1:
            spots = [(final[j], (slice(None), slice(j * width, (j + 1) * width))) for j in range(4)]
        elif group == 2:
            spots = [(final[4], (slice(None),))]
        elif group == 3:
            spots = [
                (final[5 + j][:, i * third : (i + 1) * third], (i, slice(None), slice(j * third, (j + 1) * third)))
                for i in range(3)
                for j in range(2)
            ]
            half = third // 2
            for i in range(3):
                for j in range(2):
                    side = (3 * j + i) * half
                    there = slice(2 * third + j * half, 2 * third + (j + 1) * half)
                    spots.append((final[7][:, side : side + half], (i, slice(None), there)))
        else:
            lines = width // 128
            packed = [
                sums[r : r + 1, i * 128 : (i + 1) * 128]
                for r in range(kinds[0].shape[0] // lines)
                for i in range(lines)
            ]
            spots = [(jnp.concatenate(packed, axis=0), (slice(None),))]
        for summed, spot in spots:
            grad = summed * scale
            first, second, master, ema = adam_update(
                grad, state[1][spot], state[2][spot], state[0][spot], state[3][spot], rates[group]
            )
            if group == 4:
                results = (grad, first, second, master, ema)
            else:
                results = (grad, first, second, master, master.astype(BF), ema)
            for kind, result in zip(kinds, results):
                kind[spot] = result
        for i in range(len(kinds)):
            end(base + i)
        if group == 1:
            for i, (_, dst, mid) in enumerate(passed):
                through[i].wait()
                ends.append(copy(mid, dst, pass_sem.at[i, 1]))
                ends[-1].start()
    for each in ends:
        each.wait()


def update(total, outer, final, sums, states, rates, clip_limit, passed):
    shape = jax.ShapeDtypeStruct
    outs = []
    for master, *_ in states[:4]:
        kind = shape(master.shape, F32)
        outs += [kind, kind, kind, kind, shape(master.shape, BF), kind]
    outs += [shape(states[4][0].shape, F32)] * 5 + [shape((1, 1), F32)]
    ins = (total, outer, final, sums) + tuple(array for group in states for array in group)
    held = ins + tuple(outs)
    ins += passed
    outs += [shape(array.shape, array.dtype) for array in passed]
    mem, dma = pltpu.VMEM, pltpu.SemaphoreType.DMA
    return pl.pallas_call(
        functools.partial(update_kernel, rates, clip_limit, None),
        out_shape=outs,
        in_specs=anywhere(len(ins)),
        out_specs=anywhere(len(outs)),
        scratch_shapes=[mem(array.shape, array.dtype) for array in held]
        + [dma((len(ins),)), dma((len(outs),)), dma((2, 2))]
        + [mem(array.shape, array.dtype) for array in passed],
        compiler_params=pltpu.CompilerParams(vmem_limit_bytes=VMEM_BYTES),
        name="update",
    )(*ins)


def partner_swap(values, bit):
    count = lax.axis_size(AXES)
    return lax.ppermute(values, AXES, [(place, place ^ (1 << bit)) for place in range(count)])


def bit_order():
    bits = lax.axis_size(AXES).bit_length() - 1
    return list(range(1, bits)) + [0]


def scatter_sum(rows):
    order = bit_order()
    place = lax.axis_index(AXES)
    left = list(reversed(range(len(order))))
    held = rows.reshape((2,) * len(order) + rows.shape[1:])
    for bit in order:
        axis = left.index(bit)
        mine = (place >> bit) & 1
        keep = lax.dynamic_index_in_dim(held, mine, axis, keepdims=False)
        send = lax.dynamic_index_in_dim(held, 1 - mine, axis, keepdims=False)
        total = keep.astype(F32) + partner_swap(send, bit).astype(F32)
        left.remove(bit)
        held = total.astype(BF) if left else total
    return held


def butterfly_sum(values):
    for bit in bit_order():
        values = values + partner_swap(values, bit)
    return values


def sums_by_permutes(outs, width, tabs):
    grad, g2, g1, go, sums, gq = outs
    shards = lax.axis_size(AXES)
    outer = scatter_sum(g2.reshape(shards, -1)).reshape(-1, width)
    pieces = [g1.reshape(-1, shards, width // shards, width), go.reshape(1, shards, -1, width)]
    pieces = jnp.concatenate(pieces + [gq.reshape(-1, shards, width // shards, width)], axis=0)
    pieces = pieces.swapaxes(0, 1)
    final = scatter_sum(pieces.reshape(shards, -1)).reshape(pieces.shape[1:])
    sums = butterfly_sum(sums)
    total = butterfly_sum((jnp.sum(outer * outer) + jnp.sum(final * final)).reshape(1))
    total = jnp.zeros((8, 128), F32).at[0, 0].set(total[0] + jnp.sum(sums * sums))
    return grad, total, outer, final, sums


def unswap(rows, length):
    blocks = rows.reshape(-1, length, rows.shape[-1])
    return lax.all_to_all(blocks, "seq", split_axis=1, concat_axis=0, tiled=True)


def body(
    tables_in, out_cot, segment_ids, row_ids, col_ids,
    qkv_weight, out_weight, ffn_in_weight, ffn_out_weight, small_params,
    qkv_master, qkv_first, qkv_second, qkv_ema,
    out_master, out_first, out_second, out_ema,
    ffn_in_master, ffn_in_first, ffn_in_second, ffn_in_ema,
    ffn_out_master, ffn_out_first, ffn_out_second, ffn_out_ema,
    small_first, small_second, small_ema,
):
    width, hidden = ffn_in_weight.shape
    pack = lambda values: values.reshape(-1, 128)
    small = pack(small_params)
    weights = (qkv_weight, out_weight, ffn_in_weight, ffn_out_weight)
    saved = forward(tables_in, out_cot, segment_ids, row_ids, col_ids, *weights, small)
    bits = tuple(lax.axis_size(axis).bit_length() - 1 for axis in AXES)
    linked, outs = backward(saved, weights, small, bits)
    if linked:
        input_grad, layer_out, outer, final, sums, total = outs
    else:
        length = 2 * tables_in.shape[1]
        grad, total, outer, final, sums = sums_by_permutes(outs, width, tables_in.shape[0])
        input_grad, layer_out = unswap(grad, length), unswap(saved[13], length)
    states = [
        (ffn_out_master, ffn_out_first, ffn_out_second, ffn_out_ema),
        (ffn_in_master, ffn_in_first, ffn_in_second, ffn_in_ema),
        (out_master, out_first, out_second, out_ema),
        (qkv_master, qkv_first, qkv_second, qkv_ema),
        (small, pack(small_first), pack(small_second), pack(small_ema)),
    ]
    rates = (hidden**-0.5, width**-0.5, max(width // 128, 1) ** -0.5, width**-0.5, SMALL_RATE)
    entries = 4 * width * width + 2 * width * hidden + 8 * width + hidden
    new = update(total, outer, final, sums, states, rates, math.sqrt(float(entries)), (layer_out, input_grad))
    wo_new, wi_new, o_new, qkv_new = (new[6 * i : 6 * i + 6] for i in range(4))
    sm_new = [values.reshape(-1) for values in new[24:29]]
    groups = (qkv_new, o_new, wi_new, wo_new)
    return (
        *new[30:32],
        *[group[0] for group in groups],
        sm_new[0],
        new[29].reshape(()),
        *[values for group in groups for values in group[1:]],
        sm_new[1],
        sm_new[2],
        sm_new[3],
        sm_new[4],
    )


def solution(mesh):
    rows = P("batch", "seq", None)
    ids = P("batch", None)
    shard3 = P(None, AXES, None)
    shard2 = P(AXES, None)
    in_specs = (rows, rows, ids, ids, ids) + (P(),) * 5 + (shard3,) * 4 + (shard2,) * 12 + (P(),) * 3
    out_specs = (rows, rows, shard3, shard2, shard2, shard2, P(), P())
    out_specs += (shard3,) * 5 + (shard2,) * 15 + (P(),) * 4
    return jax.shard_map(body, mesh=mesh, in_specs=in_specs, out_specs=out_specs, check_vma=False)
```

```python
import functools
import math

import jax
import jax.numpy as jnp
from jax import lax
from jax.experimental import pallas as pl
from jax.experimental.pallas import tpu as pltpu
from jax.sharding import PartitionSpec as P

HD = 64
STEP = 10
EPS_NORM = 1e-06
NEG_BIG = -1e30
BETA_ONE = 0.9
BETA_TWO = 0.999
ADAM_EPS = 1e-08
DECAY = 0.01
EMA_KEEP = 0.8
SMALL_RATE = 0.1
AXES = ("batch", "seq")
MESH = pl.DeviceIdType.MESH
VMEM_BYTES = 61 << 20
BF = jnp.bfloat16
F32 = jnp.float32


def nn(left, right):
    return lax.dot_general(left, right, (((1,), (0,)), ((), ())), preferred_element_type=F32)


def nt(left, right):
    return lax.dot_general(left, right, (((1,), (1,)), ((), ())), preferred_element_type=F32)


def tn(left, right):
    return lax.dot_general(left, right, (((0,), (0,)), ((), ())), preferred_element_type=F32)


def row_mean(values):
    return jnp.mean(values, axis=1, keepdims=True)


def column_sum(values):
    return jnp.sum(values, axis=0, keepdims=True)


def gelu_pair(inner):
    size = jnp.abs(inner) * 0.7071067811865476
    t = pl.reciprocal(1.0 + 0.3275911 * size)
    bell = jnp.exp(inner * inner * -0.5)
    series = (((1.061405429 * t - 1.453152027) * t + 1.421413741) * t - 0.284496736) * t
    half = (series + 0.254829592) * t * (0.5 * bell)
    share = jnp.where(inner > 0, 1.0 - half, half)
    return inner * share, share + inner * bell * 0.3989422804014327


def small_row(packed, index, width):
    lines = width // 128
    return jnp.concatenate([packed[index * lines + i : index * lines + i + 1, :] for i in range(lines)], axis=1)


def head_masks():
    lane = lax.broadcasted_iota(jnp.int32, (1, 2 * HD), 1)
    return (lane < HD, lane >= HD)


def forward_kernel(
    tables_h, cot_h, seg_h, row_h, col_h, wqkv_h, wo_h, w1_h, w2_h, small_h,
    x_o, q_o, k_o, v_o, e_o, rinv_o, ctx_o, h1_o, xh_o, rstd_o, a_o, g_o, dr2_o, lo_o, sg_o,
    x, cot, seg, row, col, wqkv, wo, w1, w2, small, bias, inner_bias,
    q, k, v, e, rinv, ctx, h1, xh, rstd, a, g, dr2, lo, sg, h1f,
    in_sem, out_sem, e_sem, send_sem, recv_sem,
):
    tabs, length, width = x.shape
    block = length // 2
    hidden = w1.shape[1]
    pairs = width // (2 * HD)
    batch, me = lax.axis_index("batch"), lax.axis_index("seq")
    peer = (batch, 1 - me)
    copy = pltpu.make_async_copy
    barrier = pltpu.get_barrier_semaphore()
    pl.semaphore_signal(barrier, inc=1, device_id=peer, device_id_type=MESH)
    own_rows = pl.ds(pl.multiple_of(me * block, block), block)
    peer_rows = pl.ds(pl.multiple_of((1 - me) * block, block), block)

    sources = [(small_h, small), (wqkv_h, wqkv), (seg_h, seg), (row_h, row), (col_h, col)]
    sources += [(wo_h, wo), (w1_h, w1), (w2_h, w2)]
    sources += [(tables_h.at[me * tabs + t], x.at[t, own_rows]) for t in range(tabs)]
    sources += [(cot_h.at[me * tabs + t], cot.at[t, own_rows]) for t in range(tabs)]
    loads = [copy(src, dst, in_sem.at[i]) for i, (src, dst) in enumerate(sources)]
    for i in (8, 9, 1, 0, 2, 3, 4, 5, 6, 7, 10, 11):
        loads[i].start()

    def swap(index):
        source, place = (tables_h, x) if index < tabs else (cot_h, cot)
        t = index % tabs
        return pltpu.make_async_remote_copy(
            src_ref=source.at[(1 - me) * tabs + t],
            dst_ref=place.at[t, own_rows],
            send_sem=send_sem.at[index],
            recv_sem=recv_sem.at[index],
            device_id=peer,
            device_id_type=MESH,
        )

    pl.semaphore_wait(barrier, 1)
    swap(0).start()

    stores = []

    def store(index, src, dst):
        stores.append(copy(src, dst, out_sem.at[index]))
        stores[-1].start()

    for i in (0, 1, 8, 9):
        loads[i].wait()
    gain1, gain2, shift1, shift2, bias_q, bias_v, bias_o, bias_f2 = (
        small_row(small, i, width) for i in range(8)
    )
    inner_bias[...] = small_row(small[8 * (width // 128) :, :], 0, hidden)
    masks = head_masks()
    zero = jnp.zeros((), BF)

    def project(t, rows):
        block_x = x[t, rows, :]
        q[t, rows, :] = ((nn(block_x, wqkv[0]) + bias_q) * (HD**-0.5)).astype(BF)
        k[t, rows, :] = nn(block_x, wqkv[1]).astype(BF)
        v[t, rows, :] = (nn(block_x, wqkv[2]) + bias_v).astype(BF)

    for t in range(tabs):
        project(t, own_rows)
    for t in range(1, tabs):
        swap(t).start()
    for i in (2, 3, 4):
        loads[i].wait()
    for t in range(tabs):
        keys = [ids[pl.ds(me * tabs + t, 1), :].astype(F32) for ids in (seg, row, col)]
        wide = [jnp.transpose(jnp.broadcast_to(ids, (128, length)))[:, 0:1] for ids in keys]
        seen = (wide[0] == 0.0) | (keys[0] == 0.0)
        seen = seen | (wide[1] == keys[1]) | (wide[2] == keys[2])
        bias[t] = jnp.where(seen, 0.0, NEG_BIG)

    for t in range(tabs):
        swap(t).wait_recv()
        if t == 0:
            swap(tabs).start()
        project(t, peer_rows)
        store(16 * t + 14, x.at[t], x_o.at[t])

        def pair(hp, carry):
            lanes = pl.ds(pl.multiple_of(hp * 2 * HD, 2 * HD), 2 * HD)
            slot = lax.rem(hp, 2)

            @pl.when(t * pairs + hp >= 2)
            def _():
                copy(e.at[slot], e_o.at[0, 0], e_sem.at[slot]).wait()

            q2, k2, v2 = q[t, :, lanes], k[t, :, lanes], v[t, :, lanes]
            one = jnp.ones((length, 2 * HD), BF)
            rows = 256
            for start in range(0, length, rows):
                here = slice(start, start + rows)
                for h in range(2):
                    scores = nt(jnp.where(masks[h], q2[here], zero), k2) + bias[t, here, :]
                    top = jnp.max(scores, axis=1, keepdims=True)
                    e[slot, here, h * length : (h + 1) * length] = jnp.exp(scores - top).astype(BF)
            right = [
                jnp.concatenate([jnp.where(m, v2, zero), jnp.where(m, one, zero)], axis=1)
                for m in masks
            ]
            both = nn(e[slot], jnp.concatenate(right, axis=0))
            inverse = pl.reciprocal(both[:, 2 * HD :])
            rinv[t, :, lanes] = inverse.astype(BF)
            ctx[t, :, lanes] = (both[:, : 2 * HD] * inverse).astype(BF)
            copy(e.at[slot], e_o.at[t, hp], e_sem.at[slot]).start()
            return carry

        lax.fori_loop(0, pairs, pair, 0)
        for i, (src, dst) in enumerate(((q, q_o), (k, k_o), (v, v_o), (rinv, rinv_o), (ctx, ctx_o))):
            store(16 * t + i, src.at[t], dst.at[t])
        if t == 0:
            for later in range(tabs + 1, 2 * tabs):
                swap(later).start()
            loads[5].wait()
        sum1 = x[t].astype(F32) + nn(ctx[t], wo[...]) + bias_o
        centre = sum1 - row_mean(sum1)
        scale = lax.rsqrt(row_mean(centre * centre) + EPS_NORM)
        unit = centre * scale
        xh[t] = unit.astype(BF)
        rstd[t] = jnp.broadcast_to(scale, (length, 128))
        normed = unit * gain1 + shift1
        h1f[...] = normed
        h1[t] = normed.astype(BF)
        for i, (src, dst) in enumerate(((h1, h1_o), (xh, xh_o), (rstd, rstd_o))):
            store(16 * t + 5 + i, src.at[t], dst.at[t])
        if t == 0:
            loads[6].wait()
        rows = pl.ds(t * length, length)
        step = 768

        def inner(j, carry):
            for sub in range(width // step):
                here = slice(sub * step, (sub + 1) * step)
                there = pl.ds(pl.multiple_of(j * width + sub * step, step), step)
                active, slope = gelu_pair(nn(h1[t], w1[:, there]) + inner_bias[0:1, there])
                a[j, rows, here] = active.astype(BF)
                g[j, rows, here] = slope.astype(BF)
            return carry

        lax.fori_loop(0, hidden // width, inner, 0)
        store(16 * t + 8, a.at[:, rows], a_o.at[:, rows])
        store(16 * t + 9, g.at[:, rows], g_o.at[:, rows])
        if t == 0:
            loads[7].wait()
        sum2 = h1f[...] + bias_f2
        for j in range(hidden // width):
            sum2 = sum2 + nn(a[j, rows, :], w2[j * width : (j + 1) * width, :])
        centre = sum2 - row_mean(sum2)
        scale = lax.rsqrt(row_mean(centre * centre) + EPS_NORM)
        unit = centre * scale
        lo[t] = (unit * gain2 + shift2).astype(BF)
        loads[10 + t].wait()
        swap(tabs + t).wait_recv()
        back = cot[t].astype(F32)
        d_unit = back * gain2
        d_sum2 = scale * (d_unit - row_mean(d_unit) - unit * row_mean(d_unit * unit))
        dr2[t] = d_sum2
        parts = [column_sum(back * unit), column_sum(back), column_sum(d_sum2.astype(BF).astype(F32))]
        parts = jnp.concatenate(parts + [jnp.zeros((5, width), F32)], axis=0)
        sg[...] = parts if t == 0 else sg[...] + parts
        store(16 * t + 10, dr2.at[t], dr2_o.at[t])
        store(16 * t + 11, lo.at[t], lo_o.at[t])
    store(12, sg, sg_o)
    for stored in stores:
        stored.wait()
    for slot in range(2):
        copy(e.at[slot], e_o.at[0, 0], e_sem.at[slot]).wait()
    for index in range(2 * tabs):
        swap(index).wait_send()


def anywhere(count):
    return [pl.BlockSpec(memory_space=pl.ANY)] * count


def forward(tables_in, out_cot, seg, row, col, wqkv, wo, w1, w2, small):
    tabs, length = tables_in.shape[0] // 2, tables_in.shape[1] * 2
    width, hidden = w1.shape
    pairs, chunks, rows = width // (2 * HD), hidden // width, tabs * length
    shape = jax.ShapeDtypeStruct
    act = shape((tabs, length, width), BF)
    wide = shape((chunks, rows, width), BF)
    outs = [act] * 4 + [shape((tabs, pairs, length, 2 * length), BF)] + [act] * 4
    outs += [shape((tabs, length, 128), F32), wide, wide, shape(act.shape, F32), act]
    outs += [shape((8, width), F32)]
    ins = (tables_in, out_cot, seg, row, col, wqkv, wo, w1, w2, small)
    like = lambda array: pltpu.VMEM(array.shape, array.dtype)
    scratch = [like(act), like(act)] + [like(array) for array in ins[2:]]
    scratch += [pltpu.VMEM((tabs, length, length), F32), pltpu.VMEM((1, hidden), F32)]
    scratch += [like(array) for array in outs[1:4]] + [pltpu.VMEM((2, length, 2 * length), BF)]
    scratch += [like(array) for array in outs[5:]] + [pltpu.VMEM((length, width), F32)]
    dma = pltpu.SemaphoreType.DMA
    return pl.pallas_call(
        forward_kernel,
        out_shape=outs,
        in_specs=anywhere(len(ins)),
        out_specs=anywhere(len(outs)),
        scratch_shapes=scratch + [dma((16,)), dma((16 * tabs,)), dma((2,)), dma((8,)), dma((8,))],
        compiler_params=pltpu.CompilerParams(
            vmem_limit_bytes=VMEM_BYTES, collective_id=0, has_side_effects=True
        ),
        name="layer_forward",
    )(*ins)


PLAN = {
    ("slope", 1): (("core2", 1),),
    ("inner", 0): (("begin", 0),),
    ("inner", 1): (("begin", 1),),
    ("inner", 2): (("begin", 2), ("advance", 0), ("core2", 0),),
    ("inner", 3): (("begin", 3), ("advance", 1),),
    ("norm", 0): (("advance", 3), ("advance", 2),),
    ("norm", 1): (("advance", 0),),
    ("attn", None): (("begin", 4),),
    ("context", None): (("advance", 1),),
    ("attend", 0): (("x2", 1),),
    ("attend", 1): (("rows", 0), ("advance", 3),),
    ("attend", 2): (("advance", 2),),
    ("attend", 3): (("begin", 5), ("x2", 0),),
    ("attend", 4): (("advance", 1), ("advance", 4),),
    ("attend", 5): (("advance", 0),),
    ("attend", 6): (("advance", 5),),
    ("attend", 7): (("begin", 6), ("advance", 1), ("advance", 2), ("y2", 1),),
    ("attend", 9): (("advance", 4), ("advance", 6), ("y2", 0),),
    ("attend", 10): (("begin", 7), ("advance", 1),),
    ("attend", 11): (("begin", 8), ("advance", 5), ("advance", 7), ("advance", 6),),
    ("attended", None): (("advance", 8), ("advance", 0), ("z2", 1),),
    ("input", 1): (("advance", 5),),
    ("leave", None): (("advance", 7), ("advance", 6), ("advance", 4), ("advance", 2), ("z2", 0), ("advance", 8), ("advance", 7), ("advance", 4), ("advance", 3), ("advance", 2), ("near", 0), ("advance", 6), ("advance", 5), ("advance", 3), ("advance", 7), ("advance", 4), ("w2", 0), ("advance", 8), ("advance", 3), ("advance", 5), ("advance", 0), ("advance", 6), ("advance", 7), ("far", 0),),
}


class Link:
    FIRST_Y = ("core", "y", "z", "w", "x")
    FIRST_Z = ("core", "z", "w", "y", "x")

    def __init__(self, rest, g2, g1, full, sm, grad, lo_h, outs):
        (self.half2, self.x2, self.y2, self.z2, self.w2, self.half, self.two, self.one, self.last) = rest[:9]
        (self.x_send, self.x_get, self.final2, self.final, self.slots8, self.slots4) = rest[9:15]
        (self.square8, self.square4, self.plane_out, self.plane_get, self.line_out, self.line_get) = rest[15:21]
        self.send_sem, self.recv_sem, self.own_sem = rest[21:]
        self.g2, self.g1, self.full, self.sm, self.grad = g2, g1, full, sm, grad
        self.lo_h, self.outs = lo_h, outs
        batch, seq = lax.axis_index("batch"), lax.axis_index("seq")
        self.batch, self.seq = batch, seq
        self.bit = {
            "core": lax.rem(batch, 2),
            "y": lax.rem(batch // 2, 2),
            "z": lax.rem(batch // 4, 2),
            "w": batch // 8,
            "x": seq,
        }
        self.jump = {"core": 1, "y": 2, "z": 4, "w": 8}
        width = g1.shape[-1]
        whole = pl.ds(0, width)
        self.chunks = [(c, whole) for c in range(7)]
        self.chunks += [(7, pl.ds(0, width // 2)), (7, pl.ds(width // 2, width // 2))]
        y, z = self.FIRST_Y, self.FIRST_Z
        self.order = [z, y, y, z, z, y, y, y, y]
        count = len(self.chunks)
        self.state = [0] * count
        self.direct = count - 1
        self.memo = None
        self.halves2 = 0
        self.held = [["w", "z", "y"] for _ in range(count)]
        self.near = [None] + [tuple(n for b, n in ((1, "x"), (2, "core"), (4, "y")) if m & b) for m in range(1, 8)]
        self.far = [None] + [tuple(n for b, n in ((1, "z"), (2, "w")) if m & b) for m in range(1, 4)]

    def device(self, names):
        batch, seq = self.batch, self.seq
        for name in names:
            if name == "x":
                seq = 1 - seq
            else:
                batch = batch + self.jump[name] * (1 - 2 * self.bit[name])
        return (batch, seq)

    def remote(self, index, src, dst, names):
        return pltpu.make_async_remote_copy(
            src_ref=src,
            dst_ref=dst,
            send_sem=self.send_sem.at[index],
            recv_sem=self.recv_sem.at[index],
            device_id=self.device(names),
            device_id_type=MESH,
        )

    def full_part(self, chunk, core):
        buffer, cols = self.chunks[chunk]
        kept = self.g1.shape[0]
        rows = pl.ds(0, self.g1.shape[-2])
        ref, index = (self.g1, buffer) if buffer < kept else (self.full, (buffer + 3) % 4)
        return ref.at[index, :, :, :, core, rows, cols]

    def stage(self, chunk, number, where=()):
        buffer, cols = self.chunks[chunk]
        ref = (self.half, self.two, self.one, self.last)[number]
        where = tuple(where) + (slice(None),) * (len(ref.shape) - 3 - len(where))
        return ref.at[(buffer,) + where + (slice(None), cols)]

    def pick(self, chunk, name, other):
        value = 1 - self.bit[name] if other else self.bit[name]
        return tuple(value if axis == name else slice(None) for axis in self.held[chunk])

    def phase(self, chunk, number):
        name = self.order[chunk][number]
        buffer, cols = self.chunks[chunk]
        index = chunk * 5 + number
        if name == "core":
            src, dst = self.full_part(chunk, 1 - self.bit["core"]), self.stage(chunk, 0)
        elif name == "x":
            src, dst = self.x_send.at[buffer, :, cols], self.x_get.at[buffer, :, cols]
        else:
            src = self.stage(chunk, number - 1, self.pick(chunk, name, True))
            dst = self.stage(chunk, number)
        return self.remote(index, src, dst, (name,))

    def flips(self, names):
        values = [self.bit[name] for name in names]
        for m in range(4):
            flip = [(m >> i) & 1 for i in range(2)]
            low, high = (1 - v if f else v for v, f in zip(values, flip))
            yield m, 2 * high + low, tuple(n for n, f in zip(names, flip) if f)

    def plane(self):
        return [
            self.remote(40 + m, self.plane_out.at[place], self.plane_get.at[m - 1], names)
            for m, place, names in self.flips(("x", "y"))
            if m
        ]

    def line(self):
        return [
            self.remote(84 + m, self.line_out.at[place], self.line_get.at[m - 1], names)
            for m, place, names in self.flips(("z", "w"))
            if m
        ]

    def advance_direct(self):
        chunk = self.direct
        buffer, cols = self.chunks[chunk]
        number = self.state[chunk]
        if number == 0:
            self.phase(chunk, 0).wait_recv()
            total = self.stage(chunk, 0)[...].astype(F32) + self.full_part(chunk, self.bit["core"])[...].astype(F32)
            share = total.shape[3] // 2
            pad = jnp.zeros(total.shape[:2] + (self.plane_out.shape[3] - share, total.shape[4]), F32)
            for y in range(2):
                for x in range(2):
                    rows = total[:, :, y, x * share : (x + 1) * share]
                    self.plane_out[2 * y + x] = jnp.concatenate([rows, pad], axis=2).astype(BF)
            self.start_all(self.plane())
            self.state[chunk] = 1
            return
        sent = self.plane() if number == 1 else self.line()
        out, get = (self.plane_out, self.plane_get) if number == 1 else (self.line_out, self.line_get)
        for each in sent:
            each.wait_recv()
        names = ("x", "y") if number == 1 else ("z", "w")
        total = out[2 * self.bit[names[1]] + self.bit[names[0]]].astype(F32)
        for m in range(3):
            total = total + get[m].astype(F32)
        if number == 1:
            self.line_out[...] = total.reshape(self.line_out.shape).astype(BF)
            self.start_all(self.line())
            self.state[chunk] = 2
        else:
            self.final.at[buffer, :, cols][...] = total[0 : self.final.shape[1]]
            self.state[chunk] = 5

    def begin(self, chunk):
        self.phase(chunk, 0).start()

    def advance(self, *chunks):
        for chunk in chunks:
            if chunk == self.direct:
                self.advance_direct()
                continue
            number = self.state[chunk]
            name = self.order[chunk][number]
            buffer, cols = self.chunks[chunk]
            self.phase(chunk, number).wait_recv()
            if name == "x":
                rows = self.final.shape[1]
                here = self.x_get.at[buffer, :, cols][...].astype(F32)[0:rows]
                ref = self.final.at[buffer, :, cols]
                ref[...] = ref[...] + here
                self.state[chunk] = 5
                continue
            if name == "core":
                kept = self.full_part(chunk, self.bit["core"])
            else:
                kept = self.stage(chunk, number - 1, self.pick(chunk, name, False))
                self.held[chunk].remove(name)
            ref = self.stage(chunk, number)
            total = ref[...].astype(F32) + kept[...].astype(F32)
            if number < 3:
                ref[...] = total.astype(BF)
            else:
                rows = total.shape[0] // 2
                low, high = total[0:rows], total[rows:]
                upper = self.seq == 1
                self.final.at[buffer, :, cols][...] = jnp.where(upper, high, low)
                pad = jnp.zeros((self.x_send.shape[1] - rows, low.shape[1]), F32)
                gone = jnp.concatenate([jnp.where(upper, low, high), pad], axis=0)
                self.x_send.at[buffer, :, cols][...] = gone.astype(BF)
            self.state[chunk] = number + 1
            self.phase(chunk, number + 1).start()

    def core2(self, j):
        src = self.g2.at[j, :, 1 - self.bit["core"]]
        return self.remote(50 + j, src, self.half2.at[j // 2, j % 2], ("core",))

    def core2_done(self, *which):
        for j in which:
            self.core2(j).wait_recv()
            kept = self.g2[j, :, self.bit["core"]].astype(F32)
            self.half2[j // 2, j % 2] = (self.half2[j // 2, j % 2].astype(F32) + kept).astype(BF)

    def side2(self, seq):
        rows = self.x2.shape[3]
        return pl.ds(pl.multiple_of(seq * rows, rows), rows)

    def copy_x2(self, w):
        src = self.half2.at[w, :, :, self.side2(1 - self.seq)]
        return self.remote(54 + w, src, self.x2.at[w], ("x",))

    def copy_y2(self, w):
        return self.remote(56 + w, self.x2.at[w, :, 1 - self.bit["y"]], self.y2.at[w], ("y",))

    def copy_z2(self, w):
        return self.remote(58 + w, self.y2.at[w, 1 - self.bit["z"]], self.z2.at[w], ("z",))

    def copy_w2(self):
        return self.remote(60, self.z2.at[1 - self.bit["w"]], self.w2, ("w",))

    def x2_done(self, w):
        self.copy_x2(w).wait_recv()
        for z in range(2):
            kept = self.half2[w, z, :, self.side2(self.seq), :].astype(F32)
            self.x2[w, z] = (self.x2[w, z].astype(F32) + kept).astype(BF)
        self.copy_y2(w).start()

    def y2_done(self, w):
        self.copy_y2(w).wait_recv()
        kept = self.x2[w, :, self.bit["y"]].astype(F32)
        self.y2[w] = (self.y2[w].astype(F32) + kept).astype(BF)
        self.copy_z2(w).start()

    def z2_done(self, w):
        self.copy_z2(w).wait_recv()
        kept = self.y2[w, self.bit["z"]].astype(F32)
        self.z2[w] = (self.z2[w].astype(F32) + kept).astype(BF)

    def w2_done(self):
        self.copy_w2().wait_recv()
        self.final2[...] = self.z2[self.bit["w"]].astype(F32) + self.w2[...].astype(F32)

    def back(self, index, src, table, tabs):
        block = self.outs[0].shape[1]
        there = pl.ds(pl.multiple_of((1 - self.seq) * block, block), block)
        dst = self.outs[1 if index == 61 else 0]
        if index == 61:
            return self.remote(61, src.at[:, there], dst.at[pl.ds(self.seq * tabs, tabs)], ("x",))
        rows = pl.ds(pl.multiple_of(table * 2 * block + (1 - self.seq) * block, block), block)
        return self.remote(index, src.at[rows], dst.at[self.seq * tabs + table], ("x",))

    def keep(self, index, src, table, tabs):
        block = self.outs[0].shape[1]
        sem = self.own_sem.at[index - 61]
        dst = self.outs[1 if index == 61 else 0]
        here = pl.ds(pl.multiple_of(self.seq * block, block), block)
        if index == 61:
            return pltpu.make_async_copy(src.at[:, here], dst.at[pl.ds(self.seq * tabs, tabs)], sem)
        rows = pl.ds(pl.multiple_of(table * 2 * block + self.seq * block, block), block)
        return pltpu.make_async_copy(src.at[rows], dst.at[self.seq * tabs + table], sem)

    def spread(self, base, slots, groups):
        return [
            self.remote(base + m, slots.at[0], slots.at[m], groups[m])
            for m in range(1, len(groups))
        ]

    def gathered(self, base, slots, groups):
        for sent in self.spread(base, slots, groups):
            sent.wait_recv()
        terms = [slots[m] for m in range(len(groups))]
        while len(terms) > 1:
            terms = [terms[i] + terms[i + 1] for i in range(0, len(terms), 2)]
        return terms[0]

    def start_all(self, copies):
        for each in copies:
            each.start()

    def act(self, kind, index):
        if kind == "begin":
            self.begin(index)
        elif kind == "advance":
            self.advance(index)
        elif kind == "core2":
            self.core2_done(2 * index, 2 * index + 1)
            self.copy_x2(index).start()
        elif kind == "x2":
            self.x2_done(index)
        elif kind == "y2":
            self.y2_done(index)
        elif kind == "z2":
            self.z2_done(index)
            self.halves2 += 1
            if self.halves2 == 2:
                self.copy_w2().start()
        elif kind == "w2":
            self.w2_done()
        elif kind == "rows":
            self.back(61, self.lo_h, 0, self.lo_h.shape[0]).start()
        elif kind == "near":
            self.slots4[0] = self.gathered(64, self.slots8, self.near)
            self.start_all(self.spread(71, self.slots4, self.far))
        elif kind == "far":
            self.sm[...] = self.gathered(71, self.slots4, self.far)

    def act_all(self, moves):
        for move in moves:
            self.act(*move)

    def at(self, name, n=None):
        tabs = self.lo_h.shape[0]
        if name == "attend":
            if self.memo is None:
                self.memo = (list(self.state), [list(held) for held in self.held], self.halves2)
            self.state, self.held = list(self.memo[0]), [list(held) for held in self.memo[1]]
            self.halves2 = self.memo[2]
            for (when, k), moves in PLAN.items():
                if when == name:
                    pl.when(n == k)(functools.partial(self.act_all, moves))
            return
        if name == "enter":
            barrier = pltpu.get_barrier_semaphore()
            for names in self.near[1:] + self.far[1:]:
                pl.semaphore_signal(barrier, inc=1, device_id=self.device(names), device_id_type=MESH)
        elif name == "outer":
            if n == 0:
                pl.semaphore_wait(pltpu.get_barrier_semaphore(), len(self.near) + len(self.far) - 2)
                self.keep(61, self.lo_h, 0, tabs).start()
            self.core2(n).start()
        elif name == "attended":
            self.slots8[0] = self.sm[...]
            self.start_all(self.spread(64, self.slots8, self.near))
        elif name == "input":
            self.back(62 + n, self.grad, n, tabs).start()
            self.keep(62 + n, self.grad, n, tabs).start()
        if name != "input" or n == tabs - 1:
            self.act_all(PLAN.get((name, n), ()))
        if name == "leave":
            self.finish(tabs)

    def finish(self, tabs):
        fold = lambda values: sum(
            (values * values)[:, i * 128 : (i + 1) * 128] for i in range(values.shape[1] // 128)
        )
        tile = lambda rows: jnp.sum(rows.reshape(rows.shape[0] // 8, 8, 128), axis=0)
        square = tile(fold(self.final2[...]))
        for buffer in range(self.final.shape[0]):
            square = square + tile(fold(self.final[buffer]))
        self.square8[0] = square
        near = self.spread(74, self.square8, self.near)
        self.start_all(near)
        ends = [(self.final2, self.outs[2]), (self.final, self.outs[3]), (self.sm, self.outs[4])]
        ends = [pltpu.make_async_copy(src, dst, self.own_sem.at[3 + i]) for i, (src, dst) in enumerate(ends)]
        self.start_all(ends)
        for chunk in range(len(self.state)):
            self.held[chunk] = ["w", "z", "y"]
            for number in range(1 if chunk == self.direct else 5):
                self.phase(chunk, number).wait_send()
                name = self.order[chunk][number]
                if name in self.held[chunk]:
                    self.held[chunk].remove(name)
        self.square4[0] = self.gathered(74, self.square8, self.near)
        far = self.spread(81, self.square4, self.far)
        self.start_all(far)
        small = tile(fold(self.sm[...]))
        sent = [self.core2(j) for j in range(4)] + [self.copy_w2()]
        sent += [copy(w) for copy in (self.copy_x2, self.copy_y2, self.copy_z2) for w in range(2)]
        sent += [self.back(61, self.lo_h, 0, tabs)]
        sent += [self.back(62 + t, self.grad, t, tabs) for t in range(tabs)]
        sent += self.plane() + self.line()
        sent += self.spread(64, self.slots8, self.near) + self.spread(71, self.slots4, self.far) + near
        for each in sent:
            each.wait_send()
        self.back(61, self.lo_h, 0, tabs).wait_recv()
        self.keep(61, self.lo_h, 0, tabs).wait()
        for t in range(tabs):
            self.back(62 + t, self.grad, t, tabs).wait_recv()
            self.keep(62 + t, self.grad, t, tabs).wait()
        self.square8[0] = self.gathered(81, self.square4, self.far) + small
        end = pltpu.make_async_copy(self.square8.at[0], self.outs[5], self.own_sem.at[6])
        end.start()
        for each in far:
            each.wait_send()
        for each in ends:
            each.wait()
        end.wait()


def backward_kernel(
    count, a_h, g_h, dr2_h, h1_h, xh_h, rstd_h, rinv_h, ctx_h, q_h, k_h, v_h, x_h, e_h, lo_h,
    wqkv_h, wo_h, w1_h, w2_h, small_h, sg_h,
    *rest,
):
    outs, rest = rest[:count], rest[count:]
    A, U, W, WO, dr, df, h1, rstd, ctx, e, small, sm, g2, g1 = rest[:14]
    in_sem, e_sem, out_sem = rest[14:17]
    chunks, rows, width = A.shape
    tabs, pairs, length, _ = e_h.shape
    share = g1.shape[-2]
    corner = (slice(None),) * (len(U.shape) - 3) + (slice(0, share),)
    copy = pltpu.make_async_copy
    link = Link(rest[17:], g2, g1, U, sm, h1, lo_h, outs) if len(rest) > 17 else None
    loads = {}
    used = [0]

    def load(name, *both):
        loads[name] = []
        for src, dst in both:
            loads[name].append(copy(src, dst, in_sem.at[used[0]]))
            used[0] += 1
            loads[name][-1].start()

    def need(*names):
        for name in names:
            for loaded in loads[name]:
                loaded.wait()

    load("dr2", (dr2_h, dr))
    load("a", *[(a_h.at[j], A.at[j]) for j in range(chunks)])
    load("small", (small_h, small), (sg_h, sm.at[pl.ds(0, 8)]))
    load("w2", (w2_h, W))
    load("g", *[(g_h.at[j], U.at[j]) for j in range(chunks)])
    load("h1", (h1_h, h1))
    load("rstd", (rstd_h, rstd))
    load("wo", (wo_h, WO))
    load("ctx", (ctx_h, ctx))
    at = link.at if link else (lambda *key: None)
    at("enter")
    half = rows // 2
    halves = [slice(i * half, (i + 1) * half) for i in range(2)]
    inside = U.shape[2:]
    take = lambda j, i: U[j, i].reshape(half, width)
    need("small", "dr2")
    first = sm[0:8, :]
    blank = jnp.zeros((1, width), F32)
    order = [blank, first[0:1], blank, first[1:2], blank, blank, blank, first[2:3]]
    sm[...] = jnp.concatenate(order + [jnp.zeros((8, width), F32)], axis=0)
    gain1 = small_row(small, 0, width)
    df[...] = dr[...].astype(BF)

    for j in range(chunks):
        loads["a"][j].wait()
        g2[j] = tn(A[j], df[...]).astype(BF).reshape(g2.shape[1:])
        at("outer", j)
    load("qkv", *[(src, A.at[i]) for i, src in enumerate((q_h, k_h, v_h))])
    load("unit", (xh_h, A.at[3]))

    need("w2")
    for j in range(chunks):
        loads["g"][j].wait()
        total = blank
        for i, half_rows in enumerate(halves):
            d_active = nt(df[half_rows, :], W[j * width : (j + 1) * width, :])
            d_inner = (d_active * take(j, i).astype(F32)).astype(BF)
            U[j, i] = d_inner.reshape(inside)
            total = total + column_sum(d_inner.astype(F32))
        sm[8 + j : 9 + j, :] = total
        at("slope", j)
    load("w1", *[(w1_h.at[:, pl.ds(j * width, width)], W.at[pl.ds(j * width, width)]) for j in range(chunks)])

    need("h1")
    for j in range(chunks):
        g1[j] = tn(h1[...], U[j].reshape(rows, width)).astype(BF).reshape(g1.shape[1:])
        at("inner", j)

    load("rinv", (rinv_h, h1))
    need("w1", "rstd", "unit")
    d_gain, d_shift, d_bias = blank, blank, blank
    for i, half_rows in enumerate(halves):
        d_normed = dr[half_rows, :]
        for j in range(chunks):
            d_normed = d_normed + nt(take(j, i), W[j * width : (j + 1) * width, :])
        unit = A[3, half_rows, :].astype(F32)
        d_shift = d_shift + column_sum(d_normed)
        d_gain = d_gain + column_sum(d_normed * unit)
        d_unit = d_normed * gain1
        d_sum1 = d_unit - row_mean(d_unit) - unit * row_mean(d_unit * unit)
        d_sum1 = rstd[half_rows, 0:1] * d_sum1
        dr[half_rows, :] = d_sum1
        d_attn = d_sum1.astype(BF)
        df[half_rows, :] = d_attn
        d_bias = d_bias + column_sum(d_attn.astype(F32))
        at("norm", i)
    load("wqkv", (wqkv_h, W.at[pl.ds(0, 3 * width)]))
    load("x", (x_h, A.at[3]))
    sm[0:1, :] = d_gain
    sm[2:3, :] = d_shift
    sm[6:7, :] = d_bias

    need("ctx", "wo")
    U[(3,) + corner] = tn(ctx[...], df[...]).astype(BF).reshape(g1.shape[1:])
    at("attn")
    need("rinv")
    for half_rows in halves:
        d_ctx = nt(df[half_rows, :], WO[...]) * h1[half_rows, :].astype(F32)
        df[half_rows, :] = d_ctx.astype(BF)
    at("context")

    need("qkv", "x", "wqkv")
    masks = head_masks()
    zero = jnp.zeros((), BF)
    steps = tabs * pairs
    split = steps - 2 * tabs

    def place(n):
        late = n // split
        table = (1 - late) * lax.rem(n, tabs) + late * ((n - split) // 2)
        return table, (1 - late) * (n // tabs) + late * (pairs - 2 + lax.rem(n, 2))

    def weight_grad(buffer, first, last, side):
        cols = slice(first * 2 * HD, last * 2 * HD)
        grads = jnp.concatenate([A[i, :, cols] for i in range(3)], axis=1)
        spot = (buffer,) + corner + (slice(side, side + grads.shape[1]),)
        total = tn(A[3], grads).astype(BF)
        U[spot] = total.reshape(g1.shape[1:-1] + (grads.shape[1],))

    due = {3: (0, 0, 2, 0), 7: (1, 2, 4, 0), 10: (2, 4, 5, 0), 11: (2, 5, 6, width // 2)}

    def input_grad(table):
        half_rows = halves[table]
        d_input = dr[half_rows, :]
        for j in range(3):
            d_input = d_input + nt(A[j, half_rows, :], W[j * width : (j + 1) * width, :])
        h1[half_rows, :] = d_input.astype(BF)
        at("input", table)

    def fetch(n, slot):
        table, hp = place(n)
        copy(e_h.at[table, hp], e.at[slot], e_sem.at[slot]).start()

    fetch(0, 0)

    def attend(n, carry):
        table, hp = place(n)
        slot = lax.rem(n, 2)

        @pl.when(n + 1 < steps)
        def _():
            fetch(n + 1, 1 - slot)

        lanes = pl.ds(pl.multiple_of(hp * 2 * HD, 2 * HD), 2 * HD)
        here = pl.ds(pl.multiple_of(table * length, length), length)
        q2, k2, v2 = (A[i, here, lanes] for i in range(3))
        d_ctx = df[here, lanes]
        less = (-(ctx[here, lanes].astype(F32) * d_ctx.astype(F32))).astype(BF)
        right = jnp.concatenate([v2, jnp.ones((length, 2 * HD), BF)], axis=1)
        copy(e_h.at[0, 0], e.at[slot], e_sem.at[slot]).wait()
        d_query = d_key = d_value = None
        for h in range(2):
            mine = lambda values: jnp.where(masks[h], values, zero)
            d_head = mine(d_ctx)
            weights = e[slot, :, h * length : (h + 1) * length]
            d_raw = nt(jnp.concatenate([d_head, mine(less)], axis=1), right)
            d_scores = (weights.astype(F32) * d_raw).astype(BF)
            add = lambda held, new: new if held is None else held + new
            d_value = add(d_value, tn(weights, d_head))
            d_key = add(d_key, tn(d_scores, mine(q2)))
            d_query = add(d_query, nn(d_scores, mine(k2)))
        d_query = (d_query * (HD**-0.5)).astype(BF)
        d_value = d_value.astype(BF)
        A[0, here, lanes] = d_query
        A[1, here, lanes] = d_key.astype(BF)
        A[2, here, lanes] = d_value
        sm[4:5, lanes] = sm[4:5, lanes] + column_sum(d_query.astype(F32))
        sm[5:6, lanes] = sm[5:6, lanes] + column_sum(d_value.astype(F32))

        for step, what in due.items():
            pl.when(n == step)(functools.partial(weight_grad, *what))
        pl.when(n == steps - 3)(functools.partial(input_grad, 0))

        at("attend", n)
        return carry

    lax.fori_loop(0, steps, attend, 0)
    at("attended")
    input_grad(1)
    if link:
        at("leave")
        return
    pieces = [(h1, outs[0]), (g2, outs[1]), (g1, outs[2]), (U.at[3, :, pl.ds(0, share)], outs[3]), (sm, outs[4])]
    pieces += [(U.at[i, :, pl.ds(0, share)], outs[5].at[i]) for i in range(3)]
    ends = [copy(src, dst, out_sem.at[i]) for i, (src, dst) in enumerate(pieces)]
    for end in ends:
        end.start()
    for end in ends:
        end.wait()


def backward(saved, weights, small, mesh_bits):
    (x, q, k, v, e, rinv, ctx, h1, xh, rstd, a, g, dr2, lo, sg) = saved
    wqkv, wo, w1, w2 = weights
    chunks, rows, width = a.shape
    hidden = w1.shape[1]
    tabs, length = x.shape[:2]
    shape = jax.ShapeDtypeStruct
    linked = mesh_bits == (4, 1) and width % 256 == 0 and chunks == 4
    lead = (2, 2, 2, 2) if linked else (2,)
    share, part = width // math.prod(lead), rows // math.prod(lead)
    flat = lambda array: array.reshape(rows, array.shape[-1])
    g2 = shape((chunks, 2, 2, width // 4, width) if linked else (chunks, width, width), BF)
    g1 = shape((chunks,) + lead + (share, width), BF)
    go = shape(lead + (share, width), BF)
    small_sum = shape((16, width), F32)
    ins = (a, g.reshape((chunks,) + lead + (part, width)))
    ins += tuple(flat(array) for array in (dr2, h1, xh, rstd, rinv, ctx, q, k, v, x))
    ins += (e, lo, wqkv.reshape(3 * width, width), wo, w1, w2, small, sg)
    mem, dma = pltpu.VMEM, pltpu.SemaphoreType.DMA
    act = mem((rows, width), BF)
    scratch = [mem(a.shape, BF), mem(ins[1].shape, BF), mem(w2.shape, BF), mem(wo.shape, BF)]
    scratch += [mem((rows, width), F32), act, act, mem((rows, 128), F32), act]
    scratch += [mem((2,) + e.shape[2:], BF), mem(small.shape, F32), mem(small_sum.shape, F32)]
    scratch += [mem(array.shape, BF) for array in (g2, g1)]
    scratch += [dma((32,)), dma((2,)), dma((8,))]
    if linked:
        blocks = shape((2 * tabs, length // 2, width), BF)
        quarter, count, half = width // 4, chunks + 4, share // 2
        outs = [blocks, blocks, shape((quarter // 2, width), F32), shape((count, half, width), F32)]
        outs += [small_sum, shape((8, 128), F32)]
        scratch += [mem((2, 2, 2, quarter, width), BF)]
        scratch += [mem((2,) * i + (quarter // 2, width), BF) for i in (3, 2, 1, 0)]
        scratch += [mem((count,) + (2,) * i + (share, width), BF) for i in (3, 2, 1, 0)]
        scratch += [mem((count, 32, width), BF)] * 2
        scratch += [mem(outs[2].shape, F32), mem(outs[3].shape, F32)]
        scratch += [mem((8,) + small_sum.shape, F32), mem((4,) + small_sum.shape, F32)]
        scratch += [mem((8, 8, 128), F32), mem((4, 8, 128), F32)]
        side = (32, width // 2)
        scratch += [mem((4, 2, 2) + side, BF), mem((3, 2, 2) + side, BF), mem((4,) + side, BF), mem((3,) + side, BF)]
        scratch += [dma((88,)), dma((88,)), dma((8,))]
        params = pltpu.CompilerParams(
            vmem_limit_bytes=VMEM_BYTES, collective_id=1, has_side_effects=True
        )
    else:
        outs = [shape((rows, width), BF), g2, g1, go, small_sum, shape((3,) + go.shape, BF)]
        params = pltpu.CompilerParams(vmem_limit_bytes=VMEM_BYTES)
    return linked, pl.pallas_call(
        functools.partial(backward_kernel, len(outs)),
        out_shape=outs,
        in_specs=anywhere(len(ins)),
        out_specs=anywhere(len(outs)),
        scratch_shapes=scratch,
        compiler_params=params,
        name="layer_backward",
    )(*ins)


def adam_update(grad_new, first, second, master, ema_old, rate):
    first_new = BETA_ONE * first + (1.0 - BETA_ONE) * grad_new
    second_new = BETA_TWO * second + (1.0 - BETA_TWO) * grad_new * grad_new
    fix_one = 1.0 - BETA_ONE**STEP
    fix_two = 1.0 - BETA_TWO**STEP
    master_new = master - rate * (
        first_new / fix_one / (jnp.sqrt(second_new / fix_two) + ADAM_EPS) + DECAY * master
    )
    ema_new = EMA_KEEP * ema_old + (1.0 - EMA_KEEP) * master_new
    return (first_new, second_new, master_new, ema_new)


def update_kernel(rates, clip_limit, names, *refs):
    total_in, outer_in, final_in, sum_in = refs[:4]
    states_in = [refs[4 + 4 * i : 8 + 4 * i] for i in range(5)]
    count_out = 6 * 4 + 5 + 1
    passed = refs[24:26]
    outs = refs[26 : 26 + count_out]
    refs = refs[26 + count_out :]
    passed = tuple(zip(passed, refs[:2], refs[-2:]))
    refs = refs[2:-2]
    total, outer, final, sums = refs[:4]
    states = [refs[4 + 4 * i : 8 + 4 * i] for i in range(5)]
    held = refs[24 : 24 + count_out]
    in_sem, out_sem, pass_sem = refs[24 + count_out :]
    copy = pltpu.make_async_copy
    loads = []

    def load(src, dst):
        loads.append(copy(src, dst, in_sem.at[len(loads)]))
        loads[-1].start()

    for src, dst in zip((total_in, outer_in, final_in, sum_in), (total, outer, final, sums)):
        load(src, dst)
    for group in range(5):
        for src, dst in zip(states_in[group], states[group]):
            load(src, dst)
    ends = []
    through = [copy(src, mid, pass_sem.at[i, 0]) for i, (src, _, mid) in enumerate(passed)]
    for each in through:
        each.start()

    def end(index):
        ends.append(copy(held[index], outs[index], out_sem.at[index]))
        ends[-1].start()

    width = outer.shape[-1]
    for i in range(4):
        loads[i].wait()
    norm = jnp.sqrt(jnp.sum(jnp.sum(total[...], axis=0, keepdims=True), axis=1, keepdims=True))
    scale = jnp.minimum(1.0, clip_limit / norm)
    held[29][...] = norm
    end(29)
    third = width // 3
    for group in range(5):
        for i in range(4):
            loads[4 + 4 * group + i].wait()
        state = states[group]
        base = 6 * group
        kinds = held[base : base + (5 if group == 4 else 6)]
        if group == 0:
            spots = [(outer[...], (slice(None),))]
        elif group == 1:
            spots = [(final[j], (slice(None), slice(j * width, (j + 1) * width))) for j in range(4)]
        elif group == 2:
            spots = [(final[4], (slice(None),))]
        elif group == 3:
            spots = [
                (final[5 + j][:, i * third : (i + 1) * third], (i, slice(None), slice(j * third, (j + 1) * third)))
                for i in range(3)
                for j in range(2)
            ]
            half = third // 2
            for i in range(3):
                for j in range(2):
                    side = (3 * j + i) * half
                    there = slice(2 * third + j * half, 2 * third + (j + 1) * half)
                    spots.append((final[7][:, side : side + half], (i, slice(None), there)))
        else:
            lines = width // 128
            packed = [
                sums[r : r + 1, i * 128 : (i + 1) * 128]
                for r in range(kinds[0].shape[0] // lines)
                for i in range(lines)
            ]
            spots = [(jnp.concatenate(packed, axis=0), (slice(None),))]
        for summed, spot in spots:
            grad = summed * scale
            first, second, master, ema = adam_update(
                grad, state[1][spot], state[2][spot], state[0][spot], state[3][spot], rates[group]
            )
            if group == 4:
                results = (grad, first, second, master, ema)
            else:
                results = (grad, first, second, master, master.astype(BF), ema)
            for kind, result in zip(kinds, results):
                kind[spot] = result
        for i in range(len(kinds)):
            end(base + i)
        if group == 1:
            for i, (_, dst, mid) in enumerate(passed):
                through[i].wait()
                ends.append(copy(mid, dst, pass_sem.at[i, 1]))
                ends[-1].start()
    for each in ends:
        each.wait()


def update(total, outer, final, sums, states, rates, clip_limit, passed):
    shape = jax.ShapeDtypeStruct
    outs = []
    for master, *_ in states[:4]:
        kind = shape(master.shape, F32)
        outs += [kind, kind, kind, kind, shape(master.shape, BF), kind]
    outs += [shape(states[4][0].shape, F32)] * 5 + [shape((1, 1), F32)]
    ins = (total, outer, final, sums) + tuple(array for group in states for array in group)
    held = ins + tuple(outs)
    ins += passed
    outs += [shape(array.shape, array.dtype) for array in passed]
    mem, dma = pltpu.VMEM, pltpu.SemaphoreType.DMA
    return pl.pallas_call(
        functools.partial(update_kernel, rates, clip_limit, None),
        out_shape=outs,
        in_specs=anywhere(len(ins)),
        out_specs=anywhere(len(outs)),
        scratch_shapes=[mem(array.shape, array.dtype) for array in held]
        + [dma((len(ins),)), dma((len(outs),)), dma((2, 2))]
        + [mem(array.shape, array.dtype) for array in passed],
        compiler_params=pltpu.CompilerParams(vmem_limit_bytes=VMEM_BYTES),
        name="update",
    )(*ins)


def partner_swap(values, bit):
    count = lax.axis_size(AXES)
    return lax.ppermute(values, AXES, [(place, place ^ (1 << bit)) for place in range(count)])


def bit_order():
    bits = lax.axis_size(AXES).bit_length() - 1
    return list(range(1, bits)) + [0]


def scatter_sum(rows):
    order = bit_order()
    place = lax.axis_index(AXES)
    left = list(reversed(range(len(order))))
    held = rows.reshape((2,) * len(order) + rows.shape[1:])
    for bit in order:
        axis = left.index(bit)
        mine = (place >> bit) & 1
        keep = lax.dynamic_index_in_dim(held, mine, axis, keepdims=False)
        send = lax.dynamic_index_in_dim(held, 1 - mine, axis, keepdims=False)
        total = keep.astype(F32) + partner_swap(send, bit).astype(F32)
        left.remove(bit)
        held = total.astype(BF) if left else total
    return held


def butterfly_sum(values):
    for bit in bit_order():
        values = values + partner_swap(values, bit)
    return values


def sums_by_permutes(outs, width, tabs):
    grad, g2, g1, go, sums, gq = outs
    shards = lax.axis_size(AXES)
    outer = scatter_sum(g2.reshape(shards, -1)).reshape(-1, width)
    pieces = [g1.reshape(-1, shards, width // shards, width), go.reshape(1, shards, -1, width)]
    pieces = jnp.concatenate(pieces + [gq.reshape(-1, shards, width // shards, width)], axis=0)
    pieces = pieces.swapaxes(0, 1)
    final = scatter_sum(pieces.reshape(shards, -1)).reshape(pieces.shape[1:])
    sums = butterfly_sum(sums)
    total = butterfly_sum((jnp.sum(outer * outer) + jnp.sum(final * final)).reshape(1))
    total = jnp.zeros((8, 128), F32).at[0, 0].set(total[0] + jnp.sum(sums * sums))
    return grad, total, outer, final, sums


def unswap(rows, length):
    blocks = rows.reshape(-1, length, rows.shape[-1])
    return lax.all_to_all(blocks, "seq", split_axis=1, concat_axis=0, tiled=True)


def body(
    tables_in, out_cot, segment_ids, row_ids, col_ids,
    qkv_weight, out_weight, ffn_in_weight, ffn_out_weight, small_params,
    qkv_master, qkv_first, qkv_second, qkv_ema,
    out_master, out_first, out_second, out_ema,
    ffn_in_master, ffn_in_first, ffn_in_second, ffn_in_ema,
    ffn_out_master, ffn_out_first, ffn_out_second, ffn_out_ema,
    small_first, small_second, small_ema,
):
    width, hidden = ffn_in_weight.shape
    pack = lambda values: values.reshape(-1, 128)
    small = pack(small_params)
    weights = (qkv_weight, out_weight, ffn_in_weight, ffn_out_weight)
    saved = forward(tables_in, out_cot, segment_ids, row_ids, col_ids, *weights, small)
    bits = tuple(lax.axis_size(axis).bit_length() - 1 for axis in AXES)
    linked, outs = backward(saved, weights, small, bits)
    if linked:
        input_grad, layer_out, outer, final, sums, total = outs
    else:
        length = 2 * tables_in.shape[1]
        grad, total, outer, final, sums = sums_by_permutes(outs, width, tables_in.shape[0])
        input_grad, layer_out = unswap(grad, length), unswap(saved[13], length)
    states = [
        (ffn_out_master, ffn_out_first, ffn_out_second, ffn_out_ema),
        (ffn_in_master, ffn_in_first, ffn_in_second, ffn_in_ema),
        (out_master, out_first, out_second, out_ema),
        (qkv_master, qkv_first, qkv_second, qkv_ema),
        (small, pack(small_first), pack(small_second), pack(small_ema)),
    ]
    rates = (hidden**-0.5, width**-0.5, max(width // 128, 1) ** -0.5, width**-0.5, SMALL_RATE)
    entries = 4 * width * width + 2 * width * hidden + 8 * width + hidden
    new = update(total, outer, final, sums, states, rates, math.sqrt(float(entries)), (layer_out, input_grad))
    wo_new, wi_new, o_new, qkv_new = (new[6 * i : 6 * i + 6] for i in range(4))
    sm_new = [values.reshape(-1) for values in new[24:29]]
    groups = (qkv_new, o_new, wi_new, wo_new)
    return (
        *new[30:32],
        *[group[0] for group in groups],
        sm_new[0],
        new[29].reshape(()),
        *[values for group in groups for values in group[1:]],
        sm_new[1],
        sm_new[2],
        sm_new[3],
        sm_new[4],
    )


def solution(mesh):
    rows = P("batch", "seq", None)
    ids = P("batch", None)
    shard3 = P(None, AXES, None)
    shard2 = P(AXES, None)
    in_specs = (rows, rows, ids, ids, ids) + (P(),) * 5 + (shard3,) * 4 + (shard2,) * 12 + (P(),) * 3
    out_specs = (rows, rows, shard3, shard2, shard2, shard2, P(), P())
    out_specs += (shard3,) * 5 + (shard2,) * 15 + (P(),) * 4
    return jax.shard_map(body, mesh=mesh, in_specs=in_specs, out_specs=out_specs, check_vma=False)
```
